512 devices in a mesh: row: 16 (over x, z_lo, core), col: 32 (over z_hi, y).
Axes of the slice: x: 4, y: 8, z: 8 (z_hi: 4, z_lo: 2; z = z_hi * 2 + z_lo), core: 2. Of those that a mesh axis runs over, the one named last changes fastest.
Arguments:
- vectors: float32 [28672, 128], P('row'), may hold values from -6 to 6
- tiles: float32 [16, 32, 10, 56, 56], P('row', 'col'), may hold values from -0.1875 to 0.1875
- tile_pos: int32 [16, 32, 2, 10], P('row', 'col'), may hold values from 0 to 31, as said below
- diag_blocks: float32 [512, 56, 56], P(('row', 'col')), as said below
Outputs:
- filtered: float32 [28672, 128], P('row')
The draws below stay inside these ranges and needn't reach their ends.
Inputs may be any that keep to these rules, and one draw needn't show every extreme that they name: For each device position (r, c), tile_pos[r, c, 0, t] is below 32 and tile_pos[r, c, 1, t] below 16; no two entries of one device are equal pairs; with I and J as in the reference program, I differs from J, and I < J exactly when I + J is odd, so no block and its mirror are both stored. Where 10 + 1 <= 32, the stored blocks of the device at (r, c) lie in 10 different local block rows, none of them among c * 1 to c + 1 - 1. `diag_blocks`: every diagonal block is symmetric.
All inputs are finite; a program needn't handle non-finite values.
Results may differ from the reference program's by a relative error of at most 0.00011.
Values sent between devices are 32-bit elements; how exact they have to be, the bound alone decides.
No kernel may reach another device: no remote copies, remote signals or barrier semaphores. Data moves between devices by JAX's collectives and lax.ppermute only.
A program may use at most 64 MiB of HBM per device.

```python
import math
import jax
import jax.numpy as jnp
from jax import lax

ORB = 56
VECS = 128
STORED_ROW = 10
DEGREE = 3
BLK_SLICE = 1
BLOCKS = 512
TILES_DEV = 10
N_ROW = 16
N_COL = 32


def draw_tile_pos(key, part):
    key = jax.random.fold_in(key, 11)
    group_rows = BLK_SLICE * N_COL
    group_cols = BLK_SLICE * N_ROW
    pairs_total = group_rows * group_cols
    spread = 2 * group_rows + 2
    far_global = (N_ROW - 1) * group_rows
    forced_row = BLK_SLICE + (far_global + 1 + BLK_SLICE) % 2
    forced_col = (N_ROW - 1) * BLK_SLICE

    def one_device(device_key, row_index, col_index):
        order_key, rank_key = jax.random.split(device_key)
        local_row = jnp.arange(group_rows, dtype=jnp.int32)[:, None]
        local_col = jnp.arange(group_cols, dtype=jnp.int32)[None, :]
        global_row = row_index * group_rows + local_row
        global_col = local_col // BLK_SLICE * group_rows + col_index * BLK_SLICE + local_col % BLK_SLICE
        odd_sum = (global_row + global_col) % 2 == 1
        allowed = (global_row != global_col) & ((global_row < global_col) == odd_sum)
        first_device = (row_index == 0) & (col_index == 0)
        last_device = (row_index == 0) & (col_index == N_COL - 1)
        forced = first_device & (local_row == forced_row) & (local_col == forced_col)
        ranking = jax.random.permutation(rank_key, pairs_total).astype(jnp.int32).reshape(group_rows, group_cols)
        ranking = jnp.where(forced, -1, ranking)
        earlier = allowed[:, None, :] & (ranking[:, None, :] < ranking[:, :, None])
        within = jnp.sum(earlier.astype(jnp.int32), axis=2)
        rows_flat = jnp.arange(group_rows, dtype=jnp.int32)
        priority = jax.random.permutation(order_key, group_rows).astype(jnp.int32)
        own_rows = rows_flat // BLK_SLICE == col_index
        priority = jnp.where(own_rows, priority + group_rows, priority)
        priority = jnp.where(first_device & (rows_flat == group_rows - 1), -1, priority)
        priority = jnp.where(last_device & (rows_flat == 0), -2, priority)
        priority = jnp.where(first_device & (rows_flat == forced_row), -3, priority)
        priority = priority + 2
        flat_index = jnp.arange(pairs_total, dtype=jnp.int32).reshape(group_rows, group_cols)
        scores = jnp.where(allowed, within * spread + priority[:, None], spread * group_cols + flat_index)
        chosen = jnp.argsort(scores.reshape(-1), stable=True)[:TILES_DEV].astype(jnp.int32)
        return jnp.stack([chosen // group_cols, chosen % group_cols]).astype(jnp.int32)
    device_keys = jax.random.split(key, N_ROW * N_COL)
    row_ids = jnp.repeat(jnp.arange(N_ROW, dtype=jnp.int32), N_COL)
    col_ids = jnp.tile(jnp.arange(N_COL, dtype=jnp.int32), N_ROW)
    result = jax.vmap(one_device)(device_keys, row_ids, col_ids)
    return result.reshape(N_ROW, N_COL, 2, TILES_DEV).astype(jnp.int32)


def draw_diag_blocks(key, part):
    key = jax.random.fold_in(key, 23)
    noise_key, level_key = jax.random.split(key)
    noise = jax.random.normal(noise_key, (BLOCKS, ORB, ORB), jnp.float32)
    levels = jax.random.uniform(level_key, (BLOCKS, ORB), jnp.float32, 0.0, 5.0)
    symmetric = (noise + jnp.swapaxes(noise, 1, 2)) * (0.5 / math.sqrt(ORB))
    identity = jnp.eye(ORB, dtype=jnp.float32)
    return (symmetric + identity[None, :, :] * levels[:, :, None]).astype(jnp.float32)


def shard_levels(key, extent, cuts, least, largest):
    loudness = 1.0
    for axis_at, blocks in cuts:
        heights = jax.random.uniform(jax.random.fold_in(jax.random.fold_in(key, 6), axis_at), (blocks,), jnp.float32, least / len(cuts), largest / len(cuts))
        loudness = loudness * jnp.repeat(jnp.exp(heights), extent[axis_at] // blocks).reshape((-1,) + (1,) * (len(extent) - 1 - axis_at))
    return loudness


def bell_draw(stream_key, extent, width, reach, cuts=(), kind=jnp.bfloat16):
    values = jax.random.normal(stream_key, extent, jnp.float32) * width
    if len(cuts) > 0:
        values = shard_levels(stream_key, extent, cuts, -0.22, 0.18) * values
    return jnp.clip(values, min=-reach, max=reach).astype(kind)


def setup_inputs(seed: int = 0) -> dict:
    splits = jax.random.split(jax.random.key(seed), 5)
    vectors = bell_draw(splits[0], (BLOCKS * ORB, VECS), 1.0, 6.0, ((0, 16),), jnp.float32)
    tiles = bell_draw(splits[1], (N_ROW, N_COL, TILES_DEV, ORB, ORB), (2 * STORED_ROW * ORB) ** -0.5, 0.1875, ((0, 16), (1, 32)), jnp.float32)
    tile_pos = draw_tile_pos(jax.random.fold_in(splits[4], 71), 0)
    diag_blocks = draw_diag_blocks(jax.random.fold_in(splits[4], 71), 0)
    return {"vectors": vectors, "tiles": tiles, "tile_pos": tile_pos, "diag_blocks": diag_blocks}


filter_low = 0.0
filter_high = 8.0


def apply_operator(field, tiles, tile_pos, diag_blocks):
    blocks = field.reshape(-1, ORB, VECS)
    row_blocks = BLK_SLICE * N_COL
    total_blocks = row_blocks * N_ROW
    rows_local = tile_pos[:, :, 0, :]
    cols_local = tile_pos[:, :, 1, :]
    group = jnp.arange(N_ROW, dtype=jnp.int32)[:, None, None]
    column = jnp.arange(N_COL, dtype=jnp.int32)[None, :, None]
    global_rows = (group * row_blocks + rows_local).reshape(-1).astype(jnp.int32)
    global_cols = ((cols_local // BLK_SLICE) * row_blocks + column * BLK_SLICE + cols_local % BLK_SLICE).reshape(-1).astype(jnp.int32)
    tile_data = tiles.reshape(-1, ORB, ORB)
    direct = jnp.einsum("tab,tbk->tak", tile_data, blocks[global_cols], precision=lax.Precision.HIGHEST)
    direct_sum = jax.ops.segment_sum(direct, global_rows, num_segments=total_blocks)
    mirror = jnp.einsum("tba,tbk->tak", tile_data, blocks[global_rows], precision=lax.Precision.HIGHEST)
    mirror_sum = jax.ops.segment_sum(mirror, global_cols, num_segments=total_blocks)
    diagonal = jnp.einsum("sab,sbk->sak", diag_blocks, blocks, precision=lax.Precision.HIGHEST)
    return (direct_sum + mirror_sum + diagonal).reshape(field.shape)


def reference(vectors, tiles, tile_pos, diag_blocks):
    centre = 0.5 * (filter_high + filter_low)
    half_width = 0.5 * (filter_high - filter_low)
    previous = vectors
    current = (apply_operator(vectors, tiles, tile_pos, diag_blocks) - centre * vectors) / half_width
    for step in range(DEGREE - 1):
        image = apply_operator(current, tiles, tile_pos, diag_blocks)
        following = 2.0 * (image - centre * current) / half_width - previous
        previous, current = current, following
    return current
```

```python
import functools

import jax
import jax.numpy as jnp
from jax import lax
from jax.experimental import pallas as pl
from jax.experimental.pallas import tpu as pltpu
from jax.sharding import Mesh, PartitionSpec as P

ORB = 56
DEGREE = 3
LANES = 128
N_X, N_ZL, N_CORE, N_ZH, N_Y = 4, 2, 2, 4, 8
N_R = N_X * N_ZL
TILES = 10
SLOTS = TILES + 1
SOURCES = N_CORE * N_ZH
WIDE = 640
VS = 16
ROW_AX = ("x", "zl")
GROUPS = 8

filter_low = 0.0
filter_high = 8.0

f32 = jnp.float32
bf16 = jnp.bfloat16


def params():
    return pltpu.CompilerParams(vmem_limit_bytes=40 * 1024 * 1024)


def vmem(n):
    return [pl.BlockSpec(memory_space=pltpu.VMEM)] * n


def lane_iota(rows=ORB):
    return lax.broadcasted_iota(jnp.int32, (rows, LANES), 1)


def roll_to(x, source, target):
    shift = (target - source) % LANES
    return x if shift == 0 else pltpu.roll(x, shift, 1)


def pack_kernel(tiles_ref, diag_ref, pos_ref, out_ref):
    lane = lane_iota()
    pieces = [tiles_ref[t] for t in range(TILES)] + [diag_ref[...]]
    wide = [
        jnp.concatenate([p, jnp.zeros((ORB, LANES - ORB), f32)], axis=1) for p in pieces
    ]
    places = jnp.broadcast_to(pos_ref[...], (ORB, LANES))
    for q in range(WIDE // LANES):
        total = jnp.zeros((ORB, LANES), f32)
        for t in range(SLOTS):
            start = t * ORB - q * LANES
            if start <= -ORB or start >= LANES:
                continue
            inside = (lane >= max(start, 0)) & (lane < min(start + ORB, LANES))
            total = jnp.where(inside, roll_to(wide[t], 0, start), total)
        if q == WIDE // LANES - 1:
            start = SLOTS * ORB - q * LANES
            total = jnp.where(lane >= start, roll_to(places, 0, start), total)
        out_ref[:, q * LANES : (q + 1) * LANES] = total


def pack(tile_data, diag, places):
    return pl.pallas_call(
        pack_kernel,
        out_shape=jax.ShapeDtypeStruct((ORB, WIDE), f32),
        in_specs=vmem(3),
        out_specs=vmem(1)[0],
        compiler_params=params(),
        name="pack",
    )(tile_data, diag, places)


def two_terms(x):
    high = x.astype(bf16).astype(f32)
    low = x - high
    return (high + pltpu.roll(low, 64, 1)).astype(bf16)


def unpack_kernel(in_ref, plain_ref, turned_ref):
    lane = lane_iota()

    def one_source(s, carry):
        for t in range(SLOTS):
            start = t * ORB
            q, off = start // LANES, start % LANES
            x = roll_to(in_ref[s, :, q * LANES : (q + 1) * LANES], off, 0)
            if off + ORB > LANES:
                y = roll_to(in_ref[s, :, (q + 1) * LANES : (q + 2) * LANES], off, 0)
                x = jnp.where(lane < LANES - off, x, y)
            x = jnp.where(lane < ORB, x, 0.0)
            plain_ref[s * SLOTS + t] = two_terms(x)
            square = jnp.concatenate([x, jnp.zeros((LANES - ORB, LANES), f32)], axis=0)
            turned_ref[s * SLOTS + t] = two_terms(square.T[:ORB])
        return carry

    lax.fori_loop(0, SOURCES, one_source, 0)


def unpack(packed):
    shape = jax.ShapeDtypeStruct((SOURCES * SLOTS, ORB, LANES), bf16)
    return pl.pallas_call(
        unpack_kernel,
        out_shape=(shape, shape),
        in_specs=vmem(1),
        out_specs=tuple(vmem(2)),
        compiler_params=params(),
        name="unpack",
    )(packed)


def slice_kernel(zh_ref, in_ref, out_ref):
    lane = lane_iota()
    start = zh_ref[0] * (2 * VS)
    for yp in range(N_Y // 2):
        for k in range(N_CORE):
            total = jnp.zeros((ORB, LANES), f32)
            for half in range(2):
                for z in range(N_ZH):
                    target = half * 64 + z * VS
                    x = in_ref[z * N_Y + 2 * yp + half]
                    shift = lax.rem(target - k * VS + LANES - start + LANES, LANES)
                    x = pltpu.roll(x, shift, 1)
                    inside = (lane >= target) & (lane < target + VS)
                    total = jnp.where(inside, x, total)
            out_ref[k, yp] = total


def slice_vectors(zh, blocks):
    return pl.pallas_call(
        slice_kernel,
        out_shape=jax.ShapeDtypeStruct((N_CORE, N_Y // 2, ORB, LANES), f32),
        in_specs=[pl.BlockSpec(memory_space=pltpu.SMEM)] + vmem(1),
        out_specs=vmem(1)[0],
        compiler_params=params(),
        name="slice_vectors",
    )(zh, blocks)


def join_kernel(in_ref, out_ref):
    lane = lane_iota()
    for yp in range(N_Y // 2):
        a, b = in_ref[0, yp], in_ref[1, yp]
        out_ref[2 * yp] = jnp.where(lane < 64, a, pltpu.roll(b, 64, 1))
        out_ref[2 * yp + 1] = jnp.where(lane < 64, pltpu.roll(a, 64, 1), b)


def join_cores(both):
    return pl.pallas_call(
        join_kernel,
        out_shape=jax.ShapeDtypeStruct((N_Y, ORB, LANES), f32),
        in_specs=vmem(1),
        out_specs=vmem(1)[0],
        compiler_params=params(),
        name="join_cores",
    )(both)


def product_kernel(
    pos_ref, me_ref, cols_ref, rows_ref, plain_ref, turned_ref,
    out_cols_ref, out_rows_ref, vc_ref, vr_ref, acc_c_ref, acc_r_ref,
):
    for src, dst in ((cols_ref, vc_ref), (rows_ref, vr_ref)):
        for chunk in range(GROUPS):
            x = src[chunk].T
            high = x.astype(bf16)
            low = (x - high.astype(f32)).astype(bf16)
            for o in range(GROUPS):
                dst[chunk * GROUPS + o, 0:VS] = high[o * VS : (o + 1) * VS]
                dst[chunk * GROUPS + o, VS : 2 * VS] = low[o * VS : (o + 1) * VS]
    acc_c_ref[...] = jnp.zeros_like(acc_c_ref)
    acc_r_ref[...] = jnp.zeros_like(acc_r_ref)
    my_r, my_y = me_ref[0], me_ref[1]

    def times(v, block):
        both = jnp.dot(v, block, preferred_element_type=f32)
        return both[:VS] + both[VS:]

    def one_source(s, carry):
        core_s, zh_s = s // N_ZH, s % N_ZH
        for t in range(SLOTS):
            n = s * SLOTS + t
            if t < TILES:
                i, g = pos_ref[s, t], pos_ref[s, TILES + t]
                row = (i % N_Y) * GROUPS + core_s * N_ZH + i // N_Y
                col = (g // N_CORE) * GROUPS + (g % N_CORE) * N_ZH + zh_s
                acc_r_ref[row] += times(vc_ref[col], turned_ref[n])
                acc_c_ref[col] += times(vr_ref[row], plain_ref[n])
            else:
                acc_r_ref[my_y * GROUPS + s] += times(vc_ref[my_r * GROUPS + s], turned_ref[n])
        return carry

    lax.fori_loop(0, SOURCES, one_source, 0)
    for acc, out in ((acc_c_ref, out_cols_ref), (acc_r_ref, out_rows_ref)):
        for chunk in range(GROUPS):
            x = acc[chunk * GROUPS : (chunk + 1) * GROUPS].reshape(LANES, LANES)
            x = x + pltpu.roll(x, 64, 1)
            out[chunk] = x.T[:ORB]


def product(places, me, cols, rows, plain, turned):
    shape = jax.ShapeDtypeStruct((GROUPS, ORB, LANES), f32)
    smem = pl.BlockSpec(memory_space=pltpu.SMEM)
    return pl.pallas_call(
        product_kernel,
        out_shape=(shape, shape),
        in_specs=[smem, smem] + vmem(4),
        out_specs=tuple(vmem(2)),
        scratch_shapes=[
            pltpu.VMEM((GROUPS * GROUPS, 2 * VS, ORB), bf16),
            pltpu.VMEM((GROUPS * GROUPS, 2 * VS, ORB), bf16),
            pltpu.VMEM((GROUPS * GROUPS, VS, LANES), f32),
            pltpu.VMEM((GROUPS * GROUPS, VS, LANES), f32),
        ],
        compiler_params=params(),
        name="product",
    )(places, me, cols, rows, plain, turned)


def spread_kernel(in_ref, out_ref):
    lane = lane_iota()
    for y in range(N_Y):
        for z in range(N_ZH):
            total = jnp.zeros((ORB, LANES), f32)
            for h in range(N_ZH):
                for k in range(N_CORE):
                    target = h * 2 * VS + k * VS
                    x = roll_to(in_ref[h, y], k * 64 + z * VS, target)
                    inside = (lane >= target) & (lane < target + VS)
                    total = jnp.where(inside, x, total)
            out_ref[z * N_Y + y] = total


def spread(gathered):
    return pl.pallas_call(
        spread_kernel,
        out_shape=jax.ShapeDtypeStruct((N_ZH * N_Y, ORB, LANES), f32),
        in_specs=vmem(1),
        out_specs=vmem(1)[0],
        compiler_params=params(),
        name="spread",
    )(gathered)


def exchange(x, axes):
    return lax.all_to_all(x, axes, split_axis=0, concat_axis=0, tiled=True)


def gather(x, axes, n):
    return exchange(jnp.broadcast_to(x[None], (n,) + x.shape), axes)


def body(vectors, tiles, tile_pos, diag_blocks):
    zh = lax.axis_index("zh")
    y = lax.axis_index("y")
    r = lax.axis_index("x") * N_ZL + lax.axis_index("zl")
    core = lax.axis_index("core")
    me = jnp.stack([r, y]).astype(jnp.int32)

    places = jnp.pad(tile_pos.reshape(1, 2 * TILES).astype(f32), ((0, 0), (0, LANES - 2 * TILES)))
    packed = pack(tiles[0, 0], diag_blocks[0], places)
    packed = gather(packed, "zh", N_ZH)

    sliced = slice_vectors(zh.reshape(1).astype(jnp.int32), vectors.reshape(-1, ORB, LANES))
    rows = join_cores(exchange(sliced, "core"))
    current = lax.dynamic_slice_in_dim(rows, y, 1, 0)[0]
    cols = gather(current, ROW_AX, N_R)

    packed = gather(packed, "core", N_CORE).reshape(SOURCES, ORB, WIDE)
    where = packed[:, 0, SLOTS * ORB : SLOTS * ORB + 2 * TILES].astype(jnp.int32)
    plain, turned = unpack(packed)

    centre = 0.5 * (filter_high + filter_low)
    half_width = 0.5 * (filter_high - filter_low)
    previous = None
    for step in range(DEGREE):
        out_cols, out_rows = product(where, me, cols, rows, plain, turned)
        got_rows = exchange(out_rows, "y")
        got_cols = exchange(out_cols, ROW_AX)
        image = jnp.sum(got_cols, 0) + jnp.sum(got_rows, 0)
        shifted = (image - centre * current) / half_width
        following = shifted if previous is None else 2.0 * shifted - previous
        previous, current = current, following
        if step < DEGREE - 1:
            rows = gather(current, "y", N_Y)
            cols = gather(current, ROW_AX, N_R)

    lane = lane_iota()
    swapped = jnp.concatenate([current[:, 64:], current[:, :64]], axis=1)
    mine = (lane // 64) == core
    first = jnp.where(core == 0, current, swapped)
    second = jnp.where(core == 1, current, swapped)
    halves = jnp.where(mine[None], jnp.stack([first, second]), 0.0)
    result = jnp.sum(exchange(halves, "core"), 0)
    result = gather(result, ("zh", "y"), N_ZH * N_Y).reshape(N_ZH, N_Y, ORB, LANES)
    return spread(result).reshape(vectors.shape)


def solution(mesh):
    fine = Mesh(
        mesh.devices.reshape(N_X, N_ZL, N_CORE, N_ZH, N_Y), ("x", "zl", "core", "zh", "y")
    )
    row, col = ("x", "zl", "core"), ("zh", "y")
    return jax.shard_map(
        body,
        mesh=fine,
        in_specs=(
            P(row, None),
            P(row, col, None, None, None),
            P(row, col, None, None),
            P(row + col, None, None),
        ),
        out_specs=P(row, None),
        check_vma=False,
    )
```

```python
import functools

import jax
import jax.numpy as jnp
from jax import lax
from jax.experimental import pallas as pl
from jax.experimental.pallas import tpu as pltpu
from jax.sharding import Mesh, PartitionSpec as P

ORB = 56
DEGREE = 3
LANES = 128
N_X, N_ZL, N_CORE, N_ZH, N_Y = 4, 2, 2, 4, 8
N_R = N_X * N_ZL
TILES = 10
SLOTS = TILES + 1
SOURCES = N_CORE * N_ZH
WIDE = 640
VS = 16
PLACE = SLOTS * ORB - (WIDE - LANES)
ROW_AX = ("x", "zl")
GROUPS = 8

filter_low = 0.0
filter_high = 8.0

f32 = jnp.float32
bf16 = jnp.bfloat16


def params():
    return pltpu.CompilerParams(vmem_limit_bytes=40 * 1024 * 1024)


def vmem(n):
    return [pl.BlockSpec(memory_space=pltpu.VMEM)] * n


def lane_iota(rows=ORB):
    return lax.broadcasted_iota(jnp.int32, (rows, LANES), 1)


def roll_to(x, source, target):
    shift = (target - source) % LANES
    return x if shift == 0 else pltpu.roll(x, shift, 1)


def pack_kernel(tiles_ref, diag_ref, pos_ref, out_ref):
    lane = lane_iota()
    pieces = [tiles_ref[t] for t in range(TILES)] + [diag_ref[...]]
    wide = [
        jnp.concatenate([p, jnp.zeros((ORB, LANES - ORB), f32)], axis=1) for p in pieces
    ]
    places = jnp.broadcast_to(pos_ref[...], (ORB, LANES))
    for q in range(WIDE // LANES):
        total = jnp.zeros((ORB, LANES), f32)
        for t in range(SLOTS):
            start = t * ORB - q * LANES
            if start <= -ORB or start >= LANES:
                continue
            inside = (lane >= max(start, 0)) & (lane < min(start + ORB, LANES))
            total = jnp.where(inside, roll_to(wide[t], 0, start), total)
        if q == WIDE // LANES - 1:
            start = SLOTS * ORB - q * LANES
            total = jnp.where(lane >= start, roll_to(places, 0, start), total)
        out_ref[:, q * LANES : (q + 1) * LANES] = total


def pack(tile_data, diag, places):
    return pl.pallas_call(
        pack_kernel,
        out_shape=jax.ShapeDtypeStruct((ORB, WIDE), f32),
        in_specs=vmem(3),
        out_specs=vmem(1)[0],
        compiler_params=params(),
        name="pack",
    )(tile_data, diag, places)


def two_terms(x):
    high = x.astype(bf16).astype(f32)
    low = x - high
    return (high + pltpu.roll(low, 64, 1)).astype(bf16)


def unpack_kernel(in_ref, blocks_ref, places_ref):
    lane = lane_iota()

    def one_source(s, carry):
        for t in range(SLOTS):
            start = t * ORB
            q, off = start // LANES, start % LANES
            x = roll_to(in_ref[s, :, q * LANES : (q + 1) * LANES], off, 0)
            if off + ORB > LANES:
                y = roll_to(in_ref[s, :, (q + 1) * LANES : (q + 2) * LANES], off, 0)
                x = jnp.where(lane < LANES - off, x, y)
            blocks_ref[s * SLOTS + t] = two_terms(jnp.where(lane < ORB, x, 0.0))
        return carry

    lax.fori_loop(0, SOURCES, one_source, 0)
    for s in range(SOURCES):
        last = in_ref[s, 0:1, WIDE - LANES : WIDE]
        shown = lax.broadcasted_iota(jnp.int32, (1, LANES), 1) >= PLACE
        places_ref[s : s + 1] = jnp.where(shown, last, 0.0).astype(jnp.int32)


def unpack(packed):
    return pl.pallas_call(
        unpack_kernel,
        out_shape=(
            jax.ShapeDtypeStruct((SOURCES * SLOTS, ORB, LANES), bf16),
            jax.ShapeDtypeStruct((SOURCES, LANES), jnp.int32),
        ),
        in_specs=vmem(1),
        out_specs=tuple(vmem(2)),
        compiler_params=params(),
        name="unpack",
    )(packed)


def slice_kernel(zh_ref, in_ref, out_ref):
    lane = lane_iota()
    start = zh_ref[0] * (2 * VS)
    for yp in range(N_Y // 2):
        for k in range(N_CORE):
            total = jnp.zeros((ORB, LANES), f32)
            for half in range(2):
                for z in range(N_ZH):
                    target = half * 64 + z * VS
                    x = in_ref[z * N_Y + 2 * yp + half]
                    shift = lax.rem(target - k * VS + LANES - start + LANES, LANES)
                    x = pltpu.roll(x, shift, 1)
                    inside = (lane >= target) & (lane < target + VS)
                    total = jnp.where(inside, x, total)
            out_ref[k, yp] = total


def slice_vectors(zh, blocks):
    return pl.pallas_call(
        slice_kernel,
        out_shape=jax.ShapeDtypeStruct((N_CORE, N_Y // 2, ORB, LANES), f32),
        in_specs=[pl.BlockSpec(memory_space=pltpu.SMEM)] + vmem(1),
        out_specs=vmem(1)[0],
        compiler_params=params(),
        name="slice_vectors",
    )(zh, blocks)


def join_kernel(core_ref, mine_ref, other_ref, out_ref):
    lane = lane_iota()
    is_zero = core_ref[0] == 0
    for yp in range(N_Y // 2):
        mine, other = mine_ref[yp], other_ref[yp]
        a = jnp.where(is_zero, mine, other)
        b = jnp.where(is_zero, other, mine)
        out_ref[2 * yp] = jnp.where(lane < 64, a, pltpu.roll(b, 64, 1))
        out_ref[2 * yp + 1] = jnp.where(lane < 64, pltpu.roll(a, 64, 1), b)


def join_cores(core, mine, other):
    return pl.pallas_call(
        join_kernel,
        out_shape=jax.ShapeDtypeStruct((N_Y, ORB, LANES), f32),
        in_specs=[pl.BlockSpec(memory_space=pltpu.SMEM)] + vmem(2),
        out_specs=vmem(1)[0],
        compiler_params=params(),
        name="join_cores",
    )(core, mine, other)


def split_terms(src_ref, dst_ref):
    gap = jnp.zeros((64 - ORB, LANES), f32)
    for chunk in range(GROUPS):
        x = src_ref[chunk]
        x = jnp.concatenate([x, gap, x, gap], axis=0).T
        high = x.astype(bf16)
        low = (x - high.astype(f32)).astype(bf16)
        for o in range(GROUPS):
            dst_ref[chunk * GROUPS + o, 0:VS] = high[o * VS : (o + 1) * VS]
            dst_ref[chunk * GROUPS + o, VS : 2 * VS] = low[o * VS : (o + 1) * VS]


def row_col(pos_ref, s, t):
    i, g = pos_ref[s, PLACE + t], pos_ref[s, PLACE + TILES + t]
    row = (i & 7) * GROUPS + (s // N_ZH) * N_ZH + (i >> 3)
    col = (g >> 1) * GROUPS + (g & 1) * N_ZH + s % N_ZH
    return row, col


def mirror_kernel(pos_ref, rows_ref, blocks_ref, out_ref, v_ref, acc_ref):
    split_terms(rows_ref, v_ref)
    acc_ref[...] = jnp.zeros_like(acc_ref)

    def one_source(s, carry):
        for t in range(TILES):
            row, col = row_col(pos_ref, s, t)
            both = jnp.dot(v_ref[row][:, :ORB], blocks_ref[s * SLOTS + t], preferred_element_type=f32)
            acc_ref[col] += both[:VS] + both[VS:]
        return carry

    lax.fori_loop(0, SOURCES, one_source, 0)
    for chunk in range(GROUPS):
        x = acc_ref[chunk * GROUPS : (chunk + 1) * GROUPS].reshape(LANES, LANES)
        x = x + pltpu.roll(x, 64, 1)
        out_ref[chunk] = x.T[:ORB]


def direct_kernel(pos_ref, me_ref, cols_ref, blocks_ref, out_ref, v_ref, acc_ref):
    split_terms(cols_ref, v_ref)
    acc_ref[...] = jnp.zeros_like(acc_ref)
    my_r, my_y = me_ref[0], me_ref[1]

    def one_source(s, carry):
        for t in range(SLOTS):
            if t < TILES:
                row, col = row_col(pos_ref, s, t)
            else:
                row, col = my_y * GROUPS + s, my_r * GROUPS + s
            both = lax.dot_general(
                v_ref[col], blocks_ref[s * SLOTS + t], (((1,), (1,)), ((), ())),
                preferred_element_type=f32,
            )
            acc_ref[row, :, 0:ORB] += both[:VS] + both[VS:]
        return carry

    lax.fori_loop(0, SOURCES, one_source, 0)
    for chunk in range(GROUPS):
        x = acc_ref[chunk * GROUPS : (chunk + 1) * GROUPS].reshape(LANES, LANES)
        out_ref[chunk] = x.T[:ORB]


def product(kernel, name, scalars, field, blocks):
    smem = pl.BlockSpec(memory_space=pltpu.SMEM)
    return pl.pallas_call(
        kernel,
        out_shape=jax.ShapeDtypeStruct((GROUPS, ORB, LANES), f32),
        in_specs=[smem] * len(scalars) + vmem(2),
        out_specs=vmem(1)[0],
        scratch_shapes=[
            pltpu.VMEM((GROUPS * GROUPS, 2 * VS, LANES), bf16),
            pltpu.VMEM((GROUPS * GROUPS, VS, LANES), f32),
        ],
        compiler_params=params(),
        cost_estimate=pl.CostEstimate(flops=200000000, bytes_accessed=4000000, transcendentals=0),
        name=name,
    )(*scalars, field, blocks)


def spread_kernel(in_ref, out_ref):
    lane = lane_iota()
    for y in range(N_Y):
        for z in range(N_ZH):
            total = jnp.zeros((ORB, LANES), f32)
            for h in range(N_ZH):
                for k in range(N_CORE):
                    target = h * 2 * VS + k * VS
                    x = roll_to(in_ref[h, y], k * 64 + z * VS, target)
                    inside = (lane >= target) & (lane < target + VS)
                    total = jnp.where(inside, x, total)
            out_ref[z * N_Y + y] = total


def spread(gathered):
    return pl.pallas_call(
        spread_kernel,
        out_shape=jax.ShapeDtypeStruct((N_ZH * N_Y, ORB, LANES), f32),
        in_specs=vmem(1),
        out_specs=vmem(1)[0],
        compiler_params=params(),
        name="spread",
    )(gathered)


def exchange(x, axes):
    return lax.all_to_all(x, axes, split_axis=0, concat_axis=0, tiled=True)


def gather(x, axes, n):
    return exchange(jnp.broadcast_to(x[None], (n,) + x.shape), axes)


def body(vectors, tiles, tile_pos, diag_blocks):
    zh = lax.axis_index("zh")
    y = lax.axis_index("y")
    r = lax.axis_index("x") * N_ZL + lax.axis_index("zl")
    core = lax.axis_index("core")
    me = jnp.stack([r, y]).astype(jnp.int32)

    places = jnp.pad(tile_pos.reshape(1, 2 * TILES).astype(f32), ((0, 0), (0, LANES - 2 * TILES)))
    packed = pack(tiles[0, 0], diag_blocks[0], places)
    packed = gather(packed, "zh", N_ZH)

    sliced = slice_vectors(zh.reshape(1).astype(jnp.int32), vectors.reshape(-1, ORB, LANES))
    mine = lax.dynamic_index_in_dim(sliced, core, 0, keepdims=False)
    other = lax.dynamic_index_in_dim(sliced, 1 - core, 0, keepdims=False)
    other = lax.ppermute(other, "core", [(0, 1), (1, 0)])
    rows = join_cores(core.reshape(1).astype(jnp.int32), mine, other)
    current = lax.dynamic_index_in_dim(rows, y, 0, keepdims=False)
    cols = lax.all_gather(current, ROW_AX, axis=0, tiled=False)
    packed, cols = lax.optimization_barrier((packed, cols))

    packed = gather(packed.reshape(N_ZH * ORB, WIDE), "core", N_CORE)
    blocks, where = unpack(packed.reshape(SOURCES, ORB, WIDE))

    centre = 0.5 * (filter_high + filter_low)
    half_width = 0.5 * (filter_high - filter_low)
    previous = None
    for step in range(DEGREE):
        out_cols = product(mirror_kernel, "mirror", (where,), rows, blocks)
        got_cols = exchange(out_cols, ROW_AX)
        out_rows = product(direct_kernel, "direct", (where, me), cols, blocks)
        got_rows = exchange(out_rows, "y")
        image = jnp.sum(got_cols, 0) + jnp.sum(got_rows, 0)
        shifted = (image - centre * current) / half_width
        following = shifted if previous is None else 2.0 * shifted - previous
        previous, current = current, following
        if step < DEGREE - 1:
            rows = gather(current, "y", N_Y)
            cols = gather(current, ROW_AX, N_R)

    lane = lane_iota()
    swapped = jnp.concatenate([current[:, 64:], current[:, :64]], axis=1)
    mine = (lane // 64) == core
    first = jnp.where(core == 0, current, swapped)
    second = jnp.where(core == 1, current, swapped)
    halves = jnp.where(mine[None], jnp.stack([first, second]), 0.0)
    result = jnp.sum(exchange(halves, "core"), 0)
    result = gather(result, ("zh", "y"), N_ZH * N_Y).reshape(N_ZH, N_Y, ORB, LANES)
    return spread(result).reshape(vectors.shape)


def solution(mesh):
    fine = Mesh(
        mesh.devices.reshape(N_X, N_ZL, N_CORE, N_ZH, N_Y), ("x", "zl", "core", "zh", "y")
    )
    row, col = ("x", "zl", "core"), ("zh", "y")
    return jax.shard_map(
        body,
        mesh=fine,
        in_specs=(
            P(row, None),
            P(row, col, None, None, None),
            P(row, col, None, None),
            P(row + col, None, None),
        ),
        out_specs=P(row, None),
        check_vma=False,
    )
```

```python
import functools

import jax
import jax.numpy as jnp
from jax import lax
from jax.experimental import pallas as pl
from jax.experimental.pallas import tpu as pltpu
from jax.sharding import Mesh, PartitionSpec as P

ORB = 56
DEGREE = 3
LANES = 128
N_X, N_ZL, N_CORE, N_ZH, N_Y = 4, 2, 2, 4, 8
N_R = N_X * N_ZL
TILES = 10
SLOTS = TILES + 1
SOURCES = N_CORE * N_ZH
WIDE = 640
VS = 16
PLACE = SLOTS * ORB - (WIDE - LANES)
ROW_AX = ("x", "zl")
GROUPS = 8

filter_low = 0.0
filter_high = 8.0

f32 = jnp.float32
bf16 = jnp.bfloat16


def params():
    return pltpu.CompilerParams(vmem_limit_bytes=40 * 1024 * 1024)


def vmem(n):
    return [pl.BlockSpec(memory_space=pltpu.VMEM)] * n


def lane_iota(rows=ORB):
    return lax.broadcasted_iota(jnp.int32, (rows, LANES), 1)


def roll_to(x, source, target):
    shift = (target - source) % LANES
    return x if shift == 0 else pltpu.roll(x, shift, 1)


def pack_kernel(tiles_ref, diag_ref, pos_ref, out_ref):
    lane = lane_iota()
    pieces = [tiles_ref[t] for t in range(TILES)] + [diag_ref[...]]
    wide = [
        jnp.concatenate([p, jnp.zeros((ORB, LANES - ORB), f32)], axis=1) for p in pieces
    ]
    gap = jnp.zeros((1, LANES - 2 * TILES), f32)
    both = pos_ref[...].astype(f32)
    places = jnp.concatenate([both[0:1], both[1:2], gap], axis=1)
    places = jnp.broadcast_to(places, (ORB, LANES))
    for q in range(WIDE // LANES):
        total = jnp.zeros((ORB, LANES), f32)
        for t in range(SLOTS):
            start = t * ORB - q * LANES
            if start <= -ORB or start >= LANES:
                continue
            inside = (lane >= max(start, 0)) & (lane < min(start + ORB, LANES))
            total = jnp.where(inside, roll_to(wide[t], 0, start), total)
        if q == WIDE // LANES - 1:
            start = SLOTS * ORB - q * LANES
            total = jnp.where(lane >= start, roll_to(places, 0, start), total)
        out_ref[:, q * LANES : (q + 1) * LANES] = total


def pack(tile_data, diag, places):
    return pl.pallas_call(
        pack_kernel,
        out_shape=jax.ShapeDtypeStruct((ORB, WIDE), f32),
        in_specs=vmem(3),
        out_specs=vmem(1)[0],
        compiler_params=params(),
        name="pack",
    )(tile_data, diag, places)


def two_terms(x):
    high = x.astype(bf16).astype(f32)
    low = x - high
    return (high + pltpu.roll(low, 64, 1)).astype(bf16)


def unpack_kernel(in_ref, blocks_ref, places_ref):
    lane = lane_iota()

    def one_source(s, carry):
        for t in range(SLOTS):
            start = t * ORB
            q, off = start // LANES, start % LANES
            x = roll_to(in_ref[s, :, q * LANES : (q + 1) * LANES], off, 0)
            if off + ORB > LANES:
                y = roll_to(in_ref[s, :, (q + 1) * LANES : (q + 2) * LANES], off, 0)
                x = jnp.where(lane < LANES - off, x, y)
            blocks_ref[s * SLOTS + t] = two_terms(jnp.where(lane < ORB, x, 0.0))
        return carry

    lax.fori_loop(0, SOURCES, one_source, 0)
    for s in range(SOURCES):
        last = in_ref[s, 0:1, WIDE - LANES : WIDE]
        shown = lax.broadcasted_iota(jnp.int32, (1, LANES), 1) >= PLACE
        places_ref[s : s + 1] = jnp.where(shown, last, 0.0).astype(jnp.int32)


def unpack(packed):
    return pl.pallas_call(
        unpack_kernel,
        out_shape=(
            jax.ShapeDtypeStruct((SOURCES * SLOTS, ORB, LANES), bf16),
            jax.ShapeDtypeStruct((SOURCES, LANES), jnp.int32),
        ),
        in_specs=vmem(1),
        out_specs=tuple(vmem(2)),
        compiler_params=params(),
        name="unpack",
    )(packed)


def slice_kernel(zh_ref, in_ref, out_ref):
    lane = lane_iota()
    start = zh_ref[0] * (2 * VS)
    for yp in range(N_Y // 2):
        for k in range(N_CORE):
            total = jnp.zeros((ORB, LANES), f32)
            for half in range(2):
                for z in range(N_ZH):
                    target = half * 64 + z * VS
                    x = in_ref[z * N_Y + 2 * yp + half]
                    shift = lax.rem(target - k * VS + LANES - start + LANES, LANES)
                    x = pltpu.roll(x, shift, 1)
                    inside = (lane >= target) & (lane < target + VS)
                    total = jnp.where(inside, x, total)
            out_ref[k, yp] = total


def slice_vectors(zh, blocks):
    return pl.pallas_call(
        slice_kernel,
        out_shape=jax.ShapeDtypeStruct((N_CORE, N_Y // 2, ORB, LANES), f32),
        in_specs=[pl.BlockSpec(memory_space=pltpu.SMEM)] + vmem(1),
        out_specs=vmem(1)[0],
        compiler_params=params(),
        name="slice_vectors",
    )(zh, blocks)


def join_kernel(core_ref, mine_ref, other_ref, out_ref):
    lane = lane_iota()
    is_zero = core_ref[0] == 0
    for yp in range(N_Y // 2):
        mine, other = mine_ref[yp], other_ref[yp]
        a = jnp.where(is_zero, mine, other)
        b = jnp.where(is_zero, other, mine)
        out_ref[2 * yp] = jnp.where(lane < 64, a, pltpu.roll(b, 64, 1))
        out_ref[2 * yp + 1] = jnp.where(lane < 64, pltpu.roll(a, 64, 1), b)


def join_cores(core, mine, other):
    return pl.pallas_call(
        join_kernel,
        out_shape=jax.ShapeDtypeStruct((N_Y, ORB, LANES), f32),
        in_specs=[pl.BlockSpec(memory_space=pltpu.SMEM)] + vmem(2),
        out_specs=vmem(1)[0],
        compiler_params=params(),
        name="join_cores",
    )(core, mine, other)


def split_terms(src_ref, dst_ref):
    gap = jnp.zeros((64 - ORB, LANES), f32)
    for chunk in range(GROUPS):
        x = src_ref[chunk]
        x = jnp.concatenate([x, gap, x, gap], axis=0).T
        high = x.astype(bf16)
        low = (x - high.astype(f32)).astype(bf16)
        for o in range(GROUPS):
            dst_ref[chunk * GROUPS + o, 0:VS] = high[o * VS : (o + 1) * VS]
            dst_ref[chunk * GROUPS + o, VS : 2 * VS] = low[o * VS : (o + 1) * VS]


def row_col(pos_ref, s, t):
    i, g = pos_ref[s, PLACE + t], pos_ref[s, PLACE + TILES + t]
    row = (i & 7) * GROUPS + (s // N_ZH) * N_ZH + (i >> 3)
    col = (g >> 1) * GROUPS + (g & 1) * N_ZH + s % N_ZH
    return row, col


def mirror_kernel(pos_ref, rows_ref, blocks_ref, out_ref, v_ref, acc_ref):
    split_terms(rows_ref, v_ref)
    acc_ref[...] = jnp.zeros_like(acc_ref)

    def one_source(s, carry):
        for t in range(TILES):
            row, col = row_col(pos_ref, s, t)
            both = jnp.dot(v_ref[row][:, :ORB], blocks_ref[s * SLOTS + t], preferred_element_type=f32)
            acc_ref[col] += both[:VS] + both[VS:]
        return carry

    lax.fori_loop(0, SOURCES, one_source, 0)
    for chunk in range(GROUPS):
        x = acc_ref[chunk * GROUPS : (chunk + 1) * GROUPS].reshape(LANES, LANES)
        x = x + pltpu.roll(x, 64, 1)
        out_ref[chunk] = x.T[:ORB]


def direct_kernel(pos_ref, me_ref, cols_ref, blocks_ref, out_ref, v_ref, acc_ref):
    split_terms(cols_ref, v_ref)
    acc_ref[...] = jnp.zeros_like(acc_ref)
    my_r, my_y = me_ref[0], me_ref[1]

    def one_source(s, carry):
        for t in range(SLOTS):
            if t < TILES:
                row, col = row_col(pos_ref, s, t)
            else:
                row, col = my_y * GROUPS + s, my_r * GROUPS + s
            both = lax.dot_general(
                v_ref[col], blocks_ref[s * SLOTS + t], (((1,), (1,)), ((), ())),
                preferred_element_type=f32,
            )
            acc_ref[row, :, 0:ORB] += both[:VS] + both[VS:]
        return carry

    lax.fori_loop(0, SOURCES, one_source, 0)
    for chunk in range(GROUPS):
        x = acc_ref[chunk * GROUPS : (chunk + 1) * GROUPS].reshape(LANES, LANES)
        out_ref[chunk] = x.T[:ORB]


def product(kernel, name, scalars, field, blocks):
    smem = pl.BlockSpec(memory_space=pltpu.SMEM)
    return pl.pallas_call(
        kernel,
        out_shape=jax.ShapeDtypeStruct((GROUPS, ORB, LANES), f32),
        in_specs=[smem] * len(scalars) + vmem(2),
        out_specs=vmem(1)[0],
        scratch_shapes=[
            pltpu.VMEM((GROUPS * GROUPS, 2 * VS, LANES), bf16),
            pltpu.VMEM((GROUPS * GROUPS, VS, LANES), f32),
        ],
        compiler_params=params(),
        cost_estimate=pl.CostEstimate(flops=200000000, bytes_accessed=4000000, transcendentals=0),
        name=name,
    )(*scalars, field, blocks)


def spread_kernel(in_ref, out_ref):
    lane = lane_iota()
    for y in range(N_Y):
        for z in range(N_ZH):
            total = jnp.zeros((ORB, LANES), f32)
            for h in range(N_ZH):
                for k in range(N_CORE):
                    target = h * 2 * VS + k * VS
                    x = roll_to(in_ref[h, y], k * 64 + z * VS, target)
                    inside = (lane >= target) & (lane < target + VS)
                    total = jnp.where(inside, x, total)
            out_ref[z * N_Y + y] = total


def spread(gathered):
    return pl.pallas_call(
        spread_kernel,
        out_shape=jax.ShapeDtypeStruct((N_ZH * N_Y, ORB, LANES), f32),
        in_specs=vmem(1),
        out_specs=vmem(1)[0],
        compiler_params=params(),
        name="spread",
    )(gathered)


def exchange(x, axes):
    return lax.all_to_all(x, axes, split_axis=0, concat_axis=0, tiled=True)


def gather(x, axes, n):
    return exchange(jnp.broadcast_to(x[None], (n,) + x.shape), axes)


def body(vectors, tiles, tile_pos, diag_blocks):
    zh = lax.axis_index("zh")
    y = lax.axis_index("y")
    r = lax.axis_index("x") * N_ZL + lax.axis_index("zl")
    core = lax.axis_index("core")
    me = jnp.stack([r, y]).astype(jnp.int32)

    packed = pack(tiles[0, 0], diag_blocks[0], tile_pos[0, 0])
    packed = gather(packed, "zh", N_ZH)

    sliced = slice_vectors(zh.reshape(1).astype(jnp.int32), vectors.reshape(-1, ORB, LANES))
    mine = lax.dynamic_index_in_dim(sliced, core, 0, keepdims=False)
    other = lax.dynamic_index_in_dim(sliced, 1 - core, 0, keepdims=False)
    other = lax.ppermute(other, "core", [(0, 1), (1, 0)])
    rows = join_cores(core.reshape(1).astype(jnp.int32), mine, other)
    current = lax.dynamic_index_in_dim(rows, y, 0, keepdims=False)
    packed, rows = lax.optimization_barrier((packed, rows))
    packed = gather(packed.reshape(N_ZH * ORB, WIDE), "core", N_CORE)
    packed, first = lax.optimization_barrier((packed, current))
    cols = gather(first, ROW_AX, N_R)
    blocks, where = unpack(packed.reshape(SOURCES, ORB, WIDE))

    centre = 0.5 * (filter_high + filter_low)
    half_width = 0.5 * (filter_high - filter_low)
    previous = None
    for step in range(DEGREE):
        out_cols = product(mirror_kernel, "mirror", (where,), rows, blocks)
        got_cols = exchange(out_cols, ROW_AX)
        out_rows = product(direct_kernel, "direct", (where, me), cols, blocks)
        got_rows = exchange(out_rows, "y")
        image = jnp.sum(got_cols, 0) + jnp.sum(got_rows, 0)
        shifted = (image - centre * current) / half_width
        following = shifted if previous is None else 2.0 * shifted - previous
        previous, current = current, following
        if step < DEGREE - 1:
            rows = gather(current, "y", N_Y)
            cols = gather(current, ROW_AX, N_R)

    lane = lane_iota()
    swapped = jnp.concatenate([current[:, 64:], current[:, :64]], axis=1)
    mine = (lane // 64) == core
    first = jnp.where(core == 0, current, swapped)
    second = jnp.where(core == 1, current, swapped)
    halves = jnp.where(mine[None], jnp.stack([first, second]), 0.0)
    result = jnp.sum(exchange(halves, "core"), 0)
    result = gather(result, ("zh", "y"), N_ZH * N_Y).reshape(N_ZH, N_Y, ORB, LANES)
    return spread(result).reshape(vectors.shape)


def solution(mesh):
    fine = Mesh(
        mesh.devices.reshape(N_X, N_ZL, N_CORE, N_ZH, N_Y), ("x", "zl", "core", "zh", "y")
    )
    row, col = ("x", "zl", "core"), ("zh", "y")
    return jax.shard_map(
        body,
        mesh=fine,
        in_specs=(
            P(row, None),
            P(row, col, None, None, None),
            P(row, col, None, None),
            P(row + col, None, None),
        ),
        out_specs=P(row, None),
        check_vma=False,
    )
```

```python
import functools

import jax
import jax.numpy as jnp
from jax import lax
from jax.experimental import pallas as pl
from jax.experimental.pallas import tpu as pltpu
from jax.sharding import Mesh, PartitionSpec as P

ORB = 56
DEGREE = 3
LANES = 128
N_X, N_ZL, N_CORE, N_ZH, N_Y = 4, 2, 2, 4, 8
N_R = N_X * N_ZL
TILES = 10
SLOTS = TILES + 1
SOURCES = N_CORE * N_Y
WIDE = 640
VS = 8
PLACE = SLOTS * ORB - (WIDE - LANES)
ROW_AX = ("x", "zl")
GROUPS = N_CORE * N_Y

filter_low = 0.0
filter_high = 8.0

f32 = jnp.float32
bf16 = jnp.bfloat16


def params():
    return pltpu.CompilerParams(vmem_limit_bytes=40 * 1024 * 1024)


def vmem(n):
    return [pl.BlockSpec(memory_space=pltpu.VMEM)] * n


def lane_iota(rows=ORB):
    return lax.broadcasted_iota(jnp.int32, (rows, LANES), 1)


def roll_to(x, source, target):
    shift = (target - source) % LANES
    return x if shift == 0 else pltpu.roll(x, shift, 1)


def pack_kernel(tiles_ref, diag_ref, pos_ref, out_ref):
    lane = lane_iota()
    pieces = [tiles_ref[t] for t in range(TILES)] + [diag_ref[...]]
    wide = [
        jnp.concatenate([p, jnp.zeros((ORB, LANES - ORB), f32)], axis=1) for p in pieces
    ]
    gap = jnp.zeros((1, LANES - 2 * TILES), f32)
    both = pos_ref[...].astype(f32)
    places = jnp.concatenate([both[0:1], both[1:2], gap], axis=1)
    places = jnp.broadcast_to(places, (ORB, LANES))
    for q in range(WIDE // LANES):
        total = jnp.zeros((ORB, LANES), f32)
        for t in range(SLOTS):
            start = t * ORB - q * LANES
            if start <= -ORB or start >= LANES:
                continue
            inside = (lane >= max(start, 0)) & (lane < min(start + ORB, LANES))
            total = jnp.where(inside, roll_to(wide[t], 0, start), total)
        if q == WIDE // LANES - 1:
            start = SLOTS * ORB - q * LANES
            total = jnp.where(lane >= start, roll_to(places, 0, start), total)
        out_ref[:, q * LANES : (q + 1) * LANES] = total


def pack(tile_data, diag, places):
    return pl.pallas_call(
        pack_kernel,
        out_shape=jax.ShapeDtypeStruct((ORB, WIDE), f32),
        in_specs=vmem(3),
        out_specs=vmem(1)[0],
        compiler_params=params(),
        name="pack",
    )(tile_data, diag, places)


def two_terms(x):
    high = x.astype(bf16).astype(f32)
    low = x - high
    return (high + pltpu.roll(low, 64, 1)).astype(bf16)


def unpack_kernel(in_ref, blocks_ref, places_ref):
    lane = lane_iota()

    def one_source(s, carry):
        for t in range(SLOTS):
            start = t * ORB
            q, off = start // LANES, start % LANES
            x = roll_to(in_ref[s, :, q * LANES : (q + 1) * LANES], off, 0)
            if off + ORB > LANES:
                y = roll_to(in_ref[s, :, (q + 1) * LANES : (q + 2) * LANES], off, 0)
                x = jnp.where(lane < LANES - off, x, y)
            blocks_ref[s * SLOTS + t] = two_terms(jnp.where(lane < ORB, x, 0.0))
        return carry

    lax.fori_loop(0, SOURCES, one_source, 0)
    for s in range(SOURCES):
        last = in_ref[s, 0:1, WIDE - LANES : WIDE]
        shown = lax.broadcasted_iota(jnp.int32, (1, LANES), 1) >= PLACE
        places_ref[s : s + 1] = jnp.where(shown, last, 0.0).astype(jnp.int32)


def unpack(packed):
    return pl.pallas_call(
        unpack_kernel,
        out_shape=(
            jax.ShapeDtypeStruct((SOURCES * SLOTS, ORB, LANES), bf16),
            jax.ShapeDtypeStruct((SOURCES, LANES), jnp.int32),
        ),
        in_specs=vmem(1),
        out_specs=tuple(vmem(2)),
        compiler_params=params(),
        name="unpack",
    )(packed)


def slice_kernel(y_ref, in_ref, out_ref):
    lane = lane_iota()
    start = y_ref[0] * (2 * VS)
    for zp in range(N_ZH // 2):
        for k in range(N_CORE):
            total = jnp.zeros((ORB, LANES), f32)
            for half in range(2):
                for y in range(N_Y):
                    target = half * 64 + y * VS
                    x = in_ref[(2 * zp + half) * N_Y + y]
                    shift = lax.rem(target - k * VS + LANES - start + LANES, LANES)
                    x = pltpu.roll(x, shift, 1)
                    inside = (lane >= target) & (lane < target + VS)
                    total = jnp.where(inside, x, total)
            out_ref[k, zp] = total


def slice_vectors(y, blocks):
    return pl.pallas_call(
        slice_kernel,
        out_shape=jax.ShapeDtypeStruct((N_CORE, N_ZH // 2, ORB, LANES), f32),
        in_specs=[pl.BlockSpec(memory_space=pltpu.SMEM)] + vmem(1),
        out_specs=vmem(1)[0],
        compiler_params=params(),
        name="slice_vectors",
    )(y, blocks)


def join_kernel(core_ref, mine_ref, other_ref, out_ref):
    lane = lane_iota()
    is_zero = core_ref[0] == 0
    for zp in range(N_ZH // 2):
        mine, other = mine_ref[zp], other_ref[zp]
        a = jnp.where(is_zero, mine, other)
        b = jnp.where(is_zero, other, mine)
        out_ref[2 * zp] = jnp.where(lane < 64, a, pltpu.roll(b, 64, 1))
        out_ref[2 * zp + 1] = jnp.where(lane < 64, pltpu.roll(a, 64, 1), b)


def join_cores(core, mine, other):
    return pl.pallas_call(
        join_kernel,
        out_shape=jax.ShapeDtypeStruct((N_ZH, ORB, LANES), f32),
        in_specs=[pl.BlockSpec(memory_space=pltpu.SMEM)] + vmem(2),
        out_specs=vmem(1)[0],
        compiler_params=params(),
        name="join_cores",
    )(core, mine, other)


def split_terms(src_ref, dst_ref):
    gap = jnp.zeros((64 - ORB, LANES), f32)
    for chunk in range(src_ref.shape[0]):
        x = src_ref[chunk]
        x = jnp.concatenate([x, gap, x, gap], axis=0).T
        high = x.astype(bf16).astype(f32)
        low = x - high
        for o in range(GROUPS):
            rows = slice(o * VS, (o + 1) * VS)
            both = jnp.concatenate([high[rows], low[rows]], axis=0)
            dst_ref[chunk * GROUPS + o] = both.astype(bf16)


def row_col(pos_ref, s, t):
    i, g = pos_ref[s, PLACE + t], pos_ref[s, PLACE + TILES + t]
    row = (i >> 3) * GROUPS + (s >> 3) * N_Y + (i & 7)
    col = (g >> 1) * GROUPS + (g & 1) * N_Y + (s & 7)
    return row, col


def mirror_kernel(pos_ref, rows_ref, blocks_ref, out_ref, v_ref, acc_ref):
    split_terms(rows_ref, v_ref)
    acc_ref[...] = jnp.zeros_like(acc_ref)

    def one_source(s, carry):
        for t in range(TILES):
            row, col = row_col(pos_ref, s, t)
            both = jnp.dot(v_ref[row][:, :ORB], blocks_ref[s * SLOTS + t], preferred_element_type=f32)
            acc_ref[col] += both[:VS] + both[VS:]
        return carry

    lax.fori_loop(0, SOURCES, one_source, 0)
    for chunk in range(out_ref.shape[0]):
        x = acc_ref[chunk * GROUPS : (chunk + 1) * GROUPS].reshape(LANES, LANES)
        x = x + pltpu.roll(x, 64, 1)
        out_ref[chunk] = x.T[:ORB]


def direct_kernel(pos_ref, me_ref, cols_ref, blocks_ref, out_ref, v_ref, acc_ref):
    split_terms(cols_ref, v_ref)
    acc_ref[...] = jnp.zeros_like(acc_ref)
    my_r, my_zh = me_ref[0], me_ref[1]

    def one_source(s, carry):
        for t in range(SLOTS):
            if t < TILES:
                row, col = row_col(pos_ref, s, t)
            else:
                row, col = my_zh * GROUPS + s, my_r * GROUPS + s
            both = lax.dot_general(
                v_ref[col], blocks_ref[s * SLOTS + t], (((1,), (1,)), ((), ())),
                preferred_element_type=f32,
            )
            acc_ref[row, :, 0:ORB] += both[:VS] + both[VS:]
        return carry

    lax.fori_loop(0, SOURCES, one_source, 0)
    for chunk in range(out_ref.shape[0]):
        x = acc_ref[chunk * GROUPS : (chunk + 1) * GROUPS].reshape(LANES, LANES)
        out_ref[chunk] = x.T[:ORB]


def product(kernel, name, scalars, field, blocks, chunks):
    smem = pl.BlockSpec(memory_space=pltpu.SMEM)
    return pl.pallas_call(
        kernel,
        out_shape=jax.ShapeDtypeStruct((chunks, ORB, LANES), f32),
        in_specs=[smem] * len(scalars) + vmem(2),
        out_specs=vmem(1)[0],
        scratch_shapes=[
            pltpu.VMEM((field.shape[0] * GROUPS, 2 * VS, LANES), bf16),
            pltpu.VMEM((chunks * GROUPS, VS, LANES), f32),
        ],
        compiler_params=params(),
        cost_estimate=pl.CostEstimate(flops=200000000, bytes_accessed=4000000, transcendentals=0),
        name=name,
    )(*scalars, field, blocks)


def halve_kernel(core_ref, in_ref, out_ref):
    lane = lane_iota()
    core = core_ref[0]
    mine = ((lane >> 3) & 1) == core
    for z in range(N_ZH):
        for k in range(N_CORE):
            x = in_ref[z] if k == 0 else pltpu.roll(in_ref[z], 64, 1)
            x = jnp.where(lane < 64, x, 0.0)
            for step in (32, 16, 8):
                block = lane & (4 * step - 1)
                moved = pltpu.roll(x, step, 1)
                x = jnp.where(block < step, x, jnp.where((block >= 2 * step) & (block < 3 * step), moved, 0.0))
            out_ref[k, z] = jnp.where(mine, pltpu.roll(x, core * VS, 1), 0.0)


def halve(core, current):
    return pl.pallas_call(
        halve_kernel,
        out_shape=jax.ShapeDtypeStruct((N_CORE, N_ZH, ORB, LANES), f32),
        in_specs=[pl.BlockSpec(memory_space=pltpu.SMEM)] + vmem(1),
        out_specs=vmem(1)[0],
        compiler_params=params(),
        name="halve",
    )(core, current)


def spread_kernel(in_ref, out_ref):
    lane = lane_iota()
    for z in range(N_ZH):
        x = [in_ref[y, z] for y in range(N_Y)]
        for d in (4, 2, 1):
            upper = (lane & (16 * d)) != 0
            for a in range(N_Y):
                if a & d:
                    continue
                low, high = x[a], x[a + d]
                x[a] = jnp.where(upper, pltpu.roll(high, 16 * d, 1), low)
                x[a + d] = jnp.where(upper, high, pltpu.roll(low, LANES - 16 * d, 1))
        for y in range(N_Y):
            out_ref[z * N_Y + y] = x[y]


def spread(gathered):
    return pl.pallas_call(
        spread_kernel,
        out_shape=jax.ShapeDtypeStruct((N_ZH * N_Y, ORB, LANES), f32),
        in_specs=vmem(1),
        out_specs=vmem(1)[0],
        compiler_params=params(),
        name="spread",
    )(gathered)


def exchange(x, axes):
    return lax.all_to_all(x, axes, split_axis=0, concat_axis=0, tiled=True)


def gather(x, axes, n):
    return exchange(jnp.broadcast_to(x[None], (n,) + x.shape), axes)


def body(vectors, tiles, tile_pos, diag_blocks):
    zh = lax.axis_index("zh")
    y = lax.axis_index("y")
    r = lax.axis_index("x") * N_ZL + lax.axis_index("zl")
    core = lax.axis_index("core")
    me = jnp.stack([r, zh]).astype(jnp.int32)

    packed = pack(tiles[0, 0], diag_blocks[0], tile_pos[0, 0])
    packed = gather(packed, "y", N_Y)

    sliced = slice_vectors(y.reshape(1).astype(jnp.int32), vectors.reshape(-1, ORB, LANES))
    mine = lax.dynamic_index_in_dim(sliced, core, 0, keepdims=False)
    other = lax.dynamic_index_in_dim(sliced, 1 - core, 0, keepdims=False)
    other = lax.ppermute(other, "core", [(0, 1), (1, 0)])
    core_ref = core.reshape(1).astype(jnp.int32)
    current = join_cores(core_ref, mine, other)

    own = lax.dynamic_index_in_dim(current, zh, 0, keepdims=False)
    packed, current, own = lax.optimization_barrier((packed, current, own))
    packed = gather(packed.reshape(N_Y * ORB, WIDE), "core", N_CORE)
    packed, own = lax.optimization_barrier((packed, own))
    cols = gather(own, ROW_AX, N_R)
    blocks, where = unpack(packed.reshape(SOURCES, ORB, WIDE))

    centre = 0.5 * (filter_high + filter_low)
    half_width = 0.5 * (filter_high - filter_low)
    at_own = (lax.broadcasted_iota(jnp.int32, (N_ZH, 1, 1), 0) == zh)
    previous = None
    for step in range(DEGREE):
        out_cols = product(mirror_kernel, "mirror", (where,), current, blocks, N_R)
        out_cols, cols = lax.optimization_barrier((out_cols, cols))
        got_cols = exchange(out_cols, ROW_AX)
        out_rows = product(direct_kernel, "direct", (where, me), cols, blocks, N_ZH)
        partial = out_rows + jnp.where(at_own, jnp.sum(got_cols, 0)[None], 0.0)
        image = jnp.sum(gather(partial, "zh", N_ZH).reshape(N_ZH, N_ZH, ORB, LANES), 0)
        shifted = (image - centre * current) / half_width
        following = shifted if previous is None else 2.0 * shifted - previous
        previous, current = current, following
        if step < DEGREE - 1:
            cols = gather(lax.dynamic_index_in_dim(current, zh, 0, keepdims=False), ROW_AX, N_R)

    result = jnp.sum(exchange(halve(core_ref, current), "core"), 0)
    result = gather(result, "y", N_Y).reshape(N_Y, N_ZH, ORB, LANES)
    return spread(result).reshape(vectors.shape)


def solution(mesh):
    fine = Mesh(
        mesh.devices.reshape(N_X, N_ZL, N_CORE, N_ZH, N_Y), ("x", "zl", "core", "zh", "y")
    )
    row, col = ("x", "zl", "core"), ("zh", "y")
    return jax.shard_map(
        body,
        mesh=fine,
        in_specs=(
            P(row, None),
            P(row, col, None, None, None),
            P(row, col, None, None),
            P(row + col, None, None),
        ),
        out_specs=P(row, None),
        check_vma=False,
    )
```

```python
import functools

import jax
import jax.numpy as jnp
from jax import lax
from jax.experimental import pallas as pl
from jax.experimental.pallas import tpu as pltpu
from jax.sharding import Mesh, PartitionSpec as P

ORB = 56
DEGREE = 3
LANES = 128
N_X, N_ZL, N_CORE, N_ZH, N_Y = 4, 2, 2, 4, 8
N_R = N_X * N_ZL
TILES = 10
SLOTS = TILES + 1
WIDE = 640
VS = 8
PLACE = SLOTS * ORB - (WIDE - LANES)
ROW_AX = ("x", "zl")
GROUPS = N_CORE * N_Y

filter_low = 0.0
filter_high = 8.0

f32 = jnp.float32
bf16 = jnp.bfloat16


def params():
    return pltpu.CompilerParams(vmem_limit_bytes=40 * 1024 * 1024)


def vmem(n):
    return [pl.BlockSpec(memory_space=pltpu.VMEM)] * n


def lane_iota(rows=ORB):
    return lax.broadcasted_iota(jnp.int32, (rows, LANES), 1)


def roll_to(x, source, target):
    shift = (target - source) % LANES
    return x if shift == 0 else pltpu.roll(x, shift, 1)


def pack_kernel(tiles_ref, diag_ref, pos_ref, out_ref):
    lane = lane_iota()
    pieces = [tiles_ref[t] for t in range(TILES)] + [diag_ref[...]]
    wide = [
        jnp.concatenate([p, jnp.zeros((ORB, LANES - ORB), f32)], axis=1) for p in pieces
    ]
    gap = jnp.zeros((1, LANES - 2 * TILES), f32)
    both = pos_ref[...].astype(f32)
    places = jnp.concatenate([both[0:1], both[1:2], gap], axis=1)
    places = jnp.broadcast_to(places, (ORB, LANES))
    for q in range(WIDE // LANES):
        total = jnp.zeros((ORB, LANES), f32)
        for t in range(SLOTS):
            start = t * ORB - q * LANES
            if start <= -ORB or start >= LANES:
                continue
            inside = (lane >= max(start, 0)) & (lane < min(start + ORB, LANES))
            total = jnp.where(inside, roll_to(wide[t], 0, start), total)
        if q == WIDE // LANES - 1:
            start = SLOTS * ORB - q * LANES
            total = jnp.where(lane >= start, roll_to(places, 0, start), total)
        out_ref[:, q * LANES : (q + 1) * LANES] = total


def pack(tile_data, diag, places):
    return pl.pallas_call(
        pack_kernel,
        out_shape=jax.ShapeDtypeStruct((ORB, WIDE), f32),
        in_specs=vmem(3),
        out_specs=vmem(1)[0],
        compiler_params=params(),
        name="pack",
    )(tile_data, diag, places)


def two_terms(x):
    high = x.astype(bf16).astype(f32)
    low = x - high
    return (high + pltpu.roll(low, 64, 1)).astype(bf16)


def unpack_kernel(in_ref, blocks_ref, places_ref):
    lane = lane_iota()

    def one_source(s, carry):
        for t in range(SLOTS):
            start = t * ORB
            q, off = start // LANES, start % LANES
            x = roll_to(in_ref[s, :, q * LANES : (q + 1) * LANES], off, 0)
            if off + ORB > LANES:
                y = roll_to(in_ref[s, :, (q + 1) * LANES : (q + 2) * LANES], off, 0)
                x = jnp.where(lane < LANES - off, x, y)
            blocks_ref[s * SLOTS + t] = two_terms(jnp.where(lane < ORB, x, 0.0))
        return carry

    lax.fori_loop(0, N_Y, one_source, 0)
    for s in range(N_Y):
        last = in_ref[s, 0:1, WIDE - LANES : WIDE]
        shown = lax.broadcasted_iota(jnp.int32, (1, LANES), 1) >= PLACE
        places_ref[s : s + 1] = jnp.where(shown, last, 0.0).astype(jnp.int32)


def unpack(packed):
    return pl.pallas_call(
        unpack_kernel,
        out_shape=(
            jax.ShapeDtypeStruct((N_Y * SLOTS, ORB, LANES), bf16),
            jax.ShapeDtypeStruct((N_Y, LANES), jnp.int32),
        ),
        in_specs=vmem(1),
        out_specs=tuple(vmem(2)),
        compiler_params=params(),
        name="unpack",
    )(packed)


def slice_kernel(me_ref, in_ref, mine_ref, other_ref, own_ref):
    lane = lane_iota()
    zh, core, start = me_ref[1], me_ref[2], me_ref[3] * (2 * VS)

    def placed(block, k, target):
        shift = lax.rem(target - k * VS + 2 * LANES - start, LANES)
        return pltpu.roll(in_ref[block], shift, 1)

    for out_ref, k in ((mine_ref, core), (other_ref, 1 - core)):
        for zp in range(N_ZH // 2):
            total = jnp.zeros((ORB, LANES), f32)
            for half in range(2):
                for y in range(N_Y):
                    target = half * 64 + y * VS
                    inside = (lane >= target) & (lane < target + VS)
                    total = jnp.where(inside, placed((2 * zp + half) * N_Y + y, k, target), total)
            out_ref[zp] = total
    total = jnp.zeros((ORB, LANES), f32)
    for k in range(N_CORE):
        for y in range(N_Y):
            target = k * 64 + y * VS
            inside = (lane >= target) & (lane < target + VS)
            total = jnp.where(inside, placed(zh * N_Y + y, k, target), total)
    own_ref[...] = total


def slice_vectors(me, blocks):
    pair = jax.ShapeDtypeStruct((N_ZH // 2, ORB, LANES), f32)
    return pl.pallas_call(
        slice_kernel,
        out_shape=(pair, pair, jax.ShapeDtypeStruct((ORB, LANES), f32)),
        in_specs=[pl.BlockSpec(memory_space=pltpu.SMEM)] + vmem(1),
        out_specs=tuple(vmem(3)),
        compiler_params=params(),
        name="slice_vectors",
    )(me, blocks)


def join_kernel(me_ref, mine_ref, other_ref, out_ref):
    lane = lane_iota()
    is_zero = me_ref[2] == 0
    for zp in range(N_ZH // 2):
        mine, other = mine_ref[zp], other_ref[zp]
        a = jnp.where(is_zero, mine, other)
        b = jnp.where(is_zero, other, mine)
        out_ref[2 * zp] = jnp.where(lane < 64, a, pltpu.roll(b, 64, 1))
        out_ref[2 * zp + 1] = jnp.where(lane < 64, pltpu.roll(a, 64, 1), b)


def join_cores(me, mine, other):
    return pl.pallas_call(
        join_kernel,
        out_shape=jax.ShapeDtypeStruct((N_ZH, ORB, LANES), f32),
        in_specs=[pl.BlockSpec(memory_space=pltpu.SMEM)] + vmem(2),
        out_specs=vmem(1)[0],
        compiler_params=params(),
        name="join_cores",
    )(me, mine, other)


def pick_kernel(me_ref, in_ref, out_ref):
    lane = lane_iota()
    is_zero = me_ref[2] == 0
    for r in range(N_R):
        a, b = in_ref[2 * r], in_ref[2 * r + 1]
        first = jnp.where(is_zero, a, pltpu.roll(a, 64, 1))
        second = jnp.where(is_zero, pltpu.roll(b, 64, 1), b)
        out_ref[r] = jnp.where(lane < 64, first, second)


def pick_half(me, gathered):
    return pl.pallas_call(
        pick_kernel,
        out_shape=jax.ShapeDtypeStruct((N_R, ORB, LANES), f32),
        in_specs=[pl.BlockSpec(memory_space=pltpu.SMEM)] + vmem(1),
        out_specs=vmem(1)[0],
        compiler_params=params(),
        name="pick_half",
    )(me, gathered)


def split_terms(src_ref, dst_ref):
    gap = jnp.zeros((64 - ORB, LANES), f32)
    for chunk in range(src_ref.shape[0]):
        x = src_ref[chunk]
        x = jnp.concatenate([x, gap, x, gap], axis=0).T
        high = x.astype(bf16).astype(f32)
        low = x - high
        for o in range(GROUPS):
            rows = slice(o * VS, (o + 1) * VS)
            both = jnp.concatenate([high[rows], low[rows]], axis=0)
            dst_ref[chunk * GROUPS + o] = both.astype(bf16)


def row_col(pos_ref, core_s, s, t):
    i, g = pos_ref[s, PLACE + t], pos_ref[s, PLACE + TILES + t]
    row = (i >> 3) * GROUPS + core_s * N_Y + (i & 7)
    col = (g >> 1) * GROUPS + (g & 1) * N_Y + s
    return row, col


def mirror_kernel(me_ref, pos_a_ref, pos_b_ref, rows_ref, blocks_a_ref, blocks_b_ref, out_ref, v_ref, acc_ref):
    split_terms(rows_ref, v_ref)
    acc_ref[...] = jnp.zeros_like(acc_ref)
    core = me_ref[2]
    for pos_ref, blocks_ref, core_s in ((pos_a_ref, blocks_a_ref, core), (pos_b_ref, blocks_b_ref, 1 - core)):

        def one_source(s, carry, pos_ref=pos_ref, blocks_ref=blocks_ref, core_s=core_s):
            for t in range(TILES):
                row, col = row_col(pos_ref, core_s, s, t)
                both = jnp.dot(v_ref[row][:, :ORB], blocks_ref[s * SLOTS + t], preferred_element_type=f32)
                acc_ref[col] += both[:VS] + both[VS:]
            return carry

        lax.fori_loop(0, N_Y, one_source, 0)
    for chunk in range(out_ref.shape[0]):
        x = acc_ref[chunk * GROUPS : (chunk + 1) * GROUPS].reshape(LANES, LANES)
        x = x + pltpu.roll(x, 64, 1)
        out_ref[chunk] = x.T[:ORB]


def direct_kernel(me_ref, pos_a_ref, pos_b_ref, cols_ref, blocks_a_ref, blocks_b_ref, out_ref, v_ref, acc_ref):
    split_terms(cols_ref, v_ref)
    acc_ref[...] = jnp.zeros_like(acc_ref)
    my_r, my_zh, core = me_ref[0], me_ref[1], me_ref[2]
    for pos_ref, blocks_ref, core_s in ((pos_a_ref, blocks_a_ref, core), (pos_b_ref, blocks_b_ref, 1 - core)):

        def one_source(s, carry, pos_ref=pos_ref, blocks_ref=blocks_ref, core_s=core_s):
            for t in range(SLOTS):
                if t < TILES:
                    row, col = row_col(pos_ref, core_s, s, t)
                else:
                    row = my_zh * GROUPS + core_s * N_Y + s
                    col = my_r * GROUPS + core_s * N_Y + s
                both = lax.dot_general(
                    v_ref[col], blocks_ref[s * SLOTS + t], (((1,), (1,)), ((), ())),
                    preferred_element_type=f32,
                )
                acc_ref[row, :, 0:ORB] += both[:VS] + both[VS:]
            return carry

        lax.fori_loop(0, N_Y, one_source, 0)
    for chunk in range(out_ref.shape[0]):
        x = acc_ref[chunk * GROUPS : (chunk + 1) * GROUPS].reshape(LANES, LANES)
        out_ref[chunk] = x.T[:ORB]


def product(kernel, name, scalars, field, blocks, chunks):
    smem = pl.BlockSpec(memory_space=pltpu.SMEM)
    return pl.pallas_call(
        kernel,
        out_shape=jax.ShapeDtypeStruct((chunks, ORB, LANES), f32),
        in_specs=[smem] * len(scalars) + vmem(1 + len(blocks)),
        out_specs=vmem(1)[0],
        scratch_shapes=[
            pltpu.VMEM((field.shape[0] * GROUPS, 2 * VS, LANES), bf16),
            pltpu.VMEM((chunks * GROUPS, VS, LANES), f32),
        ],
        compiler_params=params(),
        cost_estimate=pl.CostEstimate(flops=200000000, bytes_accessed=4000000, transcendentals=0),
        name=name,
    )(*scalars, field, *blocks)


def halve_kernel(me_ref, in_ref, out_ref):
    lane = lane_iota()
    core = me_ref[2]
    mine = ((lane >> 3) & 1) == core
    for z in range(N_ZH):
        for k in range(N_CORE):
            x = in_ref[z] if k == 0 else pltpu.roll(in_ref[z], 64, 1)
            x = jnp.where(lane < 64, x, 0.0)
            for step in (32, 16, 8):
                block = lane & (4 * step - 1)
                moved = pltpu.roll(x, step, 1)
                x = jnp.where(block < step, x, jnp.where((block >= 2 * step) & (block < 3 * step), moved, 0.0))
            out_ref[k, z] = jnp.where(mine, pltpu.roll(x, core * VS, 1), 0.0)


def halve(me, current):
    return pl.pallas_call(
        halve_kernel,
        out_shape=jax.ShapeDtypeStruct((N_CORE, N_ZH, ORB, LANES), f32),
        in_specs=[pl.BlockSpec(memory_space=pltpu.SMEM)] + vmem(1),
        out_specs=vmem(1)[0],
        compiler_params=params(),
        name="halve",
    )(me, current)


def spread_kernel(in_ref, out_ref):
    lane = lane_iota()
    for z in range(N_ZH):
        x = [in_ref[y, z] for y in range(N_Y)]
        for d in (4, 2, 1):
            upper = (lane & (16 * d)) != 0
            for a in range(N_Y):
                if a & d:
                    continue
                low, high = x[a], x[a + d]
                x[a] = jnp.where(upper, pltpu.roll(high, 16 * d, 1), low)
                x[a + d] = jnp.where(upper, high, pltpu.roll(low, LANES - 16 * d, 1))
        for y in range(N_Y):
            out_ref[z * N_Y + y] = x[y]


def spread(gathered):
    return pl.pallas_call(
        spread_kernel,
        out_shape=jax.ShapeDtypeStruct((N_ZH * N_Y, ORB, LANES), f32),
        in_specs=vmem(1),
        out_specs=vmem(1)[0],
        compiler_params=params(),
        name="spread",
    )(gathered)


def exchange(x, axes):
    return lax.all_to_all(x, axes, split_axis=0, concat_axis=0, tiled=True)


def gather(x, axes, n):
    return exchange(jnp.broadcast_to(x[None], (n,) + x.shape), axes)


def body(vectors, tiles, tile_pos, diag_blocks):
    zh = lax.axis_index("zh")
    r = lax.axis_index("x") * N_ZL + lax.axis_index("zl")
    me = jnp.stack([r, zh, lax.axis_index("core"), lax.axis_index("y")]).astype(jnp.int32)
    swap = [(0, 1), (1, 0)]

    packed = pack(tiles[0, 0], diag_blocks[0], tile_pos[0, 0])
    packed = gather(packed, "y", N_Y)

    mine, other, own = slice_vectors(me, vectors.reshape(-1, ORB, LANES))
    cols = pick_half(me, lax.all_gather(own, ("x", "zl", "core"), axis=0, tiled=False))
    current = join_cores(me, mine, lax.ppermute(other, "core", swap))

    packed, current, cols = lax.optimization_barrier((packed, current, cols))
    blocks_a, pos_a = unpack(packed)
    blocks_b, pos_b = unpack(lax.ppermute(packed, "core", swap))
    where, blocks = (me, pos_a, pos_b), (blocks_a, blocks_b)

    centre = 0.5 * (filter_high + filter_low)
    half_width = 0.5 * (filter_high - filter_low)
    at_own = (lax.broadcasted_iota(jnp.int32, (N_ZH, 1, 1), 0) == zh)
    previous = None
    for step in range(DEGREE):
        out_cols = product(mirror_kernel, "mirror", where, current, blocks, N_R)
        out_cols, cols = lax.optimization_barrier((out_cols, cols))
        got_cols = exchange(out_cols, ROW_AX)
        out_rows = product(direct_kernel, "direct", where, cols, blocks, N_ZH)
        partial = out_rows + jnp.where(at_own, jnp.sum(got_cols, 0)[None], 0.0)
        image = jnp.sum(gather(partial, "zh", N_ZH).reshape(N_ZH, N_ZH, ORB, LANES), 0)
        shifted = (image - centre * current) / half_width
        following = shifted if previous is None else 2.0 * shifted - previous
        previous, current = current, following
        if step < DEGREE - 1:
            cols = gather(lax.dynamic_index_in_dim(current, zh, 0, keepdims=False), ROW_AX, N_R)

    result = jnp.sum(exchange(halve(me, current), "core"), 0)
    result = gather(result, "y", N_Y).reshape(N_Y, N_ZH, ORB, LANES)
    return spread(result).reshape(vectors.shape)


def solution(mesh):
    fine = Mesh(
        mesh.devices.reshape(N_X, N_ZL, N_CORE, N_ZH, N_Y), ("x", "zl", "core", "zh", "y")
    )
    row, col = ("x", "zl", "core"), ("zh", "y")
    return jax.shard_map(
        body,
        mesh=fine,
        in_specs=(
            P(row, None),
            P(row, col, None, None, None),
            P(row, col, None, None),
            P(row + col, None, None),
        ),
        out_specs=P(row, None),
        check_vma=False,
    )
```

```python
import functools

import jax
import jax.numpy as jnp
from jax import lax
from jax.experimental import pallas as pl
from jax.experimental.pallas import tpu as pltpu
from jax.sharding import Mesh, PartitionSpec as P

ORB = 56
DEGREE = 3
LANES = 128
N_X, N_ZL, N_CORE, N_ZH, N_Y = 4, 2, 2, 4, 8
N_R = N_X * N_ZL
TILES = 10
SLOTS = TILES + 1
WIDE = 640
VS = 8
PLACE = SLOTS * ORB - (WIDE - LANES)
ROW_AX = ("x", "zl")
GROUPS = N_CORE * N_Y

filter_low = 0.0
filter_high = 8.0

f32 = jnp.float32
bf16 = jnp.bfloat16


def params():
    return pltpu.CompilerParams(vmem_limit_bytes=40 * 1024 * 1024)


def vmem(n):
    return [pl.BlockSpec(memory_space=pltpu.VMEM)] * n


def lane_iota(rows=ORB):
    return lax.broadcasted_iota(jnp.int32, (rows, LANES), 1)


def roll_to(x, source, target):
    shift = (target - source) % LANES
    return x if shift == 0 else pltpu.roll(x, shift, 1)


def pack_kernel(tiles_hbm, diag_hbm, pos_hbm, out_hbm, tiles_ref, diag_ref, pos_ref, out_ref, sems, out_sems):
    copies = [
        pltpu.make_async_copy(src, dst, sems.at[k])
        for k, (src, dst) in enumerate(((tiles_hbm, tiles_ref), (diag_hbm, diag_ref), (pos_hbm, pos_ref)))
    ]
    for copy in copies:
        copy.start()
    for copy in copies:
        copy.wait()
    lane = lane_iota()
    pieces = [tiles_ref[t] for t in range(TILES)] + [diag_ref[...]]
    wide = [
        jnp.concatenate([p, jnp.zeros((ORB, LANES - ORB), f32)], axis=1) for p in pieces
    ]
    gap = jnp.zeros((1, LANES - 2 * TILES), f32)
    both = pos_ref[...].astype(f32)
    places = jnp.concatenate([both[0:1], both[1:2], gap], axis=1)
    places = jnp.broadcast_to(places, (ORB, LANES))
    for q in range(WIDE // LANES):
        total = jnp.zeros((ORB, LANES), f32)
        for t in range(SLOTS):
            start = t * ORB - q * LANES
            if start <= -ORB or start >= LANES:
                continue
            inside = (lane >= max(start, 0)) & (lane < min(start + ORB, LANES))
            total = jnp.where(inside, roll_to(wide[t], 0, start), total)
        if q == WIDE // LANES - 1:
            start = SLOTS * ORB - q * LANES
            total = jnp.where(lane >= start, roll_to(places, 0, start), total)
        out_ref[:, q * LANES : (q + 1) * LANES] = total
    copies = [pltpu.make_async_copy(out_ref, out_hbm.at[k], out_sems.at[k]) for k in range(N_Y)]
    for copy in copies:
        copy.start()
    for copy in copies:
        copy.wait()


def pack(tile_data, diag, places):
    return pl.pallas_call(
        pack_kernel,
        out_shape=jax.ShapeDtypeStruct((N_Y, ORB, WIDE), f32),
        in_specs=[pl.BlockSpec(memory_space=pl.ANY)] * 3,
        out_specs=pl.BlockSpec(memory_space=pl.ANY),
        scratch_shapes=[
            pltpu.VMEM((TILES, ORB, ORB), f32),
            pltpu.VMEM((ORB, ORB), f32),
            pltpu.VMEM((2, TILES), jnp.int32),
            pltpu.VMEM((ORB, WIDE), f32),
            pltpu.SemaphoreType.DMA((3,)),
            pltpu.SemaphoreType.DMA((N_Y,)),
        ],
        compiler_params=pltpu.CompilerParams(vmem_limit_bytes=56 * 1024 * 1024),
        name="pack",
    )(tile_data, diag, places)


def unpack_kernel(in_ref, blocks_ref, places_ref):
    x = in_ref[...].reshape(N_Y * ORB, WIDE)
    high = x.astype(bf16)
    low = (x - high.astype(f32)).astype(bf16)
    for t in range(SLOTS):
        start = t * ORB
        q, off = start // LANES, start % LANES
        width = LANES if off + ORB <= LANES else 2 * LANES
        source = lax.broadcasted_iota(jnp.int32, (width, LANES), 0)
        target = lax.broadcasted_iota(jnp.int32, (width, LANES), 1)
        window = slice(q * LANES, q * LANES + width)
        total = None
        for term, at in ((high, 0), (low, 64)):
            hit = (target >= at) & (target < at + ORB) & (source == target - at + off)
            part = jnp.dot(term[:, window], jnp.where(hit, 1.0, 0.0).astype(bf16), preferred_element_type=f32)
            total = part if total is None else total + part
        total = total.astype(bf16)
        for s in range(N_Y):
            blocks_ref[s * SLOTS + t] = total[s * ORB : (s + 1) * ORB]
    for s in range(N_Y):
        last = in_ref[s, 0:1, WIDE - LANES : WIDE]
        shown = lax.broadcasted_iota(jnp.int32, (1, LANES), 1) >= PLACE
        places_ref[s : s + 1] = jnp.where(shown, last, 0.0).astype(jnp.int32)


def unpack(packed):
    return pl.pallas_call(
        unpack_kernel,
        out_shape=(
            jax.ShapeDtypeStruct((N_Y * SLOTS, ORB, LANES), bf16),
            jax.ShapeDtypeStruct((N_Y, LANES), jnp.int32),
        ),
        in_specs=vmem(1),
        out_specs=tuple(vmem(2)),
        compiler_params=params(),
        name="unpack",
    )(packed)


def slice_kernel(me_ref, in_ref, mine_ref, other_ref, own_ref):
    lane = lane_iota()
    zh, core, start = me_ref[1], me_ref[2], me_ref[3] * (2 * VS)

    def placed(block, k, target):
        shift = lax.rem(target - k * VS + 2 * LANES - start, LANES)
        return pltpu.roll(in_ref[block], shift, 1)

    for out_ref, k in ((mine_ref, core), (other_ref, 1 - core)):
        for zp in range(N_ZH // 2):
            total = jnp.zeros((ORB, LANES), f32)
            for half in range(2):
                for y in range(N_Y):
                    target = half * 64 + y * VS
                    inside = (lane >= target) & (lane < target + VS)
                    total = jnp.where(inside, placed((2 * zp + half) * N_Y + y, k, target), total)
            out_ref[zp] = total
    total = jnp.zeros((ORB, LANES), f32)
    for k in range(N_CORE):
        for y in range(N_Y):
            target = k * 64 + y * VS
            inside = (lane >= target) & (lane < target + VS)
            total = jnp.where(inside, placed(zh * N_Y + y, k, target), total)
    own_ref[...] = total


def slice_vectors(me, blocks):
    pair = jax.ShapeDtypeStruct((N_ZH // 2, ORB, LANES), f32)
    return pl.pallas_call(
        slice_kernel,
        out_shape=(pair, pair, jax.ShapeDtypeStruct((ORB, LANES), f32)),
        in_specs=[pl.BlockSpec(memory_space=pltpu.SMEM)] + vmem(1),
        out_specs=tuple(vmem(3)),
        compiler_params=params(),
        name="slice_vectors",
    )(me, blocks)


def join_kernel(me_ref, mine_ref, other_ref, out_ref):
    lane = lane_iota()
    is_zero = me_ref[2] == 0
    for zp in range(N_ZH // 2):
        mine, other = mine_ref[zp], other_ref[zp]
        a = jnp.where(is_zero, mine, other)
        b = jnp.where(is_zero, other, mine)
        out_ref[2 * zp] = jnp.where(lane < 64, a, pltpu.roll(b, 64, 1))
        out_ref[2 * zp + 1] = jnp.where(lane < 64, pltpu.roll(a, 64, 1), b)


def join_cores(me, mine, other):
    return pl.pallas_call(
        join_kernel,
        out_shape=jax.ShapeDtypeStruct((N_ZH, ORB, LANES), f32),
        in_specs=[pl.BlockSpec(memory_space=pltpu.SMEM)] + vmem(2),
        out_specs=vmem(1)[0],
        compiler_params=params(),
        name="join_cores",
    )(me, mine, other)


def pick_kernel(me_ref, in_ref, out_ref):
    lane = lane_iota()
    is_zero = me_ref[2] == 0
    for r in range(N_R):
        a, b = in_ref[2 * r], in_ref[2 * r + 1]
        first = jnp.where(is_zero, a, pltpu.roll(a, 64, 1))
        second = jnp.where(is_zero, pltpu.roll(b, 64, 1), b)
        out_ref[r] = jnp.where(lane < 64, first, second)


def pick_half(me, gathered):
    return pl.pallas_call(
        pick_kernel,
        out_shape=jax.ShapeDtypeStruct((N_R, ORB, LANES), f32),
        in_specs=[pl.BlockSpec(memory_space=pltpu.SMEM)] + vmem(1),
        out_specs=vmem(1)[0],
        compiler_params=params(),
        name="pick_half",
    )(me, gathered)


def split_terms(src_ref, dst_ref):
    gap = jnp.zeros((64 - ORB, LANES), f32)
    for chunk in range(src_ref.shape[0]):
        x = src_ref[chunk]
        x = jnp.concatenate([x, gap, x, gap], axis=0).T
        high = x.astype(bf16).astype(f32)
        low = x - high
        for o in range(GROUPS):
            rows = slice(o * VS, (o + 1) * VS)
            both = jnp.concatenate([high[rows], low[rows]], axis=0)
            dst_ref[chunk * GROUPS + o] = both.astype(bf16)


def row_col(pos_ref, core_s, s, t):
    i, g = pos_ref[s, PLACE + t], pos_ref[s, PLACE + TILES + t]
    row = (i >> 3) * GROUPS + core_s * N_Y + (i & 7)
    col = (g >> 1) * GROUPS + (g & 1) * N_Y + s
    return row, col


def mirror_kernel(me_ref, pos_a_ref, pos_b_ref, rows_ref, blocks_a_ref, blocks_b_ref, out_ref, v_ref, acc_ref):
    split_terms(rows_ref, v_ref)
    acc_ref[...] = jnp.zeros_like(acc_ref)
    core = me_ref[2]
    for pos_ref, blocks_ref, core_s in ((pos_a_ref, blocks_a_ref, core), (pos_b_ref, blocks_b_ref, 1 - core)):

        def one_source(s, carry, pos_ref=pos_ref, blocks_ref=blocks_ref, core_s=core_s):
            for t in range(TILES):
                row, col = row_col(pos_ref, core_s, s, t)
                both = jnp.dot(v_ref[row][:, :ORB], blocks_ref[s * SLOTS + t], preferred_element_type=f32)
                acc_ref[col] += both[:VS] + both[VS:]
            return carry

        lax.fori_loop(0, N_Y, one_source, 0)
    for chunk in range(out_ref.shape[0]):
        x = acc_ref[chunk * GROUPS : (chunk + 1) * GROUPS].reshape(LANES, LANES)
        x = x + pltpu.roll(x, 64, 1)
        out_ref[chunk] = x.T[:ORB]


def direct_kernel(me_ref, pos_a_ref, pos_b_ref, cols_ref, blocks_a_ref, blocks_b_ref, out_ref, v_ref, acc_ref):
    split_terms(cols_ref, v_ref)
    acc_ref[...] = jnp.zeros_like(acc_ref)
    my_r, my_zh, core = me_ref[0], me_ref[1], me_ref[2]
    for pos_ref, blocks_ref, core_s in ((pos_a_ref, blocks_a_ref, core), (pos_b_ref, blocks_b_ref, 1 - core)):

        def one_source(s, carry, pos_ref=pos_ref, blocks_ref=blocks_ref, core_s=core_s):
            for t in range(SLOTS):
                if t < TILES:
                    row, col = row_col(pos_ref, core_s, s, t)
                else:
                    row = my_zh * GROUPS + core_s * N_Y + s
                    col = my_r * GROUPS + core_s * N_Y + s
                both = lax.dot_general(
                    v_ref[col], blocks_ref[s * SLOTS + t], (((1,), (1,)), ((), ())),
                    preferred_element_type=f32,
                )
                acc_ref[row, :, 0:ORB] += both[:VS] + both[VS:]
            return carry

        lax.fori_loop(0, N_Y, one_source, 0)
    for chunk in range(out_ref.shape[0]):
        x = acc_ref[chunk * GROUPS : (chunk + 1) * GROUPS].reshape(LANES, LANES)
        out_ref[chunk] = x.T[:ORB]


def product(kernel, name, scalars, field, blocks, chunks):
    smem = pl.BlockSpec(memory_space=pltpu.SMEM)
    return pl.pallas_call(
        kernel,
        out_shape=jax.ShapeDtypeStruct((chunks, ORB, LANES), f32),
        in_specs=[smem] * len(scalars) + vmem(1 + len(blocks)),
        out_specs=vmem(1)[0],
        scratch_shapes=[
            pltpu.VMEM((field.shape[0] * GROUPS, 2 * VS, LANES), bf16),
            pltpu.VMEM((chunks * GROUPS, VS, LANES), f32),
        ],
        compiler_params=params(),
        cost_estimate=pl.CostEstimate(flops=200000000, bytes_accessed=4000000, transcendentals=0),
        name=name,
    )(*scalars, field, *blocks)


def halve_kernel(me_ref, in_ref, out_ref):
    lane = lane_iota()
    core = me_ref[2]
    mine = ((lane >> 3) & 1) == core
    for k in range(N_CORE):
        x = in_ref[...] if k == 0 else pltpu.roll(in_ref[...], 64, 1)
        x = jnp.where(lane < 64, x, 0.0)
        for step in (32, 16, 8):
            block = lane & (4 * step - 1)
            moved = pltpu.roll(x, step, 1)
            x = jnp.where(block < step, x, jnp.where((block >= 2 * step) & (block < 3 * step), moved, 0.0))
        out_ref[k] = jnp.where(mine, pltpu.roll(x, core * VS, 1), 0.0)


def halve(me, current):
    return pl.pallas_call(
        halve_kernel,
        out_shape=jax.ShapeDtypeStruct((N_CORE, ORB, LANES), f32),
        in_specs=[pl.BlockSpec(memory_space=pltpu.SMEM)] + vmem(1),
        out_specs=vmem(1)[0],
        compiler_params=params(),
        name="halve",
    )(me, current)


def spread_kernel(in_ref, out_ref):
    lane = lane_iota()
    for z in range(N_ZH):
        x = [in_ref[z, y] for y in range(N_Y)]
        for d in (4, 2, 1):
            upper = (lane & (16 * d)) != 0
            for a in range(N_Y):
                if a & d:
                    continue
                low, high = x[a], x[a + d]
                x[a] = jnp.where(upper, pltpu.roll(high, 16 * d, 1), low)
                x[a + d] = jnp.where(upper, high, pltpu.roll(low, LANES - 16 * d, 1))
        for y in range(N_Y):
            out_ref[z * N_Y + y] = x[y]


def spread(gathered):
    return pl.pallas_call(
        spread_kernel,
        out_shape=jax.ShapeDtypeStruct((N_ZH * N_Y, ORB, LANES), f32),
        in_specs=vmem(1),
        out_specs=vmem(1)[0],
        compiler_params=params(),
        name="spread",
    )(gathered)


def exchange(x, axes):
    return lax.all_to_all(x, axes, split_axis=0, concat_axis=0, tiled=True)


def gather(x, axes, n):
    return exchange(jnp.broadcast_to(x[None], (n,) + x.shape), axes)


def body(vectors, tiles, tile_pos, diag_blocks):
    zh = lax.axis_index("zh")
    r = lax.axis_index("x") * N_ZL + lax.axis_index("zl")
    me = jnp.stack([r, zh, lax.axis_index("core"), lax.axis_index("y")]).astype(jnp.int32)
    swap = [(0, 1), (1, 0)]

    packed = pack(tiles[0, 0], diag_blocks[0], tile_pos[0, 0])
    packed = exchange(packed, "y")

    mine, other, own = slice_vectors(me, vectors.reshape(-1, ORB, LANES))
    cols = pick_half(me, lax.all_gather(own, ("x", "zl", "core"), axis=0, tiled=False))
    current = join_cores(me, mine, lax.ppermute(other, "core", swap))

    packed, current, cols = lax.optimization_barrier((packed, current, cols))
    blocks_a, pos_a = unpack(packed)
    blocks_b, pos_b = unpack(lax.ppermute(packed, "core", swap))
    where, blocks = (me, pos_a, pos_b), (blocks_a, blocks_b)

    centre = 0.5 * (filter_high + filter_low)
    half_width = 0.5 * (filter_high - filter_low)
    at_own = (lax.broadcasted_iota(jnp.int32, (N_ZH, 1, 1), 0) == zh)
    previous = None
    for step in range(DEGREE):
        out_cols = product(mirror_kernel, "mirror", where, current, blocks, N_R)
        out_cols, cols = lax.optimization_barrier((out_cols, cols))
        got_cols = exchange(out_cols, ROW_AX)
        out_rows = product(direct_kernel, "direct", where, cols, blocks, N_ZH)
        partial = out_rows + jnp.where(at_own, jnp.sum(got_cols, 0)[None], 0.0)
        if step < DEGREE - 1:
            image = jnp.sum(gather(partial, "zh", N_ZH).reshape(N_ZH, N_ZH, ORB, LANES), 0)
        else:
            image = jnp.sum(exchange(partial, "zh"), 0)
            current = lax.dynamic_index_in_dim(current, zh, 0, keepdims=False)
            previous = lax.dynamic_index_in_dim(previous, zh, 0, keepdims=False)
        shifted = (image - centre * current) / half_width
        following = shifted if previous is None else 2.0 * shifted - previous
        previous, current = current, following
        if step < DEGREE - 1:
            cols = gather(lax.dynamic_index_in_dim(current, zh, 0, keepdims=False), ROW_AX, N_R)

    result = jnp.sum(exchange(halve(me, current), "core"), 0)
    result = gather(result, ("zh", "y"), N_ZH * N_Y).reshape(N_ZH, N_Y, ORB, LANES)
    return spread(result).reshape(vectors.shape)


def solution(mesh):
    fine = Mesh(
        mesh.devices.reshape(N_X, N_ZL, N_CORE, N_ZH, N_Y), ("x", "zl", "core", "zh", "y")
    )
    row, col = ("x", "zl", "core"), ("zh", "y")
    return jax.shard_map(
        body,
        mesh=fine,
        in_specs=(
            P(row, None),
            P(row, col, None, None, None),
            P(row, col, None, None),
            P(row + col, None, None),
        ),
        out_specs=P(row, None),
        check_vma=False,
    )
```

```python
import functools

import jax
import jax.numpy as jnp
from jax import lax
from jax.experimental import pallas as pl
from jax.experimental.pallas import tpu as pltpu
from jax.sharding import Mesh, PartitionSpec as P

ORB = 56
DEGREE = 3
LANES = 128
N_X, N_ZL, N_CORE, N_ZH, N_Y = 4, 2, 2, 4, 8
N_R = N_X * N_ZL
TILES = 10
SLOTS = TILES + 1
WIDE = 640
VS = 8
PLACE = SLOTS * ORB - (WIDE - LANES)
ROW_AX = ("x", "zl")
GROUPS = N_CORE * N_Y

filter_low = 0.0
filter_high = 8.0
centre = 0.5 * (filter_high + filter_low)
half_width = 0.5 * (filter_high - filter_low)

f32 = jnp.float32
bf16 = jnp.bfloat16


def params():
    return pltpu.CompilerParams(vmem_limit_bytes=40 * 1024 * 1024)


def vmem(n):
    return [pl.BlockSpec(memory_space=pltpu.VMEM)] * n


def lane_iota(rows=ORB):
    return lax.broadcasted_iota(jnp.int32, (rows, LANES), 1)


def roll_to(x, source, target):
    shift = (target - source) % LANES
    return x if shift == 0 else pltpu.roll(x, shift, 1)


def pack_kernel(tiles_hbm, diag_hbm, pos_hbm, out_hbm, tiles_ref, diag_ref, pos_ref, out_ref, sems, out_sems):
    copies = [
        pltpu.make_async_copy(src, dst, sems.at[k])
        for k, (src, dst) in enumerate(((tiles_hbm, tiles_ref), (diag_hbm, diag_ref), (pos_hbm, pos_ref)))
    ]
    for copy in copies:
        copy.start()
    for copy in copies:
        copy.wait()
    lane = lane_iota()
    pieces = [tiles_ref[t] for t in range(TILES)] + [diag_ref[...]]
    wide = [
        jnp.concatenate([p, jnp.zeros((ORB, LANES - ORB), f32)], axis=1) for p in pieces
    ]
    gap = jnp.zeros((1, LANES - 2 * TILES), f32)
    both = pos_ref[...].astype(f32)
    places = jnp.concatenate([both[0:1], both[1:2], gap], axis=1)
    places = jnp.broadcast_to(places, (ORB, LANES))
    for q in range(WIDE // LANES):
        total = jnp.zeros((ORB, LANES), f32)
        for t in range(SLOTS):
            start = t * ORB - q * LANES
            if start <= -ORB or start >= LANES:
                continue
            inside = (lane >= max(start, 0)) & (lane < min(start + ORB, LANES))
            total = jnp.where(inside, roll_to(wide[t], 0, start), total)
        if q == WIDE // LANES - 1:
            start = SLOTS * ORB - q * LANES
            total = jnp.where(lane >= start, roll_to(places, 0, start), total)
        out_ref[:, q * LANES : (q + 1) * LANES] = total
    copies = [pltpu.make_async_copy(out_ref, out_hbm.at[k], out_sems.at[k]) for k in range(N_Y)]
    for copy in copies:
        copy.start()
    for copy in copies:
        copy.wait()


def pack(tile_data, diag, places):
    return pl.pallas_call(
        pack_kernel,
        out_shape=jax.ShapeDtypeStruct((N_Y, ORB, WIDE), f32),
        in_specs=[pl.BlockSpec(memory_space=pl.ANY)] * 3,
        out_specs=pl.BlockSpec(memory_space=pl.ANY),
        scratch_shapes=[
            pltpu.VMEM((TILES, ORB, ORB), f32),
            pltpu.VMEM((ORB, ORB), f32),
            pltpu.VMEM((2, TILES), jnp.int32),
            pltpu.VMEM((ORB, WIDE), f32),
            pltpu.SemaphoreType.DMA((3,)),
            pltpu.SemaphoreType.DMA((N_Y,)),
        ],
        compiler_params=pltpu.CompilerParams(vmem_limit_bytes=56 * 1024 * 1024),
        name="pack",
    )(tile_data, diag, places)


def unpack_kernel(in_ref, blocks_ref, places_ref):
    x = in_ref[...].reshape(N_Y * ORB, WIDE)
    high = x.astype(bf16)
    low = (x - high.astype(f32)).astype(bf16)
    for t in range(SLOTS):
        start = t * ORB
        q, off = start // LANES, start % LANES
        width = LANES if off + ORB <= LANES else 2 * LANES
        source = lax.broadcasted_iota(jnp.int32, (width, LANES), 0)
        target = lax.broadcasted_iota(jnp.int32, (width, LANES), 1)
        window = slice(q * LANES, q * LANES + width)
        total = None
        for term, at in ((high, 0), (low, 64)):
            hit = (target >= at) & (target < at + ORB) & (source == target - at + off)
            part = jnp.dot(term[:, window], jnp.where(hit, 1.0, 0.0).astype(bf16), preferred_element_type=f32)
            total = part if total is None else total + part
        total = total.astype(bf16)
        for s in range(N_Y):
            blocks_ref[s * SLOTS + t] = total[s * ORB : (s + 1) * ORB]
    for s in range(N_Y):
        last = in_ref[s, 0:1, WIDE - LANES : WIDE]
        shown = lax.broadcasted_iota(jnp.int32, (1, LANES), 1) >= PLACE
        places_ref[s : s + 1] = jnp.where(shown, last, 0.0).astype(jnp.int32)


def unpack(packed):
    return pl.pallas_call(
        unpack_kernel,
        out_shape=(
            jax.ShapeDtypeStruct((N_Y * SLOTS, ORB, LANES), bf16),
            jax.ShapeDtypeStruct((N_Y, LANES), jnp.int32),
        ),
        in_specs=vmem(1),
        out_specs=tuple(vmem(2)),
        compiler_params=params(),
        name="unpack",
    )(packed)


def slice_kernel(me_ref, in_ref, mine_ref, other_ref, own_ref):
    lane = lane_iota()
    zh, core, start = me_ref[1], me_ref[2], me_ref[3] * (2 * VS)

    def placed(block, k, target):
        shift = lax.rem(target - k * VS + 2 * LANES - start, LANES)
        return pltpu.roll(in_ref[block], shift, 1)

    for out_ref, k in ((mine_ref, core), (other_ref, 1 - core)):
        for zp in range(N_ZH // 2):
            total = jnp.zeros((ORB, LANES), f32)
            for half in range(2):
                for y in range(N_Y):
                    target = half * 64 + y * VS
                    inside = (lane >= target) & (lane < target + VS)
                    total = jnp.where(inside, placed((2 * zp + half) * N_Y + y, k, target), total)
            out_ref[zp] = total
    total = jnp.zeros((ORB, LANES), f32)
    for k in range(N_CORE):
        for y in range(N_Y):
            target = k * 64 + y * VS
            inside = (lane >= target) & (lane < target + VS)
            total = jnp.where(inside, placed(zh * N_Y + y, k, target), total)
    own_ref[...] = total


def slice_vectors(me, blocks):
    pair = jax.ShapeDtypeStruct((N_ZH // 2, ORB, LANES), f32)
    return pl.pallas_call(
        slice_kernel,
        out_shape=(pair, pair, jax.ShapeDtypeStruct((ORB, LANES), f32)),
        in_specs=[pl.BlockSpec(memory_space=pltpu.SMEM)] + vmem(1),
        out_specs=tuple(vmem(3)),
        compiler_params=params(),
        name="slice_vectors",
    )(me, blocks)


def join_kernel(me_ref, mine_ref, other_ref, out_ref):
    lane = lane_iota()
    is_zero = me_ref[2] == 0
    for zp in range(N_ZH // 2):
        mine, other = mine_ref[zp], other_ref[zp]
        a = jnp.where(is_zero, mine, other)
        b = jnp.where(is_zero, other, mine)
        out_ref[2 * zp] = jnp.where(lane < 64, a, pltpu.roll(b, 64, 1))
        out_ref[2 * zp + 1] = jnp.where(lane < 64, pltpu.roll(a, 64, 1), b)


def join_cores(me, mine, other):
    return pl.pallas_call(
        join_kernel,
        out_shape=jax.ShapeDtypeStruct((N_ZH, ORB, LANES), f32),
        in_specs=[pl.BlockSpec(memory_space=pltpu.SMEM)] + vmem(2),
        out_specs=vmem(1)[0],
        compiler_params=params(),
        name="join_cores",
    )(me, mine, other)


def pick_kernel(me_ref, in_ref, out_ref):
    lane = lane_iota()
    is_zero = me_ref[2] == 0
    for r in range(N_R):
        a, b = in_ref[2 * r], in_ref[2 * r + 1]
        first = jnp.where(is_zero, a, pltpu.roll(a, 64, 1))
        second = jnp.where(is_zero, pltpu.roll(b, 64, 1), b)
        out_ref[r] = jnp.where(lane < 64, first, second)


def pick_half(me, gathered):
    return pl.pallas_call(
        pick_kernel,
        out_shape=jax.ShapeDtypeStruct((N_R, ORB, LANES), f32),
        in_specs=[pl.BlockSpec(memory_space=pltpu.SMEM)] + vmem(1),
        out_specs=vmem(1)[0],
        compiler_params=params(),
        name="pick_half",
    )(me, gathered)


def split_terms(src_ref, dst_ref):
    gap = jnp.zeros((64 - ORB, LANES), f32)
    for chunk in range(src_ref.shape[0]):
        x = src_ref[chunk]
        x = jnp.concatenate([x, gap, x, gap], axis=0).T
        high = x.astype(bf16).astype(f32)
        low = x - high
        for o in range(GROUPS):
            rows = slice(o * VS, (o + 1) * VS)
            both = jnp.concatenate([high[rows], low[rows]], axis=0)
            dst_ref[chunk * GROUPS + o] = both.astype(bf16)


def row_col(pos_ref, core_s, s, t):
    i, g = pos_ref[s, PLACE + t], pos_ref[s, PLACE + TILES + t]
    row = (i >> 3) * GROUPS + core_s * N_Y + (i & 7)
    col = (g >> 1) * GROUPS + (g & 1) * N_Y + s
    return row, col


def mirror_kernel(me_ref, pos_a_ref, pos_b_ref, rows_ref, blocks_a_ref, blocks_b_ref, out_ref, v_ref, acc_ref):
    split_terms(rows_ref, v_ref)
    acc_ref[...] = jnp.zeros_like(acc_ref)
    core = me_ref[2]
    for pos_ref, blocks_ref, core_s in ((pos_a_ref, blocks_a_ref, core), (pos_b_ref, blocks_b_ref, 1 - core)):

        def one_source(s, carry, pos_ref=pos_ref, blocks_ref=blocks_ref, core_s=core_s):
            for t in range(TILES):
                row, col = row_col(pos_ref, core_s, s, t)
                both = jnp.dot(v_ref[row][:, :ORB], blocks_ref[s * SLOTS + t], preferred_element_type=f32)
                acc_ref[col] += both[:VS] + both[VS:]
            return carry

        lax.fori_loop(0, N_Y, one_source, 0)
    for chunk in range(out_ref.shape[0]):
        x = acc_ref[chunk * GROUPS : (chunk + 1) * GROUPS].reshape(LANES, LANES)
        x = x + pltpu.roll(x, 64, 1)
        out_ref[chunk] = x.T[:ORB]


def direct_kernel(me_ref, pos_a_ref, pos_b_ref, cols_ref, blocks_a_ref, blocks_b_ref, out_ref, v_ref, acc_ref):
    split_terms(cols_ref, v_ref)
    acc_ref[...] = jnp.zeros_like(acc_ref)
    my_r, my_zh, core = me_ref[0], me_ref[1], me_ref[2]
    for pos_ref, blocks_ref, core_s in ((pos_a_ref, blocks_a_ref, core), (pos_b_ref, blocks_b_ref, 1 - core)):

        def one_source(s, carry, pos_ref=pos_ref, blocks_ref=blocks_ref, core_s=core_s):
            for t in range(SLOTS):
                if t < TILES:
                    row, col = row_col(pos_ref, core_s, s, t)
                else:
                    row = my_zh * GROUPS + core_s * N_Y + s
                    col = my_r * GROUPS + core_s * N_Y + s
                both = lax.dot_general(
                    v_ref[col], blocks_ref[s * SLOTS + t], (((1,), (1,)), ((), ())),
                    preferred_element_type=f32,
                )
                acc_ref[row, :, 0:ORB] += both[:VS] + both[VS:]
            return carry

        lax.fori_loop(0, N_Y, one_source, 0)
    for chunk in range(out_ref.shape[0]):
        x = acc_ref[chunk * GROUPS : (chunk + 1) * GROUPS].reshape(LANES, LANES)
        out_ref[chunk] = x.T[:ORB]


def product(kernel, name, scalars, field, blocks, chunks):
    smem = pl.BlockSpec(memory_space=pltpu.SMEM)
    return pl.pallas_call(
        kernel,
        out_shape=jax.ShapeDtypeStruct((chunks, ORB, LANES), f32),
        in_specs=[smem] * len(scalars) + vmem(1 + len(blocks)),
        out_specs=vmem(1)[0],
        scratch_shapes=[
            pltpu.VMEM((field.shape[0] * GROUPS, 2 * VS, LANES), bf16),
            pltpu.VMEM((chunks * GROUPS, VS, LANES), f32),
        ],
        compiler_params=params(),
        cost_estimate=pl.CostEstimate(flops=200000000, bytes_accessed=4000000, transcendentals=0),
        name=name,
    )(*scalars, field, *blocks)


def finish_kernel(me_ref, rows_ref, own_ref, current_ref, previous_ref, out_ref):
    lane = lane_iota()
    zh, core = me_ref[1], me_ref[2]
    mine = ((lane >> 3) & 1) == core
    scale = 2.0 / half_width
    own = scale * own_ref[...] - (scale * centre) * current_ref[zh] - previous_ref[zh]
    for z in range(N_ZH):
        total = scale * rows_ref[z] + jnp.where(zh == z, own, 0.0)
        for k in range(N_CORE):
            x = total if k == 0 else pltpu.roll(total, 64, 1)
            x = jnp.where(lane < 64, x, 0.0)
            for step in (32, 16, 8):
                block = lane & (4 * step - 1)
                moved = pltpu.roll(x, step, 1)
                x = jnp.where(block < step, x, jnp.where((block >= 2 * step) & (block < 3 * step), moved, 0.0))
            out_ref[k * N_ZH + z] = jnp.where(mine, pltpu.roll(x, core * VS, 1), 0.0)


def finish(me, rows, own, current, previous):
    return pl.pallas_call(
        finish_kernel,
        out_shape=jax.ShapeDtypeStruct((N_CORE * N_ZH, ORB, LANES), f32),
        in_specs=[pl.BlockSpec(memory_space=pltpu.SMEM)] + vmem(4),
        out_specs=vmem(1)[0],
        compiler_params=params(),
        name="finish",
    )(me, rows, own, current, previous)


def spread_kernel(in_ref, out_ref):
    lane = lane_iota()
    x = [in_ref[0, y] for y in range(N_Y)]
    for d in (4, 2, 1):
        upper = (lane & (16 * d)) != 0
        for a in range(N_Y):
            if a & d:
                continue
            low, high = x[a], x[a + d]
            x[a] = jnp.where(upper, pltpu.roll(high, 16 * d, 1), low)
            x[a + d] = jnp.where(upper, high, pltpu.roll(low, LANES - 16 * d, 1))
    for y in range(N_Y):
        out_ref[y] = x[y]


def spread(gathered):
    return pl.pallas_call(
        spread_kernel,
        out_shape=jax.ShapeDtypeStruct((N_ZH * N_Y, ORB, LANES), f32),
        grid=(N_ZH,),
        in_specs=[pl.BlockSpec((1, N_Y, ORB, LANES), lambda z: (z, 0, 0, 0))],
        out_specs=pl.BlockSpec((N_Y, ORB, LANES), lambda z: (z, 0, 0)),
        compiler_params=params(),
        name="spread",
    )(gathered)


def exchange(x, axes):
    return lax.all_to_all(x, axes, split_axis=0, concat_axis=0, tiled=True)


def gather(x, axes, n):
    return exchange(jnp.broadcast_to(x[None], (n,) + x.shape), axes)


def body(vectors, tiles, tile_pos, diag_blocks):
    zh = lax.axis_index("zh")
    r = lax.axis_index("x") * N_ZL + lax.axis_index("zl")
    me = jnp.stack([r, zh, lax.axis_index("core"), lax.axis_index("y")]).astype(jnp.int32)
    swap = [(0, 1), (1, 0)]

    packed = pack(tiles[0, 0], diag_blocks[0], tile_pos[0, 0])
    packed = exchange(packed, "y")

    mine, other, own = slice_vectors(me, vectors.reshape(-1, ORB, LANES))
    cols = pick_half(me, lax.all_gather(own, ("x", "zl", "core"), axis=0, tiled=False))
    current = join_cores(me, mine, lax.ppermute(other, "core", swap))

    packed, current, cols = lax.optimization_barrier((packed, current, cols))
    blocks_a, pos_a = unpack(packed)
    blocks_b, pos_b = unpack(lax.ppermute(packed, "core", swap))
    where, blocks = (me, pos_a, pos_b), (blocks_a, blocks_b)

    at_own = (lax.broadcasted_iota(jnp.int32, (N_ZH, 1, 1), 0) == zh)
    previous = None
    for step in range(DEGREE):
        out_cols = product(mirror_kernel, "mirror", where, current, blocks, N_R)
        out_cols, cols = lax.optimization_barrier((out_cols, cols))
        got_cols = exchange(out_cols, ROW_AX)
        out_rows = product(direct_kernel, "direct", where, cols, blocks, N_ZH)
        own = jnp.sum(got_cols, 0)
        if step == DEGREE - 1:
            break
        partial = out_rows + jnp.where(at_own, own[None], 0.0)
        image = jnp.sum(gather(partial, "zh", N_ZH).reshape(N_ZH, N_ZH, ORB, LANES), 0)
        shifted = (image - centre * current) / half_width
        following = shifted if previous is None else 2.0 * shifted - previous
        previous, current = current, following
        cols = gather(lax.dynamic_index_in_dim(current, zh, 0, keepdims=False), ROW_AX, N_R)

    result = jnp.sum(exchange(finish(me, out_rows, own, current, previous), ("core", "zh")), 0)
    result = gather(result, ("zh", "y"), N_ZH * N_Y).reshape(N_ZH, N_Y, ORB, LANES)
    return spread(result).reshape(vectors.shape)


def solution(mesh):
    fine = Mesh(
        mesh.devices.reshape(N_X, N_ZL, N_CORE, N_ZH, N_Y), ("x", "zl", "core", "zh", "y")
    )
    row, col = ("x", "zl", "core"), ("zh", "y")
    return jax.shard_map(
        body,
        mesh=fine,
        in_specs=(
            P(row, None),
            P(row, col, None, None, None),
            P(row, col, None, None),
            P(row + col, None, None),
        ),
        out_specs=P(row, None),
        check_vma=False,
    )
```

```python
import functools

import jax
import jax.numpy as jnp
from jax import lax
from jax.experimental import pallas as pl
from jax.experimental.pallas import tpu as pltpu
from jax.sharding import Mesh, PartitionSpec as P

ORB = 56
DEGREE = 3
LANES = 128
N_X, N_ZL, N_CORE, N_ZH, N_Y = 4, 2, 2, 4, 8
N_R = N_X * N_ZL
TILES = 10
SLOTS = TILES + 1
WIDE = 640
VS = 8
PLACE = SLOTS * ORB - (WIDE - LANES)
ROW_AX = ("x", "zl")
GROUPS = N_CORE * N_Y

filter_low = 0.0
filter_high = 8.0
centre = 0.5 * (filter_high + filter_low)
half_width = 0.5 * (filter_high - filter_low)

f32 = jnp.float32
bf16 = jnp.bfloat16


def params():
    return pltpu.CompilerParams(vmem_limit_bytes=40 * 1024 * 1024)


def vmem(n):
    return [pl.BlockSpec(memory_space=pltpu.VMEM)] * n


def lane_iota(rows=ORB):
    return lax.broadcasted_iota(jnp.int32, (rows, LANES), 1)


def roll_to(x, source, target):
    shift = (target - source) % LANES
    return x if shift == 0 else pltpu.roll(x, shift, 1)


def pack_kernel(tiles_hbm, diag_hbm, pos_hbm, out_hbm, tiles_ref, diag_ref, pos_ref, out_ref, sems, out_sems):
    copies = [
        pltpu.make_async_copy(src, dst, sems.at[k])
        for k, (src, dst) in enumerate(((tiles_hbm, tiles_ref), (diag_hbm, diag_ref), (pos_hbm, pos_ref)))
    ]
    for copy in copies:
        copy.start()
    for copy in copies:
        copy.wait()
    lane = lane_iota()
    pieces = [tiles_ref[t] for t in range(TILES)] + [diag_ref[...]]
    wide = [
        jnp.concatenate([p, jnp.zeros((ORB, LANES - ORB), f32)], axis=1) for p in pieces
    ]
    gap = jnp.zeros((1, LANES - 2 * TILES), f32)
    both = pos_ref[...].astype(f32)
    places = jnp.concatenate([both[0:1], both[1:2], gap], axis=1)
    places = jnp.broadcast_to(places, (ORB, LANES))
    for q in range(WIDE // LANES):
        total = jnp.zeros((ORB, LANES), f32)
        for t in range(SLOTS):
            start = t * ORB - q * LANES
            if start <= -ORB or start >= LANES:
                continue
            inside = (lane >= max(start, 0)) & (lane < min(start + ORB, LANES))
            total = jnp.where(inside, roll_to(wide[t], 0, start), total)
        if q == WIDE // LANES - 1:
            start = SLOTS * ORB - q * LANES
            total = jnp.where(lane >= start, roll_to(places, 0, start), total)
        out_ref[:, q * LANES : (q + 1) * LANES] = total
    copies = [pltpu.make_async_copy(out_ref, out_hbm.at[k], out_sems.at[k]) for k in range(N_Y)]
    for copy in copies:
        copy.start()
    for copy in copies:
        copy.wait()


def pack(tile_data, diag, places):
    return pl.pallas_call(
        pack_kernel,
        out_shape=jax.ShapeDtypeStruct((N_Y, ORB, WIDE), f32),
        in_specs=[pl.BlockSpec(memory_space=pl.ANY)] * 3,
        out_specs=pl.BlockSpec(memory_space=pl.ANY),
        scratch_shapes=[
            pltpu.VMEM((TILES, ORB, ORB), f32),
            pltpu.VMEM((ORB, ORB), f32),
            pltpu.VMEM((2, TILES), jnp.int32),
            pltpu.VMEM((ORB, WIDE), f32),
            pltpu.SemaphoreType.DMA((3,)),
            pltpu.SemaphoreType.DMA((N_Y,)),
        ],
        compiler_params=pltpu.CompilerParams(vmem_limit_bytes=56 * 1024 * 1024),
        name="pack",
    )(tile_data, diag, places)


def unpack_kernel(in_ref, blocks_ref, places_ref):
    x = in_ref[...].reshape(N_Y * ORB, WIDE)
    high = x.astype(bf16)
    low = (x - high.astype(f32)).astype(bf16)
    for t in range(SLOTS):
        start = t * ORB
        q, off = start // LANES, start % LANES
        width = LANES if off + ORB <= LANES else 2 * LANES
        source = lax.broadcasted_iota(jnp.int32, (width, LANES), 0)
        target = lax.broadcasted_iota(jnp.int32, (width, LANES), 1)
        window = slice(q * LANES, q * LANES + width)
        total = None
        for term, at in ((high, 0), (low, 64)):
            hit = (target >= at) & (target < at + ORB) & (source == target - at + off)
            part = jnp.dot(term[:, window], jnp.where(hit, 1.0, 0.0).astype(bf16), preferred_element_type=f32)
            total = part if total is None else total + part
        total = total.astype(bf16)
        for s in range(N_Y):
            blocks_ref[s * SLOTS + t] = total[s * ORB : (s + 1) * ORB]
    for s in range(N_Y):
        last = in_ref[s, 0:1, WIDE - LANES : WIDE]
        shown = lax.broadcasted_iota(jnp.int32, (1, LANES), 1) >= PLACE
        places_ref[s : s + 1] = jnp.where(shown, last, 0.0).astype(jnp.int32)


def unpack(packed):
    return pl.pallas_call(
        unpack_kernel,
        out_shape=(
            jax.ShapeDtypeStruct((N_Y * SLOTS, ORB, LANES), bf16),
            jax.ShapeDtypeStruct((N_Y, LANES), jnp.int32),
        ),
        in_specs=vmem(1),
        out_specs=tuple(vmem(2)),
        compiler_params=params(),
        name="unpack",
    )(packed)


def slice_kernel(me_ref, in_ref, mine_ref, other_ref, own_ref):
    lane = lane_iota()
    zh, core, start = me_ref[1], me_ref[2], me_ref[3] * (2 * VS)

    def placed(block, k, target):
        shift = lax.rem(target - k * VS + 2 * LANES - start, LANES)
        return pltpu.roll(in_ref[block], shift, 1)

    for out_ref, k in ((mine_ref, core), (other_ref, 1 - core)):
        for zp in range(N_ZH // 2):
            total = jnp.zeros((ORB, LANES), f32)
            for half in range(2):
                for y in range(N_Y):
                    target = half * 64 + y * VS
                    inside = (lane >= target) & (lane < target + VS)
                    total = jnp.where(inside, placed((2 * zp + half) * N_Y + y, k, target), total)
            out_ref[zp] = total
    total = jnp.zeros((ORB, LANES), f32)
    for k in range(N_CORE):
        for y in range(N_Y):
            target = k * 64 + y * VS
            inside = (lane >= target) & (lane < target + VS)
            total = jnp.where(inside, placed(zh * N_Y + y, k, target), total)
    own_ref[...] = total


def slice_vectors(me, blocks):
    pair = jax.ShapeDtypeStruct((N_ZH // 2, ORB, LANES), f32)
    return pl.pallas_call(
        slice_kernel,
        out_shape=(pair, pair, jax.ShapeDtypeStruct((ORB, LANES), f32)),
        in_specs=[pl.BlockSpec(memory_space=pltpu.SMEM)] + vmem(1),
        out_specs=tuple(vmem(3)),
        compiler_params=params(),
        name="slice_vectors",
    )(me, blocks)


def join_kernel(me_ref, mine_ref, other_ref, out_ref):
    lane = lane_iota()
    is_zero = me_ref[2] == 0
    for zp in range(N_ZH // 2):
        mine, other = mine_ref[zp], other_ref[zp]
        a = jnp.where(is_zero, mine, other)
        b = jnp.where(is_zero, other, mine)
        out_ref[2 * zp] = jnp.where(lane < 64, a, pltpu.roll(b, 64, 1))
        out_ref[2 * zp + 1] = jnp.where(lane < 64, pltpu.roll(a, 64, 1), b)


def join_cores(me, mine, other):
    return pl.pallas_call(
        join_kernel,
        out_shape=jax.ShapeDtypeStruct((N_ZH, ORB, LANES), f32),
        in_specs=[pl.BlockSpec(memory_space=pltpu.SMEM)] + vmem(2),
        out_specs=vmem(1)[0],
        compiler_params=params(),
        name="join_cores",
    )(me, mine, other)


def pick_kernel(me_ref, in_ref, out_ref):
    lane = lane_iota()
    is_zero = me_ref[2] == 0
    for r in range(N_R):
        a, b = in_ref[2 * r], in_ref[2 * r + 1]
        first = jnp.where(is_zero, a, pltpu.roll(a, 64, 1))
        second = jnp.where(is_zero, pltpu.roll(b, 64, 1), b)
        out_ref[r] = jnp.where(lane < 64, first, second)


def pick_half(me, gathered):
    return pl.pallas_call(
        pick_kernel,
        out_shape=jax.ShapeDtypeStruct((N_R, ORB, LANES), f32),
        in_specs=[pl.BlockSpec(memory_space=pltpu.SMEM)] + vmem(1),
        out_specs=vmem(1)[0],
        compiler_params=params(),
        name="pick_half",
    )(me, gathered)


def split_terms(src_ref, dst_ref):
    gap = jnp.zeros((64 - ORB, LANES), f32)
    for chunk in range(src_ref.shape[0]):
        x = src_ref[chunk]
        x = jnp.concatenate([x, gap, x, gap], axis=0).T
        high = x.astype(bf16).astype(f32)
        low = x - high
        for o in range(GROUPS):
            rows = slice(o * VS, (o + 1) * VS)
            both = jnp.concatenate([high[rows], low[rows]], axis=0)
            dst_ref[chunk * GROUPS + o] = both.astype(bf16)


def row_col(pos_ref, core_s, s, t):
    i, g = pos_ref[s, PLACE + t], pos_ref[s, PLACE + TILES + t]
    row = (i >> 3) * GROUPS + core_s * N_Y + (i & 7)
    col = (g >> 1) * GROUPS + (g & 1) * N_Y + s
    return row, col


def mirror_kernel(me_ref, pos_a_ref, pos_b_ref, rows_ref, blocks_a_ref, blocks_b_ref, out_ref, v_ref, acc_ref):
    split_terms(rows_ref, v_ref)
    acc_ref[...] = jnp.zeros_like(acc_ref)
    core = me_ref[2]
    for pos_ref, blocks_ref, core_s in ((pos_a_ref, blocks_a_ref, core), (pos_b_ref, blocks_b_ref, 1 - core)):

        def one_source(s, carry, pos_ref=pos_ref, blocks_ref=blocks_ref, core_s=core_s):
            for t in range(TILES):
                row, col = row_col(pos_ref, core_s, s, t)
                both = jnp.dot(v_ref[row][:, :ORB], blocks_ref[s * SLOTS + t], preferred_element_type=f32)
                acc_ref[col] += both[:VS] + both[VS:]
            return carry

        lax.fori_loop(0, N_Y, one_source, 0)
    for chunk in range(out_ref.shape[0]):
        x = acc_ref[chunk * GROUPS : (chunk + 1) * GROUPS].reshape(LANES, LANES)
        x = x + pltpu.roll(x, 64, 1)
        out_ref[chunk] = x.T[:ORB]


def direct_kernel(me_ref, pos_a_ref, pos_b_ref, cols_ref, blocks_a_ref, blocks_b_ref, out_ref, v_ref, acc_ref):
    split_terms(cols_ref, v_ref)
    acc_ref[...] = jnp.zeros_like(acc_ref)
    my_r, my_zh, core = me_ref[0], me_ref[1], me_ref[2]
    for pos_ref, blocks_ref, core_s in ((pos_a_ref, blocks_a_ref, core), (pos_b_ref, blocks_b_ref, 1 - core)):

        def one_source(s, carry, pos_ref=pos_ref, blocks_ref=blocks_ref, core_s=core_s):
            for t in range(SLOTS):
                if t < TILES:
                    row, col = row_col(pos_ref, core_s, s, t)
                else:
                    row = my_zh * GROUPS + core_s * N_Y + s
                    col = my_r * GROUPS + core_s * N_Y + s
                both = lax.dot_general(
                    v_ref[col], blocks_ref[s * SLOTS + t], (((1,), (1,)), ((), ())),
                    preferred_element_type=f32,
                )
                acc_ref[row, :, 0:ORB] += both[:VS] + both[VS:]
            return carry

        lax.fori_loop(0, N_Y, one_source, 0)
    for chunk in range(out_ref.shape[0]):
        x = acc_ref[chunk * GROUPS : (chunk + 1) * GROUPS].reshape(LANES, LANES)
        out_ref[chunk] = x.T[:ORB]


def product(kernel, name, scalars, field, blocks, chunks):
    smem = pl.BlockSpec(memory_space=pltpu.SMEM)
    return pl.pallas_call(
        kernel,
        out_shape=jax.ShapeDtypeStruct((chunks, ORB, LANES), f32),
        in_specs=[smem] * len(scalars) + vmem(1 + len(blocks)),
        out_specs=vmem(1)[0],
        scratch_shapes=[
            pltpu.VMEM((field.shape[0] * GROUPS, 2 * VS, LANES), bf16),
            pltpu.VMEM((chunks * GROUPS, VS, LANES), f32),
        ],
        compiler_params=params(),
        cost_estimate=pl.CostEstimate(flops=200000000, bytes_accessed=4000000, transcendentals=0),
        name=name,
    )(*scalars, field, *blocks)


def finish_kernel(me_ref, rows_ref, own_ref, current_ref, previous_ref, out_ref):
    lane = lane_iota()
    zh, core = me_ref[1], me_ref[2]
    mine = ((lane >> 3) & 1) == core
    scale = 2.0 / half_width
    own = scale * own_ref[...] - (scale * centre) * current_ref[zh] - previous_ref[zh]
    for z in range(N_ZH):
        total = scale * rows_ref[z] + jnp.where(zh == z, own, 0.0)
        for k in range(N_CORE):
            x = total if k == 0 else pltpu.roll(total, 64, 1)
            x = jnp.where(lane < 64, x, 0.0)
            for step in (32, 16, 8):
                block = lane & (4 * step - 1)
                moved = pltpu.roll(x, step, 1)
                x = jnp.where(block < step, x, jnp.where((block >= 2 * step) & (block < 3 * step), moved, 0.0))
            out_ref[k * N_ZH + z] = jnp.where(mine, pltpu.roll(x, core * VS, 1), 0.0)


def finish(me, rows, own, current, previous):
    return pl.pallas_call(
        finish_kernel,
        out_shape=jax.ShapeDtypeStruct((N_CORE * N_ZH, ORB, LANES), f32),
        in_specs=[pl.BlockSpec(memory_space=pltpu.SMEM)] + vmem(4),
        out_specs=vmem(1)[0],
        compiler_params=params(),
        name="finish",
    )(me, rows, own, current, previous)


def spread_kernel(in_ref, out_hbm, held, sems):
    lane = lane_iota()
    copies = []
    for z in range(N_ZH):
        x = [in_ref[z, y] for y in range(N_Y)]
        for d in (4, 2, 1):
            upper = (lane & (16 * d)) != 0
            for a in range(N_Y):
                if a & d:
                    continue
                low, high = x[a], x[a + d]
                x[a] = jnp.where(upper, pltpu.roll(high, 16 * d, 1), low)
                x[a + d] = jnp.where(upper, high, pltpu.roll(low, LANES - 16 * d, 1))
        for y in range(N_Y):
            held[z, y] = x[y]
        copy = pltpu.make_async_copy(held.at[z], out_hbm.at[pl.ds(z * N_Y, N_Y)], sems.at[z])
        copy.start()
        copies.append(copy)
    for copy in copies:
        copy.wait()


def spread(gathered):
    return pl.pallas_call(
        spread_kernel,
        out_shape=jax.ShapeDtypeStruct((N_ZH * N_Y, ORB, LANES), f32),
        in_specs=vmem(1),
        out_specs=pl.BlockSpec(memory_space=pl.ANY),
        scratch_shapes=[
            pltpu.VMEM((N_ZH, N_Y, ORB, LANES), f32),
            pltpu.SemaphoreType.DMA((N_ZH,)),
        ],
        compiler_params=params(),
        name="spread",
    )(gathered)


def merge_kernel(me_ref, rows_ref, cols_ref, out_ref):
    own = cols_ref[0]
    for r in range(1, N_R):
        own = own + cols_ref[r]
    for z in range(N_ZH):
        total = rows_ref[z] + jnp.where(me_ref[1] == z, own, 0.0)
        for copy in range(N_ZH):
            out_ref[copy, z] = total


def merge(me, rows, cols):
    return pl.pallas_call(
        merge_kernel,
        out_shape=jax.ShapeDtypeStruct((N_ZH, N_ZH, ORB, LANES), f32),
        in_specs=[pl.BlockSpec(memory_space=pltpu.SMEM)] + vmem(2),
        out_specs=vmem(1)[0],
        compiler_params=params(),
        name="merge",
    )(me, rows, cols)


def exchange(x, axes):
    return lax.all_to_all(x, axes, split_axis=0, concat_axis=0, tiled=True)


def gather(x, axes, n):
    return exchange(jnp.broadcast_to(x[None], (n,) + x.shape), axes)


def body(vectors, tiles, tile_pos, diag_blocks):
    zh = lax.axis_index("zh")
    r = lax.axis_index("x") * N_ZL + lax.axis_index("zl")
    me = jnp.stack([r, zh, lax.axis_index("core"), lax.axis_index("y")]).astype(jnp.int32)
    swap = [(0, 1), (1, 0)]

    packed = pack(tiles[0, 0], diag_blocks[0], tile_pos[0, 0])
    packed = exchange(packed, "y")

    mine, other, own = slice_vectors(me, vectors.reshape(-1, ORB, LANES))
    cols = pick_half(me, lax.all_gather(own, ("x", "zl", "core"), axis=0, tiled=False))
    current = join_cores(me, mine, lax.ppermute(other, "core", swap))

    packed, current, cols = lax.optimization_barrier((packed, current, cols))
    blocks_a, pos_a = unpack(packed)
    blocks_b, pos_b = unpack(lax.ppermute(packed, "core", swap))
    where, blocks = (me, pos_a, pos_b), (blocks_a, blocks_b)

    previous = None
    for step in range(DEGREE):
        out_cols = product(mirror_kernel, "mirror", where, current, blocks, N_R)
        out_cols, cols = lax.optimization_barrier((out_cols, cols))
        got_cols = exchange(out_cols, ROW_AX)
        out_rows = product(direct_kernel, "direct", where, cols, blocks, N_ZH)
        if step == DEGREE - 1:
            break
        image = jnp.sum(exchange(merge(me, out_rows, got_cols), "zh"), 0)
        shifted = (image - centre * current) / half_width
        following = shifted if previous is None else 2.0 * shifted - previous
        previous, current = current, following
        cols = gather(lax.dynamic_index_in_dim(current, zh, 0, keepdims=False), ROW_AX, N_R)

    result = jnp.sum(exchange(finish(me, out_rows, jnp.sum(got_cols, 0), current, previous), ("core", "zh")), 0)
    result = gather(result, ("zh", "y"), N_ZH * N_Y).reshape(N_ZH, N_Y, ORB, LANES)
    return spread(result).reshape(vectors.shape)


def solution(mesh):
    fine = Mesh(
        mesh.devices.reshape(N_X, N_ZL, N_CORE, N_ZH, N_Y), ("x", "zl", "core", "zh", "y")
    )
    row, col = ("x", "zl", "core"), ("zh", "y")
    return jax.shard_map(
        body,
        mesh=fine,
        in_specs=(
            P(row, None),
            P(row, col, None, None, None),
            P(row, col, None, None),
            P(row + col, None, None),
        ),
        out_specs=P(row, None),
        check_vma=False,
    )
```

```python
import functools

import jax
import jax.numpy as jnp
from jax import lax
from jax.experimental import pallas as pl
from jax.experimental.pallas import tpu as pltpu
from jax.sharding import Mesh, PartitionSpec as P

ORB = 56
DEGREE = 3
LANES = 128
N_X, N_ZL, N_CORE, N_ZH, N_Y = 4, 2, 2, 4, 8
N_R = N_X * N_ZL
TILES = 10
SLOTS = TILES + 1
WIDE = 640
VS = 8
PLACE = SLOTS * ORB - (WIDE - LANES)
ROW_AX = ("x", "zl")
GROUPS = N_CORE * N_Y

filter_low = 0.0
filter_high = 8.0
centre = 0.5 * (filter_high + filter_low)
half_width = 0.5 * (filter_high - filter_low)

f32 = jnp.float32
bf16 = jnp.bfloat16


def params():
    return pltpu.CompilerParams(vmem_limit_bytes=40 * 1024 * 1024)


def vmem(n):
    return [pl.BlockSpec(memory_space=pltpu.VMEM)] * n


def lane_iota(rows=ORB):
    return lax.broadcasted_iota(jnp.int32, (rows, LANES), 1)


def roll_to(x, source, target):
    shift = (target - source) % LANES
    return x if shift == 0 else pltpu.roll(x, shift, 1)


def pack_kernel(tiles_hbm, diag_hbm, pos_hbm, out_hbm, tiles_ref, diag_ref, pos_ref, out_ref, sems, out_sems):
    copies = [
        pltpu.make_async_copy(src, dst, sems.at[k])
        for k, (src, dst) in enumerate(((tiles_hbm, tiles_ref), (diag_hbm, diag_ref), (pos_hbm, pos_ref)))
    ]
    for copy in copies:
        copy.start()
    for copy in copies:
        copy.wait()
    lane = lane_iota()
    pieces = [tiles_ref[t] for t in range(TILES)] + [diag_ref[...]]
    wide = [
        jnp.concatenate([p, jnp.zeros((ORB, LANES - ORB), f32)], axis=1) for p in pieces
    ]
    gap = jnp.zeros((1, LANES - 2 * TILES), f32)
    both = pos_ref[...].astype(f32)
    places = jnp.concatenate([both[0:1], both[1:2], gap], axis=1)
    places = jnp.broadcast_to(places, (ORB, LANES))
    for q in range(WIDE // LANES):
        total = jnp.zeros((ORB, LANES), f32)
        for t in range(SLOTS):
            start = t * ORB - q * LANES
            if start <= -ORB or start >= LANES:
                continue
            inside = (lane >= max(start, 0)) & (lane < min(start + ORB, LANES))
            total = jnp.where(inside, roll_to(wide[t], 0, start), total)
        if q == WIDE // LANES - 1:
            start = SLOTS * ORB - q * LANES
            total = jnp.where(lane >= start, roll_to(places, 0, start), total)
        out_ref[:, q * LANES : (q + 1) * LANES] = total
    copies = [pltpu.make_async_copy(out_ref, out_hbm.at[k], out_sems.at[k]) for k in range(N_Y)]
    for copy in copies:
        copy.start()
    for copy in copies:
        copy.wait()


def pack(tile_data, diag, places):
    return pl.pallas_call(
        pack_kernel,
        out_shape=jax.ShapeDtypeStruct((N_Y, ORB, WIDE), f32),
        in_specs=[pl.BlockSpec(memory_space=pl.ANY)] * 3,
        out_specs=pl.BlockSpec(memory_space=pl.ANY),
        scratch_shapes=[
            pltpu.VMEM((TILES, ORB, ORB), f32),
            pltpu.VMEM((ORB, ORB), f32),
            pltpu.VMEM((2, TILES), jnp.int32),
            pltpu.VMEM((ORB, WIDE), f32),
            pltpu.SemaphoreType.DMA((3,)),
            pltpu.SemaphoreType.DMA((N_Y,)),
        ],
        compiler_params=pltpu.CompilerParams(vmem_limit_bytes=56 * 1024 * 1024),
        name="pack",
    )(tile_data, diag, places)


def unpack_kernel(in_ref, blocks_ref, places_ref):
    x = in_ref[...].reshape(N_Y * ORB, WIDE)
    high = x.astype(bf16)
    low = (x - high.astype(f32)).astype(bf16)
    for t in range(SLOTS):
        start = t * ORB
        q, off = start // LANES, start % LANES
        width = LANES if off + ORB <= LANES else 2 * LANES
        source = lax.broadcasted_iota(jnp.int32, (width, LANES), 0)
        target = lax.broadcasted_iota(jnp.int32, (width, LANES), 1)
        window = slice(q * LANES, q * LANES + width)
        total = None
        for term, at in ((high, 0), (low, 64)):
            hit = (target >= at) & (target < at + ORB) & (source == target - at + off)
            part = jnp.dot(term[:, window], jnp.where(hit, 1.0, 0.0).astype(bf16), preferred_element_type=f32)
            total = part if total is None else total + part
        total = total.astype(bf16)
        for s in range(N_Y):
            blocks_ref[s * SLOTS + t] = total[s * ORB : (s + 1) * ORB]
    for s in range(N_Y):
        last = in_ref[s, 0:1, WIDE - LANES : WIDE]
        shown = lax.broadcasted_iota(jnp.int32, (1, LANES), 1) >= PLACE
        places_ref[s : s + 1] = jnp.where(shown, last, 0.0).astype(jnp.int32)


def unpack(packed):
    return pl.pallas_call(
        unpack_kernel,
        out_shape=(
            jax.ShapeDtypeStruct((N_Y * SLOTS, ORB, LANES), bf16),
            jax.ShapeDtypeStruct((N_Y, LANES), jnp.int32),
        ),
        in_specs=vmem(1),
        out_specs=tuple(vmem(2)),
        compiler_params=params(),
        name="unpack",
    )(packed)


def slice_kernel(me_ref, in_ref, mine_ref, other_ref, own_ref):
    lane = lane_iota()
    zh, core, start = me_ref[1], me_ref[2], me_ref[3] * (2 * VS)

    def placed(block, k, target):
        shift = lax.rem(target - k * VS + 2 * LANES - start, LANES)
        return pltpu.roll(in_ref[block], shift, 1)

    for out_ref, k in ((mine_ref, core), (other_ref, 1 - core)):
        for zp in range(N_ZH // 2):
            total = jnp.zeros((ORB, LANES), f32)
            for half in range(2):
                for y in range(N_Y):
                    target = half * 64 + y * VS
                    inside = (lane >= target) & (lane < target + VS)
                    total = jnp.where(inside, placed((2 * zp + half) * N_Y + y, k, target), total)
            out_ref[zp] = total
    total = jnp.zeros((ORB, LANES), f32)
    for k in range(N_CORE):
        for y in range(N_Y):
            target = k * 64 + y * VS
            inside = (lane >= target) & (lane < target + VS)
            total = jnp.where(inside, placed(zh * N_Y + y, k, target), total)
    own_ref[...] = total


def slice_vectors(me, blocks):
    pair = jax.ShapeDtypeStruct((N_ZH // 2, ORB, LANES), f32)
    return pl.pallas_call(
        slice_kernel,
        out_shape=(pair, pair, jax.ShapeDtypeStruct((ORB, LANES), f32)),
        in_specs=[pl.BlockSpec(memory_space=pltpu.SMEM)] + vmem(1),
        out_specs=tuple(vmem(3)),
        compiler_params=params(),
        name="slice_vectors",
    )(me, blocks)


def join_kernel(me_ref, mine_ref, other_ref, out_ref):
    lane = lane_iota()
    is_zero = me_ref[2] == 0
    for zp in range(N_ZH // 2):
        mine, other = mine_ref[zp], other_ref[zp]
        a = jnp.where(is_zero, mine, other)
        b = jnp.where(is_zero, other, mine)
        out_ref[2 * zp] = jnp.where(lane < 64, a, pltpu.roll(b, 64, 1))
        out_ref[2 * zp + 1] = jnp.where(lane < 64, pltpu.roll(a, 64, 1), b)


def join_cores(me, mine, other):
    return pl.pallas_call(
        join_kernel,
        out_shape=jax.ShapeDtypeStruct((N_ZH, ORB, LANES), f32),
        in_specs=[pl.BlockSpec(memory_space=pltpu.SMEM)] + vmem(2),
        out_specs=vmem(1)[0],
        compiler_params=params(),
        name="join_cores",
    )(me, mine, other)


def pick_kernel(me_ref, in_ref, out_ref):
    lane = lane_iota()
    is_zero = me_ref[2] == 0
    for r in range(N_R):
        a, b = in_ref[2 * r], in_ref[2 * r + 1]
        first = jnp.where(is_zero, a, pltpu.roll(a, 64, 1))
        second = jnp.where(is_zero, pltpu.roll(b, 64, 1), b)
        out_ref[r] = jnp.where(lane < 64, first, second)


def pick_half(me, gathered):
    return pl.pallas_call(
        pick_kernel,
        out_shape=jax.ShapeDtypeStruct((N_R, ORB, LANES), f32),
        in_specs=[pl.BlockSpec(memory_space=pltpu.SMEM)] + vmem(1),
        out_specs=vmem(1)[0],
        compiler_params=params(),
        name="pick_half",
    )(me, gathered)


def split_terms(src_ref, dst_ref):
    gap = jnp.zeros((64 - ORB, LANES), f32)
    for chunk in range(src_ref.shape[0]):
        x = src_ref[chunk]
        x = jnp.concatenate([x, gap, x, gap], axis=0).T
        high = x.astype(bf16).astype(f32)
        low = x - high
        for o in range(GROUPS):
            rows = slice(o * VS, (o + 1) * VS)
            both = jnp.concatenate([high[rows], low[rows]], axis=0)
            dst_ref[chunk * GROUPS + o] = both.astype(bf16)


def row_col(pos_ref, core_s, s, t):
    i, g = pos_ref[s, PLACE + t], pos_ref[s, PLACE + TILES + t]
    row = (i >> 3) * GROUPS + core_s * N_Y + (i & 7)
    col = (g >> 1) * GROUPS + (g & 1) * N_Y + s
    return row, col


def mirror_kernel(me_ref, pos_a_ref, pos_b_ref, rows_ref, blocks_a_ref, blocks_b_ref, out_ref, v_ref, acc_ref):
    split_terms(rows_ref, v_ref)
    acc_ref[...] = jnp.zeros_like(acc_ref)
    core = me_ref[2]
    parts = ((pos_a_ref, blocks_a_ref, core), (pos_b_ref, blocks_b_ref, 1 - core))

    def one_source(s, carry):
        for t in range(TILES):
            for pos_ref, blocks_ref, core_s in parts:
                row, col = row_col(pos_ref, core_s, s, t)
                both = jnp.dot(v_ref[row][:, :ORB], blocks_ref[s * SLOTS + t], preferred_element_type=f32)
                acc_ref[col] += both[:VS] + both[VS:]
        return carry

    lax.fori_loop(0, N_Y, one_source, 0)
    for chunk in range(out_ref.shape[0]):
        x = acc_ref[chunk * GROUPS : (chunk + 1) * GROUPS].reshape(LANES, LANES)
        x = x + pltpu.roll(x, 64, 1)
        out_ref[chunk] = x.T[:ORB]


def direct_kernel(me_ref, pos_a_ref, pos_b_ref, cols_ref, blocks_a_ref, blocks_b_ref, out_ref, v_ref, acc_ref):
    split_terms(cols_ref, v_ref)
    acc_ref[...] = jnp.zeros_like(acc_ref)
    my_r, my_zh, core = me_ref[0], me_ref[1], me_ref[2]
    parts = ((pos_a_ref, blocks_a_ref, core), (pos_b_ref, blocks_b_ref, 1 - core))

    def one_source(s, carry):
        for t in range(SLOTS):
            for pos_ref, blocks_ref, core_s in parts:
                if t < TILES:
                    row, col = row_col(pos_ref, core_s, s, t)
                else:
                    row = my_zh * GROUPS + core_s * N_Y + s
                    col = my_r * GROUPS + core_s * N_Y + s
                both = lax.dot_general(
                    v_ref[col], blocks_ref[s * SLOTS + t], (((1,), (1,)), ((), ())),
                    preferred_element_type=f32,
                )
                acc_ref[row, :, 0:ORB] += both[:VS] + both[VS:]
        return carry

    lax.fori_loop(0, N_Y, one_source, 0)
    for chunk in range(out_ref.shape[0]):
        x = acc_ref[chunk * GROUPS : (chunk + 1) * GROUPS].reshape(LANES, LANES)
        out_ref[chunk] = x.T[:ORB]


def product(kernel, name, scalars, field, blocks, chunks):
    smem = pl.BlockSpec(memory_space=pltpu.SMEM)
    return pl.pallas_call(
        kernel,
        out_shape=jax.ShapeDtypeStruct((chunks, ORB, LANES), f32),
        in_specs=[smem] * len(scalars) + vmem(1 + len(blocks)),
        out_specs=vmem(1)[0],
        scratch_shapes=[
            pltpu.VMEM((field.shape[0] * GROUPS, 2 * VS, LANES), bf16),
            pltpu.VMEM((chunks * GROUPS, VS, LANES), f32),
        ],
        compiler_params=params(),
        cost_estimate=pl.CostEstimate(flops=200000000, bytes_accessed=4000000, transcendentals=0),
        name=name,
    )(*scalars, field, *blocks)


def finish_kernel(me_ref, rows_ref, own_ref, current_ref, previous_ref, out_ref):
    lane = lane_iota()
    zh, core = me_ref[1], me_ref[2]
    mine = ((lane >> 3) & 1) == core
    scale = 2.0 / half_width
    own = scale * own_ref[...] - (scale * centre) * current_ref[zh] - previous_ref[zh]
    for z in range(N_ZH):
        total = scale * rows_ref[z] + jnp.where(zh == z, own, 0.0)
        for k in range(N_CORE):
            x = total if k == 0 else pltpu.roll(total, 64, 1)
            x = jnp.where(lane < 64, x, 0.0)
            for step in (32, 16, 8):
                block = lane & (4 * step - 1)
                moved = pltpu.roll(x, step, 1)
                x = jnp.where(block < step, x, jnp.where((block >= 2 * step) & (block < 3 * step), moved, 0.0))
            out_ref[k * N_ZH + z] = jnp.where(mine, pltpu.roll(x, core * VS, 1), 0.0)


def finish(me, rows, own, current, previous):
    return pl.pallas_call(
        finish_kernel,
        out_shape=jax.ShapeDtypeStruct((N_CORE * N_ZH, ORB, LANES), f32),
        in_specs=[pl.BlockSpec(memory_space=pltpu.SMEM)] + vmem(4),
        out_specs=vmem(1)[0],
        compiler_params=params(),
        name="finish",
    )(me, rows, own, current, previous)


def spread_kernel(in_ref, out_hbm, held, sems):
    lane = lane_iota()
    copies = []
    for z in range(N_ZH):
        x = [in_ref[z, y] for y in range(N_Y)]
        for d in (4, 2, 1):
            upper = (lane & (16 * d)) != 0
            for a in range(N_Y):
                if a & d:
                    continue
                low, high = x[a], x[a + d]
                x[a] = jnp.where(upper, pltpu.roll(high, 16 * d, 1), low)
                x[a + d] = jnp.where(upper, high, pltpu.roll(low, LANES - 16 * d, 1))
        for y in range(N_Y):
            held[z, y] = x[y]
        copy = pltpu.make_async_copy(held.at[z], out_hbm.at[pl.ds(z * N_Y, N_Y)], sems.at[z])
        copy.start()
        copies.append(copy)
    for copy in copies:
        copy.wait()


def spread(gathered):
    return pl.pallas_call(
        spread_kernel,
        out_shape=jax.ShapeDtypeStruct((N_ZH * N_Y, ORB, LANES), f32),
        in_specs=vmem(1),
        out_specs=pl.BlockSpec(memory_space=pl.ANY),
        scratch_shapes=[
            pltpu.VMEM((N_ZH, N_Y, ORB, LANES), f32),
            pltpu.SemaphoreType.DMA((N_ZH,)),
        ],
        compiler_params=params(),
        name="spread",
    )(gathered)


def merge_kernel(me_ref, rows_ref, cols_ref, out_ref):
    own = cols_ref[0]
    for r in range(1, N_R):
        own = own + cols_ref[r]
    for z in range(N_ZH):
        total = rows_ref[z] + jnp.where(me_ref[1] == z, own, 0.0)
        for copy in range(N_ZH):
            out_ref[copy, z] = total


def merge(me, rows, cols):
    return pl.pallas_call(
        merge_kernel,
        out_shape=jax.ShapeDtypeStruct((N_ZH, N_ZH, ORB, LANES), f32),
        in_specs=[pl.BlockSpec(memory_space=pltpu.SMEM)] + vmem(2),
        out_specs=vmem(1)[0],
        compiler_params=params(),
        name="merge",
    )(me, rows, cols)


def advance_kernel(me_ref, got_ref, *refs):
    *fields, out_ref, own_ref = refs
    for z in range(N_ZH):
        image = got_ref[0, z]
        for source in range(1, N_ZH):
            image = image + got_ref[source, z]
        shifted = (image - centre * fields[0][z]) / half_width
        out_ref[z] = shifted if len(fields) == 1 else 2.0 * shifted - fields[1][z]
    own_ref[...] = out_ref[me_ref[1]]


def advance(me, got, fields):
    return pl.pallas_call(
        advance_kernel,
        out_shape=(
            jax.ShapeDtypeStruct((N_ZH, ORB, LANES), f32),
            jax.ShapeDtypeStruct((ORB, LANES), f32),
        ),
        in_specs=[pl.BlockSpec(memory_space=pltpu.SMEM)] + vmem(1 + len(fields)),
        out_specs=tuple(vmem(2)),
        compiler_params=params(),
        name="advance",
    )(me, got, *fields)


def exchange(x, axes):
    return lax.all_to_all(x, axes, split_axis=0, concat_axis=0, tiled=True)


def gather(x, axes, n):
    return exchange(jnp.broadcast_to(x[None], (n,) + x.shape), axes)


def body(vectors, tiles, tile_pos, diag_blocks):
    zh = lax.axis_index("zh")
    r = lax.axis_index("x") * N_ZL + lax.axis_index("zl")
    me = jnp.stack([r, zh, lax.axis_index("core"), lax.axis_index("y")]).astype(jnp.int32)
    swap = [(0, 1), (1, 0)]

    packed = pack(tiles[0, 0], diag_blocks[0], tile_pos[0, 0])
    packed = exchange(packed, "y")

    mine, other, own = slice_vectors(me, vectors.reshape(-1, ORB, LANES))
    cols = pick_half(me, lax.all_gather(own, ("x", "zl", "core"), axis=0, tiled=False))
    current = join_cores(me, mine, lax.ppermute(other, "core", swap))

    packed, current, cols = lax.optimization_barrier((packed, current, cols))
    blocks_a, pos_a = unpack(packed)
    blocks_b, pos_b = unpack(lax.ppermute(packed, "core", swap))
    where, blocks = (me, pos_a, pos_b), (blocks_a, blocks_b)

    previous = None
    for step in range(DEGREE):
        out_cols = product(mirror_kernel, "mirror", where, current, blocks, N_R)
        out_cols, cols = lax.optimization_barrier((out_cols, cols))
        got_cols = exchange(out_cols, ROW_AX)
        out_rows = product(direct_kernel, "direct", where, cols, blocks, N_ZH)
        if step == DEGREE - 1:
            break
        got = exchange(merge(me, out_rows, got_cols), "zh")
        following, own = advance(me, got, (current,) if previous is None else (current, previous))
        previous, current = current, following
        cols = gather(own, ROW_AX, N_R)

    result = jnp.sum(exchange(finish(me, out_rows, jnp.sum(got_cols, 0), current, previous), ("core", "zh")), 0)
    result = gather(result, ("zh", "y"), N_ZH * N_Y).reshape(N_ZH, N_Y, ORB, LANES)
    return spread(result).reshape(vectors.shape)


def solution(mesh):
    fine = Mesh(
        mesh.devices.reshape(N_X, N_ZL, N_CORE, N_ZH, N_Y), ("x", "zl", "core", "zh", "y")
    )
    row, col = ("x", "zl", "core"), ("zh", "y")
    return jax.shard_map(
        body,
        mesh=fine,
        in_specs=(
            P(row, None),
            P(row, col, None, None, None),
            P(row, col, None, None),
            P(row + col, None, None),
        ),
        out_specs=P(row, None),
        check_vma=False,
    )
```

```python
import functools

import jax
import jax.numpy as jnp
from jax import lax
from jax.experimental import pallas as pl
from jax.experimental.pallas import tpu as pltpu
from jax.sharding import Mesh, PartitionSpec as P

ORB = 56
DEGREE = 3
LANES = 128
N_X, N_ZL, N_CORE, N_ZH, N_Y = 4, 2, 2, 4, 8
N_R = N_X * N_ZL
TILES = 10
SLOTS = TILES + 1
WIDE = 640
VS = 8
PLACE = SLOTS * ORB - (WIDE - LANES)
ROW_AX = ("x", "zl")
GROUPS = N_CORE * N_Y

filter_low = 0.0
filter_high = 8.0
centre = 0.5 * (filter_high + filter_low)
half_width = 0.5 * (filter_high - filter_low)

f32 = jnp.float32
bf16 = jnp.bfloat16


def params():
    return pltpu.CompilerParams(vmem_limit_bytes=40 * 1024 * 1024)


def vmem(n):
    return [pl.BlockSpec(memory_space=pltpu.VMEM)] * n


def lane_iota(rows=ORB):
    return lax.broadcasted_iota(jnp.int32, (rows, LANES), 1)


def roll_to(x, source, target):
    shift = (target - source) % LANES
    return x if shift == 0 else pltpu.roll(x, shift, 1)


def pack_kernel(tiles_hbm, diag_hbm, pos_hbm, out_hbm, tiles_ref, diag_ref, pos_ref, out_ref, sems, out_sems):
    copies = [
        pltpu.make_async_copy(src, dst, sems.at[k])
        for k, (src, dst) in enumerate(((tiles_hbm, tiles_ref), (diag_hbm, diag_ref), (pos_hbm, pos_ref)))
    ]
    for copy in copies:
        copy.start()
    for copy in copies:
        copy.wait()
    lane = lane_iota()
    pieces = [tiles_ref[t] for t in range(TILES)] + [diag_ref[...]]
    wide = [
        jnp.concatenate([p, jnp.zeros((ORB, LANES - ORB), f32)], axis=1) for p in pieces
    ]
    gap = jnp.zeros((1, LANES - 2 * TILES), f32)
    both = pos_ref[...].astype(f32)
    places = jnp.concatenate([both[0:1], both[1:2], gap], axis=1)
    places = jnp.broadcast_to(places, (ORB, LANES))
    for q in range(WIDE // LANES):
        total = jnp.zeros((ORB, LANES), f32)
        for t in range(SLOTS):
            start = t * ORB - q * LANES
            if start <= -ORB or start >= LANES:
                continue
            inside = (lane >= max(start, 0)) & (lane < min(start + ORB, LANES))
            total = jnp.where(inside, roll_to(wide[t], 0, start), total)
        if q == WIDE // LANES - 1:
            start = SLOTS * ORB - q * LANES
            total = jnp.where(lane >= start, roll_to(places, 0, start), total)
        out_ref[:, q * LANES : (q + 1) * LANES] = total
    copies = [pltpu.make_async_copy(out_ref, out_hbm.at[k], out_sems.at[k]) for k in range(N_Y)]
    for copy in copies:
        copy.start()
    for copy in copies:
        copy.wait()


def pack(tile_data, diag, places):
    return pl.pallas_call(
        pack_kernel,
        out_shape=jax.ShapeDtypeStruct((N_Y, ORB, WIDE), f32),
        in_specs=[pl.BlockSpec(memory_space=pl.ANY)] * 3,
        out_specs=pl.BlockSpec(memory_space=pl.ANY),
        scratch_shapes=[
            pltpu.VMEM((TILES, ORB, ORB), f32),
            pltpu.VMEM((ORB, ORB), f32),
            pltpu.VMEM((2, TILES), jnp.int32),
            pltpu.VMEM((ORB, WIDE), f32),
            pltpu.SemaphoreType.DMA((3,)),
            pltpu.SemaphoreType.DMA((N_Y,)),
        ],
        compiler_params=pltpu.CompilerParams(vmem_limit_bytes=56 * 1024 * 1024),
        name="pack",
    )(tile_data, diag, places)


def unpack_kernel(in_ref, blocks_ref, places_ref):
    x = in_ref[...].reshape(N_Y * ORB, WIDE)
    high = x.astype(bf16)
    low = (x - high.astype(f32)).astype(bf16)
    for t in range(SLOTS):
        start = t * ORB
        q, off = start // LANES, start % LANES
        width = LANES if off + ORB <= LANES else 2 * LANES
        source = lax.broadcasted_iota(jnp.int32, (width, LANES), 0)
        target = lax.broadcasted_iota(jnp.int32, (width, LANES), 1)
        window = slice(q * LANES, q * LANES + width)
        total = None
        for term, at in ((high, 0), (low, 64)):
            hit = (target >= at) & (target < at + ORB) & (source == target - at + off)
            part = jnp.dot(term[:, window], jnp.where(hit, 1.0, 0.0).astype(bf16), preferred_element_type=f32)
            total = part if total is None else total + part
        total = total.astype(bf16)
        for s in range(N_Y):
            blocks_ref[s * SLOTS + t] = total[s * ORB : (s + 1) * ORB]
    for s in range(N_Y):
        last = in_ref[s, 0:1, WIDE - LANES : WIDE]
        shown = lax.broadcasted_iota(jnp.int32, (1, LANES), 1) >= PLACE
        places_ref[s : s + 1] = jnp.where(shown, last, 0.0).astype(jnp.int32)


def unpack(packed):
    return pl.pallas_call(
        unpack_kernel,
        out_shape=(
            jax.ShapeDtypeStruct((N_Y * SLOTS, ORB, LANES), bf16),
            jax.ShapeDtypeStruct((N_Y, LANES), jnp.int32),
        ),
        in_specs=vmem(1),
        out_specs=tuple(vmem(2)),
        compiler_params=params(),
        name="unpack",
    )(packed)


def slice_kernel(me_ref, in_ref, mine_ref, other_ref, own_ref):
    lane = lane_iota()
    zh, core, start = me_ref[1], me_ref[2], me_ref[3] * (2 * VS)

    def placed(block, k, target):
        shift = lax.rem(target - k * VS + 2 * LANES - start, LANES)
        return pltpu.roll(in_ref[block], shift, 1)

    for out_ref, k in ((mine_ref, core), (other_ref, 1 - core)):
        for zp in range(N_ZH // 2):
            total = jnp.zeros((ORB, LANES), f32)
            for half in range(2):
                for y in range(N_Y):
                    target = half * 64 + y * VS
                    inside = (lane >= target) & (lane < target + VS)
                    total = jnp.where(inside, placed((2 * zp + half) * N_Y + y, k, target), total)
            out_ref[zp] = total
    total = jnp.zeros((ORB, LANES), f32)
    for k in range(N_CORE):
        for y in range(N_Y):
            target = k * 64 + y * VS
            inside = (lane >= target) & (lane < target + VS)
            total = jnp.where(inside, placed(zh * N_Y + y, k, target), total)
    own_ref[...] = total


def slice_vectors(me, blocks):
    pair = jax.ShapeDtypeStruct((N_ZH // 2, ORB, LANES), f32)
    return pl.pallas_call(
        slice_kernel,
        out_shape=(pair, pair, jax.ShapeDtypeStruct((ORB, LANES), f32)),
        in_specs=[pl.BlockSpec(memory_space=pltpu.SMEM)] + vmem(1),
        out_specs=tuple(vmem(3)),
        compiler_params=params(),
        name="slice_vectors",
    )(me, blocks)


def join_kernel(me_ref, mine_ref, other_ref, out_ref):
    lane = lane_iota()
    is_zero = me_ref[2] == 0
    for zp in range(N_ZH // 2):
        mine, other = mine_ref[zp], other_ref[zp]
        a = jnp.where(is_zero, mine, other)
        b = jnp.where(is_zero, other, mine)
        out_ref[2 * zp] = jnp.where(lane < 64, a, pltpu.roll(b, 64, 1))
        out_ref[2 * zp + 1] = jnp.where(lane < 64, pltpu.roll(a, 64, 1), b)


def join_cores(me, mine, other):
    return pl.pallas_call(
        join_kernel,
        out_shape=jax.ShapeDtypeStruct((N_ZH, ORB, LANES), f32),
        in_specs=[pl.BlockSpec(memory_space=pltpu.SMEM)] + vmem(2),
        out_specs=vmem(1)[0],
        compiler_params=params(),
        name="join_cores",
    )(me, mine, other)


def pick_kernel(me_ref, in_ref, out_ref):
    lane = lane_iota()
    is_zero = me_ref[2] == 0
    for r in range(N_R):
        a, b = in_ref[2 * r], in_ref[2 * r + 1]
        first = jnp.where(is_zero, a, pltpu.roll(a, 64, 1))
        second = jnp.where(is_zero, pltpu.roll(b, 64, 1), b)
        out_ref[r] = jnp.where(lane < 64, first, second)


def pick_half(me, gathered):
    return pl.pallas_call(
        pick_kernel,
        out_shape=jax.ShapeDtypeStruct((N_R, ORB, LANES), f32),
        in_specs=[pl.BlockSpec(memory_space=pltpu.SMEM)] + vmem(1),
        out_specs=vmem(1)[0],
        compiler_params=params(),
        name="pick_half",
    )(me, gathered)


def split_terms(src_ref, dst_ref):
    gap = jnp.zeros((64 - ORB, LANES), f32)
    for chunk in range(src_ref.shape[0]):
        x = src_ref[chunk]
        x = jnp.concatenate([x, gap, x, gap], axis=0).T
        high = x.astype(bf16).astype(f32)
        low = x - high
        for o in range(GROUPS):
            rows = slice(o * VS, (o + 1) * VS)
            both = jnp.concatenate([high[rows], low[rows]], axis=0)
            dst_ref[chunk * GROUPS + o] = both.astype(bf16)


def row_col(pos_ref, core_s, s, t):
    i, g = pos_ref[s, PLACE + t], pos_ref[s, PLACE + TILES + t]
    row = (i >> 3) * GROUPS + core_s * N_Y + (i & 7)
    col = (g >> 1) * GROUPS + (g & 1) * N_Y + s
    return row, col


def mirror_kernel(me_ref, pos_a_ref, pos_b_ref, rows_ref, blocks_a_ref, blocks_b_ref, out_ref, v_ref, acc_ref):
    split_terms(rows_ref, v_ref)
    acc_ref[...] = jnp.zeros_like(acc_ref)
    core = me_ref[2]
    parts = ((pos_a_ref, blocks_a_ref, core), (pos_b_ref, blocks_b_ref, 1 - core))

    def two_sources(pair, carry):
        for s in (2 * pair, 2 * pair + 1):
            for t in range(TILES):
                for pos_ref, blocks_ref, core_s in parts:
                    row, col = row_col(pos_ref, core_s, s, t)
                    both = jnp.dot(v_ref[row][:, :ORB], blocks_ref[s * SLOTS + t], preferred_element_type=f32)
                    acc_ref[col] += both[:VS] + both[VS:]
        return carry

    lax.fori_loop(0, N_Y // 2, two_sources, 0)
    for chunk in range(out_ref.shape[0]):
        x = acc_ref[chunk * GROUPS : (chunk + 1) * GROUPS].reshape(LANES, LANES)
        x = x + pltpu.roll(x, 64, 1)
        out_ref[chunk] = x.T[:ORB]


def direct_kernel(me_ref, pos_a_ref, pos_b_ref, cols_ref, blocks_a_ref, blocks_b_ref, out_ref, v_ref, acc_ref):
    split_terms(cols_ref, v_ref)
    acc_ref[...] = jnp.zeros_like(acc_ref)
    my_r, my_zh, core = me_ref[0], me_ref[1], me_ref[2]
    parts = ((pos_a_ref, blocks_a_ref, core), (pos_b_ref, blocks_b_ref, 1 - core))

    def one_source(s, carry):
        for t in range(SLOTS):
            for pos_ref, blocks_ref, core_s in parts:
                if t < TILES:
                    row, col = row_col(pos_ref, core_s, s, t)
                else:
                    row = my_zh * GROUPS + core_s * N_Y + s
                    col = my_r * GROUPS + core_s * N_Y + s
                both = lax.dot_general(
                    v_ref[col], blocks_ref[s * SLOTS + t], (((1,), (1,)), ((), ())),
                    preferred_element_type=f32,
                )
                acc_ref[row, :, 0:ORB] += both[:VS] + both[VS:]
        return carry

    lax.fori_loop(0, N_Y, one_source, 0)
    for chunk in range(out_ref.shape[0]):
        x = acc_ref[chunk * GROUPS : (chunk + 1) * GROUPS].reshape(LANES, LANES)
        out_ref[chunk] = x.T[:ORB]


def product(kernel, name, scalars, field, blocks, chunks):
    smem = pl.BlockSpec(memory_space=pltpu.SMEM)
    return pl.pallas_call(
        kernel,
        out_shape=jax.ShapeDtypeStruct((chunks, ORB, LANES), f32),
        in_specs=[smem] * len(scalars) + vmem(1 + len(blocks)),
        out_specs=vmem(1)[0],
        scratch_shapes=[
            pltpu.VMEM((field.shape[0] * GROUPS, 2 * VS, LANES), bf16),
            pltpu.VMEM((chunks * GROUPS, VS, LANES), f32),
        ],
        compiler_params=params(),
        cost_estimate=pl.CostEstimate(flops=200000000, bytes_accessed=4000000, transcendentals=0),
        name=name,
    )(*scalars, field, *blocks)


def finish_kernel(me_ref, rows_ref, own_ref, current_ref, previous_ref, out_ref):
    lane = lane_iota()
    zh, core = me_ref[1], me_ref[2]
    mine = ((lane >> 3) & 1) == core
    scale = 2.0 / half_width
    own = scale * own_ref[...] - (scale * centre) * current_ref[zh] - previous_ref[zh]
    for z in range(N_ZH):
        total = scale * rows_ref[z] + jnp.where(zh == z, own, 0.0)
        for k in range(N_CORE):
            x = total if k == 0 else pltpu.roll(total, 64, 1)
            x = jnp.where(lane < 64, x, 0.0)
            for step in (32, 16, 8):
                block = lane & (4 * step - 1)
                moved = pltpu.roll(x, step, 1)
                x = jnp.where(block < step, x, jnp.where((block >= 2 * step) & (block < 3 * step), moved, 0.0))
            out_ref[k * N_ZH + z] = jnp.where(mine, pltpu.roll(x, core * VS, 1), 0.0)


def finish(me, rows, own, current, previous):
    return pl.pallas_call(
        finish_kernel,
        out_shape=jax.ShapeDtypeStruct((N_CORE * N_ZH, ORB, LANES), f32),
        in_specs=[pl.BlockSpec(memory_space=pltpu.SMEM)] + vmem(4),
        out_specs=vmem(1)[0],
        compiler_params=params(),
        name="finish",
    )(me, rows, own, current, previous)


def spread_kernel(in_ref, out_hbm, held, sems):
    lane = lane_iota()
    copies = []
    for z in range(N_ZH):
        x = [in_ref[y, z] for y in range(N_Y)]
        for d in (4, 2, 1):
            upper = (lane & (16 * d)) != 0
            for a in range(N_Y):
                if a & d:
                    continue
                low, high = x[a], x[a + d]
                x[a] = jnp.where(upper, pltpu.roll(high, 16 * d, 1), low)
                x[a + d] = jnp.where(upper, high, pltpu.roll(low, LANES - 16 * d, 1))
        for y in range(N_Y):
            held[z, y] = x[y]
        copy = pltpu.make_async_copy(held.at[z], out_hbm.at[pl.ds(z * N_Y, N_Y)], sems.at[z])
        copy.start()
        copies.append(copy)
    for copy in copies:
        copy.wait()


def spread(gathered):
    return pl.pallas_call(
        spread_kernel,
        out_shape=jax.ShapeDtypeStruct((N_ZH * N_Y, ORB, LANES), f32),
        in_specs=vmem(1),
        out_specs=pl.BlockSpec(memory_space=pl.ANY),
        scratch_shapes=[
            pltpu.VMEM((N_ZH, N_Y, ORB, LANES), f32),
            pltpu.SemaphoreType.DMA((N_ZH,)),
        ],
        compiler_params=params(),
        name="spread",
    )(gathered)


def merge_kernel(me_ref, rows_ref, cols_ref, out_ref):
    own = cols_ref[0]
    for r in range(1, N_R):
        own = own + cols_ref[r]
    for z in range(N_ZH):
        total = rows_ref[z] + jnp.where(me_ref[1] == z, own, 0.0)
        for copy in range(N_ZH):
            out_ref[copy, z] = total


def merge(me, rows, cols):
    return pl.pallas_call(
        merge_kernel,
        out_shape=jax.ShapeDtypeStruct((N_ZH, N_ZH, ORB, LANES), f32),
        in_specs=[pl.BlockSpec(memory_space=pltpu.SMEM)] + vmem(2),
        out_specs=vmem(1)[0],
        compiler_params=params(),
        name="merge",
    )(me, rows, cols)


def advance_kernel(me_ref, got_ref, *refs):
    *fields, out_ref, own_ref = refs
    for z in range(N_ZH):
        image = got_ref[0, z]
        for source in range(1, N_ZH):
            image = image + got_ref[source, z]
        shifted = (image - centre * fields[0][z]) / half_width
        out_ref[z] = shifted if len(fields) == 1 else 2.0 * shifted - fields[1][z]
    own = out_ref[me_ref[1]]
    for r in range(N_R):
        own_ref[r] = own


def advance(me, got, fields):
    return pl.pallas_call(
        advance_kernel,
        out_shape=(
            jax.ShapeDtypeStruct((N_ZH, ORB, LANES), f32),
            jax.ShapeDtypeStruct((N_R, ORB, LANES), f32),
        ),
        in_specs=[pl.BlockSpec(memory_space=pltpu.SMEM)] + vmem(1 + len(fields)),
        out_specs=tuple(vmem(2)),
        compiler_params=params(),
        name="advance",
    )(me, got, *fields)


def exchange(x, axes):
    return lax.all_to_all(x, axes, split_axis=0, concat_axis=0, tiled=True)


def gather(x, axes, n):
    return exchange(jnp.broadcast_to(x[None], (n,) + x.shape), axes)


def body(vectors, tiles, tile_pos, diag_blocks):
    zh = lax.axis_index("zh")
    r = lax.axis_index("x") * N_ZL + lax.axis_index("zl")
    me = jnp.stack([r, zh, lax.axis_index("core"), lax.axis_index("y")]).astype(jnp.int32)
    swap = [(0, 1), (1, 0)]

    packed = pack(tiles[0, 0], diag_blocks[0], tile_pos[0, 0])
    packed = exchange(packed, "y")

    mine, other, own = slice_vectors(me, vectors.reshape(-1, ORB, LANES))
    cols = pick_half(me, lax.all_gather(own, ("x", "zl", "core"), axis=0, tiled=False))
    current = join_cores(me, mine, lax.ppermute(other, "core", swap))

    packed, current, cols = lax.optimization_barrier((packed, current, cols))
    blocks_a, pos_a = unpack(packed)
    blocks_b, pos_b = unpack(lax.ppermute(packed, "core", swap))
    where, blocks = (me, pos_a, pos_b), (blocks_a, blocks_b)

    previous = None
    for step in range(DEGREE):
        out_cols = product(mirror_kernel, "mirror", where, current, blocks, N_R)
        out_cols, cols = lax.optimization_barrier((out_cols, cols))
        got_cols = exchange(out_cols, ROW_AX)
        out_rows = product(direct_kernel, "direct", where, cols, blocks, N_ZH)
        if step == DEGREE - 1:
            break
        got = exchange(merge(me, out_rows, got_cols), "zh")
        following, own = advance(me, got, (current,) if previous is None else (current, previous))
        previous, current = current, following
        cols = exchange(own, ROW_AX)

    result = jnp.sum(exchange(finish(me, out_rows, jnp.sum(got_cols, 0), current, previous), ("core", "zh")), 0)
    result = gather(result, ("y", "zh"), N_ZH * N_Y).reshape(N_Y, N_ZH, ORB, LANES)
    return spread(result).reshape(vectors.shape)


def solution(mesh):
    fine = Mesh(
        mesh.devices.reshape(N_X, N_ZL, N_CORE, N_ZH, N_Y), ("x", "zl", "core", "zh", "y")
    )
    row, col = ("x", "zl", "core"), ("zh", "y")
    return jax.shard_map(
        body,
        mesh=fine,
        in_specs=(
            P(row, None),
            P(row, col, None, None, None),
            P(row, col, None, None),
            P(row + col, None, None),
        ),
        out_specs=P(row, None),
        check_vma=False,
    )
```

```python
import functools

import jax
import jax.numpy as jnp
from jax import lax
from jax.experimental import pallas as pl
from jax.experimental.pallas import tpu as pltpu
from jax.sharding import Mesh, PartitionSpec as P

ORB = 56
DEGREE = 3
LANES = 128
N_X, N_ZL, N_CORE, N_ZH, N_Y = 4, 2, 2, 4, 8
N_R = N_X * N_ZL
TILES = 10
SLOTS = TILES + 1
WIDE = 640
VS = 8
PLACE = SLOTS * ORB - (WIDE - LANES)
ROW_AX = ("x", "zl")
GROUPS = N_CORE * N_Y

filter_low = 0.0
filter_high = 8.0
centre = 0.5 * (filter_high + filter_low)
half_width = 0.5 * (filter_high - filter_low)

f32 = jnp.float32
bf16 = jnp.bfloat16


def params():
    return pltpu.CompilerParams(vmem_limit_bytes=40 * 1024 * 1024)


def vmem(n):
    return [pl.BlockSpec(memory_space=pltpu.VMEM)] * n


def lane_iota(rows=ORB):
    return lax.broadcasted_iota(jnp.int32, (rows, LANES), 1)


def roll_to(x, source, target):
    shift = (target - source) % LANES
    return x if shift == 0 else pltpu.roll(x, shift, 1)


def pack_kernel(tiles_hbm, diag_hbm, pos_hbm, out_hbm, tiles_ref, diag_ref, pos_ref, out_ref, sems, out_sems):
    copies = [
        pltpu.make_async_copy(src, dst, sems.at[k])
        for k, (src, dst) in enumerate(((tiles_hbm, tiles_ref), (diag_hbm, diag_ref), (pos_hbm, pos_ref)))
    ]
    for copy in copies:
        copy.start()
    for copy in copies:
        copy.wait()
    lane = lane_iota()
    pieces = [tiles_ref[t] for t in range(TILES)] + [diag_ref[...]]
    wide = [
        jnp.concatenate([p, jnp.zeros((ORB, LANES - ORB), f32)], axis=1) for p in pieces
    ]
    gap = jnp.zeros((1, LANES - 2 * TILES), f32)
    both = pos_ref[...].astype(f32)
    places = jnp.concatenate([both[0:1], both[1:2], gap], axis=1)
    places = jnp.broadcast_to(places, (ORB, LANES))
    for q in range(WIDE // LANES):
        total = jnp.zeros((ORB, LANES), f32)
        for t in range(SLOTS):
            start = t * ORB - q * LANES
            if start <= -ORB or start >= LANES:
                continue
            inside = (lane >= max(start, 0)) & (lane < min(start + ORB, LANES))
            total = jnp.where(inside, roll_to(wide[t], 0, start), total)
        if q == WIDE // LANES - 1:
            start = SLOTS * ORB - q * LANES
            total = jnp.where(lane >= start, roll_to(places, 0, start), total)
        out_ref[:, q * LANES : (q + 1) * LANES] = total
    copies = [pltpu.make_async_copy(out_ref, out_hbm.at[k], out_sems.at[k]) for k in range(N_Y)]
    for copy in copies:
        copy.start()
    for copy in copies:
        copy.wait()


def pack(tile_data, diag, places):
    return pl.pallas_call(
        pack_kernel,
        out_shape=jax.ShapeDtypeStruct((N_Y, ORB, WIDE), f32),
        in_specs=[pl.BlockSpec(memory_space=pl.ANY)] * 3,
        out_specs=pl.BlockSpec(memory_space=pl.ANY),
        scratch_shapes=[
            pltpu.VMEM((TILES, ORB, ORB), f32),
            pltpu.VMEM((ORB, ORB), f32),
            pltpu.VMEM((2, TILES), jnp.int32),
            pltpu.VMEM((ORB, WIDE), f32),
            pltpu.SemaphoreType.DMA((3,)),
            pltpu.SemaphoreType.DMA((N_Y,)),
        ],
        compiler_params=pltpu.CompilerParams(vmem_limit_bytes=56 * 1024 * 1024),
        name="pack",
    )(tile_data, diag, places)


def unpack_kernel(in_ref, blocks_ref, places_ref):
    x = in_ref[...].reshape(N_Y * ORB, WIDE)
    high = x.astype(bf16)
    low = (x - high.astype(f32)).astype(bf16)
    for t in range(SLOTS):
        start = t * ORB
        q, off = start // LANES, start % LANES
        width = LANES if off + ORB <= LANES else 2 * LANES
        source = lax.broadcasted_iota(jnp.int32, (width, LANES), 0)
        target = lax.broadcasted_iota(jnp.int32, (width, LANES), 1)
        window = slice(q * LANES, q * LANES + width)
        total = None
        for term, at in ((high, 0), (low, 64)):
            hit = (target >= at) & (target < at + ORB) & (source == target - at + off)
            part = jnp.dot(term[:, window], jnp.where(hit, 1.0, 0.0).astype(bf16), preferred_element_type=f32)
            total = part if total is None else total + part
        total = total.astype(bf16)
        for s in range(N_Y):
            blocks_ref[s * SLOTS + t] = total[s * ORB : (s + 1) * ORB]
    for s in range(N_Y):
        last = in_ref[s, 0:1, WIDE - LANES : WIDE]
        shown = lax.broadcasted_iota(jnp.int32, (1, LANES), 1) >= PLACE
        places_ref[s : s + 1] = jnp.where(shown, last, 0.0).astype(jnp.int32)


def unpack(packed):
    return pl.pallas_call(
        unpack_kernel,
        out_shape=(
            jax.ShapeDtypeStruct((N_Y * SLOTS, ORB, LANES), bf16),
            jax.ShapeDtypeStruct((N_Y, LANES), jnp.int32),
        ),
        in_specs=vmem(1),
        out_specs=tuple(vmem(2)),
        compiler_params=params(),
        name="unpack",
    )(packed)


def slice_kernel(me_ref, in_ref, mine_ref, other_ref, own_ref):
    lane = lane_iota()
    zh, core, start = me_ref[1], me_ref[2], me_ref[3] * (2 * VS)

    def placed(block, k, target):
        shift = lax.rem(target - k * VS + 2 * LANES - start, LANES)
        return pltpu.roll(in_ref[block], shift, 1)

    for out_ref, k in ((mine_ref, core), (other_ref, 1 - core)):
        for zp in range(N_ZH // 2):
            total = jnp.zeros((ORB, LANES), f32)
            for half in range(2):
                for y in range(N_Y):
                    target = half * 64 + y * VS
                    inside = (lane >= target) & (lane < target + VS)
                    total = jnp.where(inside, placed((2 * zp + half) * N_Y + y, k, target), total)
            out_ref[zp] = total
    total = jnp.zeros((ORB, LANES), f32)
    for k in range(N_CORE):
        for y in range(N_Y):
            target = k * 64 + y * VS
            inside = (lane >= target) & (lane < target + VS)
            total = jnp.where(inside, placed(zh * N_Y + y, k, target), total)
    own_ref[...] = total


def slice_vectors(me, blocks):
    pair = jax.ShapeDtypeStruct((N_ZH // 2, ORB, LANES), f32)
    return pl.pallas_call(
        slice_kernel,
        out_shape=(pair, pair, jax.ShapeDtypeStruct((ORB, LANES), f32)),
        in_specs=[pl.BlockSpec(memory_space=pltpu.SMEM)] + vmem(1),
        out_specs=tuple(vmem(3)),
        compiler_params=params(),
        name="slice_vectors",
    )(me, blocks)


def join_kernel(me_ref, mine_ref, other_ref, out_ref):
    lane = lane_iota()
    is_zero = me_ref[2] == 0
    for zp in range(N_ZH // 2):
        mine, other = mine_ref[zp], other_ref[zp]
        a = jnp.where(is_zero, mine, other)
        b = jnp.where(is_zero, other, mine)
        out_ref[2 * zp] = jnp.where(lane < 64, a, pltpu.roll(b, 64, 1))
        out_ref[2 * zp + 1] = jnp.where(lane < 64, pltpu.roll(a, 64, 1), b)


def join_cores(me, mine, other):
    return pl.pallas_call(
        join_kernel,
        out_shape=jax.ShapeDtypeStruct((N_ZH, ORB, LANES), f32),
        in_specs=[pl.BlockSpec(memory_space=pltpu.SMEM)] + vmem(2),
        out_specs=vmem(1)[0],
        compiler_params=params(),
        name="join_cores",
    )(me, mine, other)


def pick_kernel(me_ref, in_ref, out_ref):
    lane = lane_iota()
    is_zero = me_ref[2] == 0
    for r in range(N_R):
        a, b = in_ref[2 * r], in_ref[2 * r + 1]
        first = jnp.where(is_zero, a, pltpu.roll(a, 64, 1))
        second = jnp.where(is_zero, pltpu.roll(b, 64, 1), b)
        out_ref[r] = jnp.where(lane < 64, first, second)


def pick_half(me, gathered):
    return pl.pallas_call(
        pick_kernel,
        out_shape=jax.ShapeDtypeStruct((N_R, ORB, LANES), f32),
        in_specs=[pl.BlockSpec(memory_space=pltpu.SMEM)] + vmem(1),
        out_specs=vmem(1)[0],
        compiler_params=params(),
        name="pick_half",
    )(me, gathered)


def split_terms(src_ref, dst_ref):
    gap = jnp.zeros((64 - ORB, LANES), f32)
    for chunk in range(src_ref.shape[0]):
        x = src_ref[chunk]
        x = jnp.concatenate([x, gap, x, gap], axis=0).T
        high = x.astype(bf16).astype(f32)
        low = x - high
        for o in range(GROUPS):
            rows = slice(o * VS, (o + 1) * VS)
            both = jnp.concatenate([high[rows], low[rows]], axis=0)
            dst_ref[chunk * GROUPS + o] = both.astype(bf16)


def row_col(pos_ref, core_s, s, t):
    i, g = pos_ref[s, PLACE + t], pos_ref[s, PLACE + TILES + t]
    row = (i >> 3) * GROUPS + core_s * N_Y + (i & 7)
    col = (g >> 1) * GROUPS + (g & 1) * N_Y + s
    return row, col


def mirror_kernel(me_ref, pos_a_ref, pos_b_ref, rows_ref, blocks_a_ref, blocks_b_ref, out_ref, v_ref, acc_ref):
    split_terms(rows_ref, v_ref)
    acc_ref[...] = jnp.zeros_like(acc_ref)
    core = me_ref[2]
    parts = ((pos_a_ref, blocks_a_ref, core), (pos_b_ref, blocks_b_ref, 1 - core))

    def two_sources(pair, carry):
        for s in (2 * pair, 2 * pair + 1):
            for t in range(TILES):
                for pos_ref, blocks_ref, core_s in parts:
                    row, col = row_col(pos_ref, core_s, s, t)
                    both = jnp.dot(v_ref[row][:, :ORB], blocks_ref[s * SLOTS + t], preferred_element_type=f32)
                    acc_ref[col] += both[:VS] + both[VS:]
        return carry

    lax.fori_loop(0, N_Y // 2, two_sources, 0)
    for chunk in range(out_ref.shape[0]):
        x = acc_ref[chunk * GROUPS : (chunk + 1) * GROUPS].reshape(LANES, LANES)
        x = x + pltpu.roll(x, 64, 1)
        out_ref[chunk] = x.T[:ORB]


def direct_kernel(me_ref, pos_a_ref, pos_b_ref, cols_ref, blocks_a_ref, blocks_b_ref, out_ref, v_ref, acc_ref):
    split_terms(cols_ref, v_ref)
    acc_ref[...] = jnp.zeros_like(acc_ref)
    my_r, my_zh, core = me_ref[0], me_ref[1], me_ref[2]
    parts = ((pos_a_ref, blocks_a_ref, core), (pos_b_ref, blocks_b_ref, 1 - core))

    def one_source(s, carry):
        for t in range(SLOTS):
            for pos_ref, blocks_ref, core_s in parts:
                if t < TILES:
                    row, col = row_col(pos_ref, core_s, s, t)
                else:
                    row = my_zh * GROUPS + core_s * N_Y + s
                    col = my_r * GROUPS + core_s * N_Y + s
                both = lax.dot_general(
                    v_ref[col], blocks_ref[s * SLOTS + t], (((1,), (1,)), ((), ())),
                    preferred_element_type=f32,
                )
                acc_ref[row, :, 0:ORB] += both[:VS] + both[VS:]
        return carry

    lax.fori_loop(0, N_Y, one_source, 0)
    for chunk in range(out_ref.shape[0]):
        x = acc_ref[chunk * GROUPS : (chunk + 1) * GROUPS].reshape(LANES, LANES)
        out_ref[chunk] = x.T[:ORB]


def product(kernel, name, scalars, field, blocks, chunks):
    smem = pl.BlockSpec(memory_space=pltpu.SMEM)
    return pl.pallas_call(
        kernel,
        out_shape=jax.ShapeDtypeStruct((chunks, ORB, LANES), f32),
        in_specs=[smem] * len(scalars) + vmem(1 + len(blocks)),
        out_specs=vmem(1)[0],
        scratch_shapes=[
            pltpu.VMEM((field.shape[0] * GROUPS, 2 * VS, LANES), bf16),
            pltpu.VMEM((chunks * GROUPS, VS, LANES), f32),
        ],
        compiler_params=params(),
        cost_estimate=pl.CostEstimate(flops=200000000, bytes_accessed=4000000, transcendentals=0),
        name=name,
    )(*scalars, field, *blocks)


def finish_kernel(me_ref, rows_ref, own_ref, current_ref, previous_ref, out_ref):
    lane = lane_iota()
    zh, core = me_ref[1], me_ref[2]
    scale = 2.0 / half_width
    own = scale * own_ref[...] - (scale * centre) * current_ref[zh] - previous_ref[zh]
    for z in range(N_ZH):
        total = scale * rows_ref[z] + jnp.where(zh == z, own, 0.0)
        for k in range(N_CORE):
            x = total if k == 0 else pltpu.roll(total, 64, 1)
            x = jnp.where(lane < 64, x, 0.0)
            for step in (32, 16, 8):
                block = lane & (4 * step - 1)
                moved = pltpu.roll(x, step, 1)
                x = jnp.where(block < step, x, jnp.where((block >= 2 * step) & (block < 3 * step), moved, 0.0))
            out_ref[k * N_ZH + z] = pltpu.roll(x, core * VS, 1)


def finish(me, rows, own, current, previous):
    return pl.pallas_call(
        finish_kernel,
        out_shape=jax.ShapeDtypeStruct((N_CORE * N_ZH, ORB, LANES), f32),
        in_specs=[pl.BlockSpec(memory_space=pltpu.SMEM)] + vmem(4),
        out_specs=vmem(1)[0],
        compiler_params=params(),
        name="finish",
    )(me, rows, own, current, previous)


def spread_kernel(in_ref, out_hbm, held, sems):
    lane = lane_iota()
    copies = []
    for z in range(N_ZH):
        x = [in_ref[y, z] for y in range(N_Y)]
        for d in (4, 2, 1):
            upper = (lane & (16 * d)) != 0
            for a in range(N_Y):
                if a & d:
                    continue
                low, high = x[a], x[a + d]
                x[a] = jnp.where(upper, pltpu.roll(high, 16 * d, 1), low)
                x[a + d] = jnp.where(upper, high, pltpu.roll(low, LANES - 16 * d, 1))
        for y in range(N_Y):
            held[z, y] = x[y]
        copy = pltpu.make_async_copy(held.at[z], out_hbm.at[pl.ds(z * N_Y, N_Y)], sems.at[z])
        copy.start()
        copies.append(copy)
    for copy in copies:
        copy.wait()


def spread(gathered):
    return pl.pallas_call(
        spread_kernel,
        out_shape=jax.ShapeDtypeStruct((N_ZH * N_Y, ORB, LANES), f32),
        in_specs=vmem(1),
        out_specs=pl.BlockSpec(memory_space=pl.ANY),
        scratch_shapes=[
            pltpu.VMEM((N_ZH, N_Y, ORB, LANES), f32),
            pltpu.SemaphoreType.DMA((N_ZH,)),
        ],
        compiler_params=params(),
        name="spread",
    )(gathered)


def merge_kernel(me_ref, rows_ref, cols_ref, out_ref):
    own = cols_ref[0]
    for r in range(1, N_R):
        own = own + cols_ref[r]
    for z in range(N_ZH):
        total = rows_ref[z] + jnp.where(me_ref[1] == z, own, 0.0)
        for copy in range(N_ZH):
            out_ref[copy, z] = total


def merge(me, rows, cols):
    return pl.pallas_call(
        merge_kernel,
        out_shape=jax.ShapeDtypeStruct((N_ZH, N_ZH, ORB, LANES), f32),
        in_specs=[pl.BlockSpec(memory_space=pltpu.SMEM)] + vmem(2),
        out_specs=vmem(1)[0],
        compiler_params=params(),
        name="merge",
    )(me, rows, cols)


def exchange(x, axes):
    return lax.all_to_all(x, axes, split_axis=0, concat_axis=0, tiled=True)


def gather(x, axes, n):
    return exchange(jnp.broadcast_to(x[None], (n,) + x.shape), axes)


def body(vectors, tiles, tile_pos, diag_blocks):
    zh = lax.axis_index("zh")
    r = lax.axis_index("x") * N_ZL + lax.axis_index("zl")
    me = jnp.stack([r, zh, lax.axis_index("core"), lax.axis_index("y")]).astype(jnp.int32)
    swap = [(0, 1), (1, 0)]

    packed = pack(tiles[0, 0], diag_blocks[0], tile_pos[0, 0])
    packed = exchange(packed, "y")

    mine, other, own = slice_vectors(me, vectors.reshape(-1, ORB, LANES))
    cols = pick_half(me, lax.all_gather(own, ("x", "zl", "core"), axis=0, tiled=False))
    current = join_cores(me, mine, lax.ppermute(other, "core", swap))

    packed, current, cols = lax.optimization_barrier((packed, current, cols))
    blocks_a, pos_a = unpack(packed)
    blocks_b, pos_b = unpack(lax.ppermute(packed, "core", swap))
    where, blocks = (me, pos_a, pos_b), (blocks_a, blocks_b)

    previous = None
    for step in range(DEGREE):
        out_cols = product(mirror_kernel, "mirror", where, current, blocks, N_R)
        out_cols, cols = lax.optimization_barrier((out_cols, cols))
        got_cols = exchange(out_cols, ROW_AX)
        out_rows = product(direct_kernel, "direct", where, cols, blocks, N_ZH)
        if step == DEGREE - 1:
            break
        got = exchange(merge(me, out_rows, got_cols), "zh")
        got, current, own_at = lax.optimization_barrier((got, current, zh))
        shifted = (jnp.sum(got, 0) - centre * current) / half_width
        following = shifted if previous is None else 2.0 * shifted - previous
        previous, current = current, following
        cols = gather(lax.dynamic_index_in_dim(current, own_at, 0, keepdims=False), ROW_AX, N_R)

    result = jnp.sum(exchange(finish(me, out_rows, jnp.sum(got_cols, 0), current, previous), ("core", "zh")), 0)
    result = gather(result, ("y", "zh"), N_ZH * N_Y).reshape(N_Y, N_ZH, ORB, LANES)
    return spread(result).reshape(vectors.shape)


def solution(mesh):
    fine = Mesh(
        mesh.devices.reshape(N_X, N_ZL, N_CORE, N_ZH, N_Y), ("x", "zl", "core", "zh", "y")
    )
    row, col = ("x", "zl", "core"), ("zh", "y")
    return jax.shard_map(
        body,
        mesh=fine,
        in_specs=(
            P(row, None),
            P(row, col, None, None, None),
            P(row, col, None, None),
            P(row + col, None, None),
        ),
        out_specs=P(row, None),
        check_vma=False,
    )
```

```python
import functools

import jax
import jax.numpy as jnp
from jax import lax
from jax.experimental import pallas as pl
from jax.experimental.pallas import tpu as pltpu
from jax.sharding import Mesh, PartitionSpec as P

ORB = 56
DEGREE = 3
LANES = 128
N_X, N_ZL, N_CORE, N_ZH, N_Y = 4, 2, 2, 4, 8
N_R = N_X * N_ZL
TILES = 10
SLOTS = TILES + 1
WIDE = 640
VS = 8
PLACE = SLOTS * ORB - (WIDE - LANES)
ROW_AX = ("x", "zl")
GROUPS = N_CORE * N_Y

filter_low = 0.0
filter_high = 8.0
centre = 0.5 * (filter_high + filter_low)
half_width = 0.5 * (filter_high - filter_low)

f32 = jnp.float32
bf16 = jnp.bfloat16


def params():
    return pltpu.CompilerParams(vmem_limit_bytes=40 * 1024 * 1024)


def vmem(n):
    return [pl.BlockSpec(memory_space=pltpu.VMEM)] * n


def lane_iota(rows=ORB):
    return lax.broadcasted_iota(jnp.int32, (rows, LANES), 1)


def roll_to(x, source, target):
    shift = (target - source) % LANES
    return x if shift == 0 else pltpu.roll(x, shift, 1)


def pack_kernel(tiles_hbm, diag_hbm, pos_hbm, out_hbm, tiles_ref, diag_ref, pos_ref, out_ref, sems, out_sems):
    copies = [
        pltpu.make_async_copy(src, dst, sems.at[k])
        for k, (src, dst) in enumerate(((tiles_hbm, tiles_ref), (diag_hbm, diag_ref), (pos_hbm, pos_ref)))
    ]
    for copy in copies:
        copy.start()
    for copy in copies:
        copy.wait()
    lane = lane_iota()
    pieces = [tiles_ref[t] for t in range(TILES)] + [diag_ref[...]]
    wide = [
        jnp.concatenate([p, jnp.zeros((ORB, LANES - ORB), f32)], axis=1) for p in pieces
    ]
    gap = jnp.zeros((1, LANES - 2 * TILES), f32)
    both = pos_ref[...].astype(f32)
    places = jnp.concatenate([both[0:1], both[1:2], gap], axis=1)
    places = jnp.broadcast_to(places, (ORB, LANES))
    for q in range(WIDE // LANES):
        total = jnp.zeros((ORB, LANES), f32)
        for t in range(SLOTS):
            start = t * ORB - q * LANES
            if start <= -ORB or start >= LANES:
                continue
            inside = (lane >= max(start, 0)) & (lane < min(start + ORB, LANES))
            total = jnp.where(inside, roll_to(wide[t], 0, start), total)
        if q == WIDE // LANES - 1:
            start = SLOTS * ORB - q * LANES
            total = jnp.where(lane >= start, roll_to(places, 0, start), total)
        out_ref[:, q * LANES : (q + 1) * LANES] = total
    copies = [pltpu.make_async_copy(out_ref, out_hbm.at[k], out_sems.at[k]) for k in range(N_Y)]
    for copy in copies:
        copy.start()
    for copy in copies:
        copy.wait()


def pack(tile_data, diag, places):
    return pl.pallas_call(
        pack_kernel,
        out_shape=jax.ShapeDtypeStruct((N_Y, ORB, WIDE), f32),
        in_specs=[pl.BlockSpec(memory_space=pl.ANY)] * 3,
        out_specs=pl.BlockSpec(memory_space=pl.ANY),
        scratch_shapes=[
            pltpu.VMEM((TILES, ORB, ORB), f32),
            pltpu.VMEM((ORB, ORB), f32),
            pltpu.VMEM((2, TILES), jnp.int32),
            pltpu.VMEM((ORB, WIDE), f32),
            pltpu.SemaphoreType.DMA((3,)),
            pltpu.SemaphoreType.DMA((N_Y,)),
        ],
        compiler_params=pltpu.CompilerParams(vmem_limit_bytes=56 * 1024 * 1024),
        name="pack",
    )(tile_data, diag, places)


def unpack_kernel(in_ref, blocks_ref, places_ref):
    x = in_ref[...].reshape(N_Y * ORB, WIDE)
    high = x.astype(bf16)
    low = (x - high.astype(f32)).astype(bf16)
    for t in range(SLOTS):
        start = t * ORB
        q, off = start // LANES, start % LANES
        width = LANES if off + ORB <= LANES else 2 * LANES
        source = lax.broadcasted_iota(jnp.int32, (width, LANES), 0)
        target = lax.broadcasted_iota(jnp.int32, (width, LANES), 1)
        window = slice(q * LANES, q * LANES + width)
        total = None
        for term, at in ((high, 0), (low, 64)):
            hit = (target >= at) & (target < at + ORB) & (source == target - at + off)
            part = jnp.dot(term[:, window], jnp.where(hit, 1.0, 0.0).astype(bf16), preferred_element_type=f32)
            total = part if total is None else total + part
        for s in range(N_Y):
            blocks_ref[s * SLOTS + t] = total[s * ORB : (s + 1) * ORB].astype(bf16)
    for s in range(N_Y):
        last = in_ref[s, 0:1, WIDE - LANES : WIDE]
        shown = lax.broadcasted_iota(jnp.int32, (1, LANES), 1) >= PLACE
        places_ref[s : s + 1] = jnp.where(shown, last, 0.0).astype(jnp.int32)


def unpack(packed):
    return pl.pallas_call(
        unpack_kernel,
        out_shape=(
            jax.ShapeDtypeStruct((N_Y * SLOTS, ORB, LANES), bf16),
            jax.ShapeDtypeStruct((N_Y, LANES), jnp.int32),
        ),
        in_specs=vmem(1),
        out_specs=tuple(vmem(2)),
        compiler_params=params(),
        name="unpack",
    )(packed)


def slice_kernel(me_ref, in_ref, mine_ref, other_ref, own_ref):
    lane = lane_iota()
    zh, core, start = me_ref[1], me_ref[2], me_ref[3] * (2 * VS)

    def placed(block, k, target):
        shift = lax.rem(target - k * VS + 2 * LANES - start, LANES)
        return pltpu.roll(in_ref[block], shift, 1)

    for out_ref, k in ((mine_ref, core), (other_ref, 1 - core)):
        for zp in range(N_ZH // 2):
            total = jnp.zeros((ORB, LANES), f32)
            for half in range(2):
                for y in range(N_Y):
                    target = half * 64 + y * VS
                    inside = (lane >= target) & (lane < target + VS)
                    total = jnp.where(inside, placed((2 * zp + half) * N_Y + y, k, target), total)
            out_ref[zp] = total
    total = jnp.zeros((ORB, LANES), f32)
    for k in range(N_CORE):
        for y in range(N_Y):
            target = k * 64 + y * VS
            inside = (lane >= target) & (lane < target + VS)
            total = jnp.where(inside, placed(zh * N_Y + y, k, target), total)
    own_ref[...] = total


def slice_vectors(me, blocks):
    pair = jax.ShapeDtypeStruct((N_ZH // 2, ORB, LANES), f32)
    return pl.pallas_call(
        slice_kernel,
        out_shape=(pair, pair, jax.ShapeDtypeStruct((ORB, LANES), f32)),
        in_specs=[pl.BlockSpec(memory_space=pltpu.SMEM)] + vmem(1),
        out_specs=tuple(vmem(3)),
        compiler_params=params(),
        name="slice_vectors",
    )(me, blocks)


def join_kernel(me_ref, mine_ref, other_ref, out_ref):
    lane = lane_iota()
    is_zero = me_ref[2] == 0
    for zp in range(N_ZH // 2):
        mine, other = mine_ref[zp], other_ref[zp]
        a = jnp.where(is_zero, mine, other)
        b = jnp.where(is_zero, other, mine)
        out_ref[2 * zp] = jnp.where(lane < 64, a, pltpu.roll(b, 64, 1))
        out_ref[2 * zp + 1] = jnp.where(lane < 64, pltpu.roll(a, 64, 1), b)


def join_cores(me, mine, other):
    return pl.pallas_call(
        join_kernel,
        out_shape=jax.ShapeDtypeStruct((N_ZH, ORB, LANES), f32),
        in_specs=[pl.BlockSpec(memory_space=pltpu.SMEM)] + vmem(2),
        out_specs=vmem(1)[0],
        compiler_params=params(),
        name="join_cores",
    )(me, mine, other)


def pick_kernel(me_ref, in_ref, out_ref):
    lane = lane_iota()
    is_zero = me_ref[2] == 0
    for r in range(N_R):
        a, b = in_ref[2 * r], in_ref[2 * r + 1]
        first = jnp.where(is_zero, a, pltpu.roll(a, 64, 1))
        second = jnp.where(is_zero, pltpu.roll(b, 64, 1), b)
        out_ref[r] = jnp.where(lane < 64, first, second)


def pick_half(me, gathered):
    return pl.pallas_call(
        pick_kernel,
        out_shape=jax.ShapeDtypeStruct((N_R, ORB, LANES), f32),
        in_specs=[pl.BlockSpec(memory_space=pltpu.SMEM)] + vmem(1),
        out_specs=vmem(1)[0],
        compiler_params=params(),
        name="pick_half",
    )(me, gathered)


def split_terms(src_ref, dst_ref):
    gap = jnp.zeros((64 - ORB, LANES), f32)
    for chunk in range(src_ref.shape[0]):
        x = src_ref[chunk]
        x = jnp.concatenate([x, gap, x, gap], axis=0).T
        high = x.astype(bf16).astype(f32)
        low = x - high
        for o in range(GROUPS):
            rows = slice(o * VS, (o + 1) * VS)
            both = jnp.concatenate([high[rows], low[rows]], axis=0)
            dst_ref[chunk * GROUPS + o] = both.astype(bf16)


def row_col(pos_ref, core_s, s, t):
    i, g = pos_ref[s, PLACE + t], pos_ref[s, PLACE + TILES + t]
    row = (i >> 3) * GROUPS + core_s * N_Y + (i & 7)
    col = (g >> 1) * GROUPS + (g & 1) * N_Y + s
    return row, col


def mirror_kernel(me_ref, pos_a_ref, pos_b_ref, rows_ref, blocks_a_ref, blocks_b_ref, out_ref, v_ref, acc_ref):
    split_terms(rows_ref, v_ref)
    acc_ref[...] = jnp.zeros_like(acc_ref)
    core = me_ref[2]
    parts = ((pos_a_ref, blocks_a_ref, core), (pos_b_ref, blocks_b_ref, 1 - core))

    def two_sources(pair, carry):
        for s in (2 * pair, 2 * pair + 1):
            for t in range(TILES):
                for pos_ref, blocks_ref, core_s in parts:
                    row, col = row_col(pos_ref, core_s, s, t)
                    both = jnp.dot(v_ref[row][:, :ORB], blocks_ref[s * SLOTS + t], preferred_element_type=f32)
                    acc_ref[col] += both[:VS] + both[VS:]
        return carry

    lax.fori_loop(0, N_Y // 2, two_sources, 0)
    for chunk in range(out_ref.shape[0]):
        x = acc_ref[chunk * GROUPS : (chunk + 1) * GROUPS].reshape(LANES, LANES)
        x = x + pltpu.roll(x, 64, 1)
        out_ref[chunk] = x.T[:ORB]


def direct_kernel(me_ref, pos_a_ref, pos_b_ref, cols_ref, blocks_a_ref, blocks_b_ref, out_ref, v_ref, acc_ref):
    split_terms(cols_ref, v_ref)
    acc_ref[...] = jnp.zeros_like(acc_ref)
    my_r, my_zh, core = me_ref[0], me_ref[1], me_ref[2]
    parts = ((pos_a_ref, blocks_a_ref, core), (pos_b_ref, blocks_b_ref, 1 - core))

    def one_source(s, carry):
        for t in range(SLOTS):
            for pos_ref, blocks_ref, core_s in parts:
                if t < TILES:
                    row, col = row_col(pos_ref, core_s, s, t)
                else:
                    row = my_zh * GROUPS + core_s * N_Y + s
                    col = my_r * GROUPS + core_s * N_Y + s
                both = lax.dot_general(
                    v_ref[col], blocks_ref[s * SLOTS + t], (((1,), (1,)), ((), ())),
                    preferred_element_type=f32,
                )
                acc_ref[row, :, 0:ORB] += both[:VS] + both[VS:]
        return carry

    lax.fori_loop(0, N_Y, one_source, 0)
    for chunk in range(out_ref.shape[0]):
        x = acc_ref[chunk * GROUPS : (chunk + 1) * GROUPS].reshape(LANES, LANES)
        out_ref[chunk] = x.T[:ORB]


def product(kernel, name, scalars, field, blocks, chunks):
    smem = pl.BlockSpec(memory_space=pltpu.SMEM)
    return pl.pallas_call(
        kernel,
        out_shape=jax.ShapeDtypeStruct((chunks, ORB, LANES), f32),
        in_specs=[smem] * len(scalars) + vmem(1 + len(blocks)),
        out_specs=vmem(1)[0],
        scratch_shapes=[
            pltpu.VMEM((field.shape[0] * GROUPS, 2 * VS, LANES), bf16),
            pltpu.VMEM((chunks * GROUPS, VS, LANES), f32),
        ],
        compiler_params=params(),
        cost_estimate=pl.CostEstimate(flops=200000000, bytes_accessed=4000000, transcendentals=0),
        name=name,
    )(*scalars, field, *blocks)


def finish_kernel(me_ref, rows_ref, own_ref, current_ref, previous_ref, out_ref):
    lane = lane_iota()
    zh, core = me_ref[1], me_ref[2]
    scale = 2.0 / half_width
    own = scale * own_ref[...] - (scale * centre) * current_ref[zh] - previous_ref[zh]
    for z in range(N_ZH):
        total = scale * rows_ref[z] + jnp.where(zh == z, own, 0.0)
        for k in range(N_CORE):
            x = total if k == 0 else pltpu.roll(total, 64, 1)
            x = jnp.where(lane < 64, x, 0.0)
            for step in (32, 16, 8):
                block = lane & (4 * step - 1)
                moved = pltpu.roll(x, step, 1)
                x = jnp.where(block < step, x, jnp.where((block >= 2 * step) & (block < 3 * step), moved, 0.0))
            out_ref[k * N_ZH + z] = pltpu.roll(x, core * VS, 1)


def finish(me, rows, own, current, previous):
    return pl.pallas_call(
        finish_kernel,
        out_shape=jax.ShapeDtypeStruct((N_CORE * N_ZH, ORB, LANES), f32),
        in_specs=[pl.BlockSpec(memory_space=pltpu.SMEM)] + vmem(4),
        out_specs=vmem(1)[0],
        compiler_params=params(),
        name="finish",
    )(me, rows, own, current, previous)


def spread_kernel(in_ref, out_hbm, held, sems):
    lane = lane_iota()
    copies = []
    for z in range(N_ZH):
        x = [in_ref[y, z] for y in range(N_Y)]
        for d in (4, 2, 1):
            upper = (lane & (16 * d)) != 0
            for a in range(N_Y):
                if a & d:
                    continue
                low, high = x[a], x[a + d]
                x[a] = jnp.where(upper, pltpu.roll(high, 16 * d, 1), low)
                x[a + d] = jnp.where(upper, high, pltpu.roll(low, LANES - 16 * d, 1))
        for y in range(N_Y):
            held[z, y] = x[y]
        copy = pltpu.make_async_copy(held.at[z], out_hbm.at[pl.ds(z * N_Y, N_Y)], sems.at[z])
        copy.start()
        copies.append(copy)
    for copy in copies:
        copy.wait()


def spread(gathered):
    return pl.pallas_call(
        spread_kernel,
        out_shape=jax.ShapeDtypeStruct((N_ZH * N_Y, ORB, LANES), f32),
        in_specs=vmem(1),
        out_specs=pl.BlockSpec(memory_space=pl.ANY),
        scratch_shapes=[
            pltpu.VMEM((N_ZH, N_Y, ORB, LANES), f32),
            pltpu.SemaphoreType.DMA((N_ZH,)),
        ],
        compiler_params=params(),
        name="spread",
    )(gathered)


def merge_kernel(me_ref, rows_ref, cols_ref, out_ref):
    own = cols_ref[0]
    for r in range(1, N_R):
        own = own + cols_ref[r]
    for z in range(N_ZH):
        total = rows_ref[z] + jnp.where(me_ref[1] == z, own, 0.0)
        for copy in range(N_ZH):
            out_ref[copy, z] = total


def merge(me, rows, cols):
    return pl.pallas_call(
        merge_kernel,
        out_shape=jax.ShapeDtypeStruct((N_ZH, N_ZH, ORB, LANES), f32),
        in_specs=[pl.BlockSpec(memory_space=pltpu.SMEM)] + vmem(2),
        out_specs=vmem(1)[0],
        compiler_params=params(),
        name="merge",
    )(me, rows, cols)


def exchange(x, axes):
    return lax.all_to_all(x, axes, split_axis=0, concat_axis=0, tiled=True)


def gather(x, axes, n):
    return exchange(jnp.broadcast_to(x[None], (n,) + x.shape), axes)


def body(vectors, tiles, tile_pos, diag_blocks):
    zh = lax.axis_index("zh")
    r = lax.axis_index("x") * N_ZL + lax.axis_index("zl")
    me = jnp.stack([r, zh, lax.axis_index("core"), lax.axis_index("y")]).astype(jnp.int32)
    swap = [(0, 1), (1, 0)]

    packed = pack(tiles[0, 0], diag_blocks[0], tile_pos[0, 0])
    packed = exchange(packed, "y")

    mine, other, own = slice_vectors(me, vectors.reshape(-1, ORB, LANES))
    cols = pick_half(me, lax.all_gather(own, ("x", "zl", "core"), axis=0, tiled=False))
    current = join_cores(me, mine, lax.ppermute(other, "core", swap))

    packed, current, cols = lax.optimization_barrier((packed, current, cols))
    blocks_a, pos_a = unpack(packed)
    blocks_b, pos_b = unpack(lax.ppermute(packed, "core", swap))
    where, blocks = (me, pos_a, pos_b), (blocks_a, blocks_b)

    previous = None
    for step in range(DEGREE):
        out_cols = product(mirror_kernel, "mirror", where, current, blocks, N_R)
        out_cols, cols = lax.optimization_barrier((out_cols, cols))
        got_cols = exchange(out_cols, ROW_AX)
        out_rows = product(direct_kernel, "direct", where, cols, blocks, N_ZH)
        if step == DEGREE - 1:
            break
        got = exchange(merge(me, out_rows, got_cols), "zh")
        got, current, own_at = lax.optimization_barrier((got, current, zh))
        shifted = (jnp.sum(got, 0) - centre * current) / half_width
        following = shifted if previous is None else 2.0 * shifted - previous
        previous, current = current, following
        cols = gather(lax.dynamic_index_in_dim(current, own_at, 0, keepdims=False), ROW_AX, N_R)

    result = jnp.sum(exchange(finish(me, out_rows, jnp.sum(got_cols, 0), current, previous), ("core", "zh")), 0)
    result = gather(result, ("y", "zh"), N_ZH * N_Y).reshape(N_Y, N_ZH, ORB, LANES)
    return spread(result).reshape(vectors.shape)


def solution(mesh):
    fine = Mesh(
        mesh.devices.reshape(N_X, N_ZL, N_CORE, N_ZH, N_Y), ("x", "zl", "core", "zh", "y")
    )
    row, col = ("x", "zl", "core"), ("zh", "y")
    return jax.shard_map(
        body,
        mesh=fine,
        in_specs=(
            P(row, None),
            P(row, col, None, None, None),
            P(row, col, None, None),
            P(row + col, None, None),
        ),
        out_specs=P(row, None),
        check_vma=False,
    )
```

```python
import functools

import jax
import jax.numpy as jnp
from jax import lax
from jax.experimental import pallas as pl
from jax.experimental.pallas import tpu as pltpu
from jax.sharding import Mesh, PartitionSpec as P

ORB = 56
DEGREE = 3
LANES = 128
N_X, N_ZL, N_CORE, N_ZH, N_Y = 4, 2, 2, 4, 8
N_R = N_X * N_ZL
TILES = 10
SLOTS = TILES + 1
WIDE = 640
VS = 8
PLACE = SLOTS * ORB - (WIDE - LANES)
ROW_AX = ("x", "zl")
GROUPS = N_CORE * N_Y

filter_low = 0.0
filter_high = 8.0
centre = 0.5 * (filter_high + filter_low)
half_width = 0.5 * (filter_high - filter_low)

f32 = jnp.float32
bf16 = jnp.bfloat16


def params():
    return pltpu.CompilerParams(vmem_limit_bytes=40 * 1024 * 1024)


def vmem(n):
    return [pl.BlockSpec(memory_space=pltpu.VMEM)] * n


def lane_iota(rows=ORB):
    return lax.broadcasted_iota(jnp.int32, (rows, LANES), 1)


def roll_to(x, source, target):
    shift = (target - source) % LANES
    return x if shift == 0 else pltpu.roll(x, shift, 1)


def pack_kernel(tiles_hbm, diag_hbm, pos_hbm, out_hbm, tiles_ref, diag_ref, pos_ref, out_ref, sems, out_sems):
    copies = [
        pltpu.make_async_copy(src, dst, sems.at[k])
        for k, (src, dst) in enumerate(((tiles_hbm, tiles_ref), (diag_hbm, diag_ref), (pos_hbm, pos_ref)))
    ]
    for copy in copies:
        copy.start()
    for copy in copies:
        copy.wait()
    lane = lane_iota()
    pieces = [tiles_ref[t] for t in range(TILES)] + [diag_ref[...]]
    wide = [
        jnp.concatenate([p, jnp.zeros((ORB, LANES - ORB), f32)], axis=1) for p in pieces
    ]
    gap = jnp.zeros((1, LANES - 2 * TILES), f32)
    both = pos_ref[...].astype(f32)
    places = jnp.concatenate([both[0:1], both[1:2], gap], axis=1)
    places = jnp.broadcast_to(places, (ORB, LANES))
    for q in range(WIDE // LANES):
        total = jnp.zeros((ORB, LANES), f32)
        for t in range(SLOTS):
            start = t * ORB - q * LANES
            if start <= -ORB or start >= LANES:
                continue
            inside = (lane >= max(start, 0)) & (lane < min(start + ORB, LANES))
            total = jnp.where(inside, roll_to(wide[t], 0, start), total)
        if q == WIDE // LANES - 1:
            start = SLOTS * ORB - q * LANES
            total = jnp.where(lane >= start, roll_to(places, 0, start), total)
        out_ref[:, q * LANES : (q + 1) * LANES] = total
    copies = [pltpu.make_async_copy(out_ref, out_hbm.at[k], out_sems.at[k]) for k in range(N_Y)]
    for copy in copies:
        copy.start()
    for copy in copies:
        copy.wait()


def pack(tile_data, diag, places):
    return pl.pallas_call(
        pack_kernel,
        out_shape=jax.ShapeDtypeStruct((N_Y, ORB, WIDE), f32),
        in_specs=[pl.BlockSpec(memory_space=pl.ANY)] * 3,
        out_specs=pl.BlockSpec(memory_space=pl.ANY),
        scratch_shapes=[
            pltpu.VMEM((TILES, ORB, ORB), f32),
            pltpu.VMEM((ORB, ORB), f32),
            pltpu.VMEM((2, TILES), jnp.int32),
            pltpu.VMEM((ORB, WIDE), f32),
            pltpu.SemaphoreType.DMA((3,)),
            pltpu.SemaphoreType.DMA((N_Y,)),
        ],
        compiler_params=pltpu.CompilerParams(vmem_limit_bytes=56 * 1024 * 1024),
        name="pack",
    )(tile_data, diag, places)


def unpack_kernel(in_ref, blocks_ref, places_ref):
    x = in_ref[...].reshape(N_Y * ORB, WIDE)
    high = x.astype(bf16)
    low = (x - high.astype(f32)).astype(bf16)
    for t in range(SLOTS):
        start = t * ORB
        q, off = start // LANES, start % LANES
        width = LANES if off + ORB <= LANES else 2 * LANES
        source = lax.broadcasted_iota(jnp.int32, (width, LANES), 0)
        target = lax.broadcasted_iota(jnp.int32, (width, LANES), 1)
        window = slice(q * LANES, q * LANES + width)
        total = None
        for term, at in ((high, 0), (low, 64)):
            hit = (target >= at) & (target < at + ORB) & (source == target - at + off)
            part = jnp.dot(term[:, window], jnp.where(hit, 1.0, 0.0).astype(bf16), preferred_element_type=f32)
            total = part if total is None else total + part
        for s in range(N_Y):
            blocks_ref[s * SLOTS + t] = total[s * ORB : (s + 1) * ORB].astype(bf16)
    for s in range(N_Y):
        last = in_ref[s, 0:1, WIDE - LANES : WIDE]
        shown = lax.broadcasted_iota(jnp.int32, (1, LANES), 1) >= PLACE
        places_ref[s : s + 1] = jnp.where(shown, last, 0.0).astype(jnp.int32)


def unpack(packed):
    return pl.pallas_call(
        unpack_kernel,
        out_shape=(
            jax.ShapeDtypeStruct((N_Y * SLOTS, ORB, LANES), bf16),
            jax.ShapeDtypeStruct((N_Y, LANES), jnp.int32),
        ),
        in_specs=vmem(1),
        out_specs=tuple(vmem(2)),
        compiler_params=params(),
        name="unpack",
    )(packed)


def slice_kernel(me_ref, in_ref, mine_ref, other_ref, own_ref):
    lane = lane_iota()
    zh, core, start = me_ref[1], me_ref[2], me_ref[3] * (2 * VS)

    def placed(block, k, target):
        shift = lax.rem(target - k * VS + 2 * LANES - start, LANES)
        return pltpu.roll(in_ref[block], shift, 1)

    for out_ref, k in ((mine_ref, core), (other_ref, 1 - core)):
        for zp in range(N_ZH // 2):
            total = jnp.zeros((ORB, LANES), f32)
            for half in range(2):
                for y in range(N_Y):
                    target = half * 64 + y * VS
                    inside = (lane >= target) & (lane < target + VS)
                    total = jnp.where(inside, placed((2 * zp + half) * N_Y + y, k, target), total)
            out_ref[zp] = total
    total = jnp.zeros((ORB, LANES), f32)
    for k in range(N_CORE):
        for y in range(N_Y):
            target = k * 64 + y * VS
            inside = (lane >= target) & (lane < target + VS)
            total = jnp.where(inside, placed(zh * N_Y + y, k, target), total)
    own_ref[...] = total


def slice_vectors(me, blocks):
    pair = jax.ShapeDtypeStruct((N_ZH // 2, ORB, LANES), f32)
    return pl.pallas_call(
        slice_kernel,
        out_shape=(pair, pair, jax.ShapeDtypeStruct((ORB, LANES), f32)),
        in_specs=[pl.BlockSpec(memory_space=pltpu.SMEM)] + vmem(1),
        out_specs=tuple(vmem(3)),
        compiler_params=params(),
        name="slice_vectors",
    )(me, blocks)


def join_kernel(me_ref, mine_ref, other_ref, out_ref):
    lane = lane_iota()
    is_zero = me_ref[2] == 0
    for zp in range(N_ZH // 2):
        mine, other = mine_ref[zp], other_ref[zp]
        a = jnp.where(is_zero, mine, other)
        b = jnp.where(is_zero, other, mine)
        out_ref[2 * zp] = jnp.where(lane < 64, a, pltpu.roll(b, 64, 1))
        out_ref[2 * zp + 1] = jnp.where(lane < 64, pltpu.roll(a, 64, 1), b)


def join_cores(me, mine, other):
    return pl.pallas_call(
        join_kernel,
        out_shape=jax.ShapeDtypeStruct((N_ZH, ORB, LANES), f32),
        in_specs=[pl.BlockSpec(memory_space=pltpu.SMEM)] + vmem(2),
        out_specs=vmem(1)[0],
        compiler_params=params(),
        name="join_cores",
    )(me, mine, other)


def pick_kernel(me_ref, in_ref, out_ref):
    lane = lane_iota()
    is_zero = me_ref[2] == 0
    for r in range(N_R):
        a, b = in_ref[2 * r], in_ref[2 * r + 1]
        first = jnp.where(is_zero, a, pltpu.roll(a, 64, 1))
        second = jnp.where(is_zero, pltpu.roll(b, 64, 1), b)
        out_ref[r] = jnp.where(lane < 64, first, second)


def pick_half(me, gathered):
    return pl.pallas_call(
        pick_kernel,
        out_shape=jax.ShapeDtypeStruct((N_R, ORB, LANES), f32),
        in_specs=[pl.BlockSpec(memory_space=pltpu.SMEM)] + vmem(1),
        out_specs=vmem(1)[0],
        compiler_params=params(),
        name="pick_half",
    )(me, gathered)


def split_terms(src_ref, dst_ref):
    gap = jnp.zeros((64 - ORB, LANES), f32)
    for chunk in range(src_ref.shape[0]):
        x = src_ref[chunk]
        x = jnp.concatenate([x, gap, x, gap], axis=0).T
        high = x.astype(bf16).astype(f32)
        low = x - high
        for o in range(GROUPS):
            rows = slice(o * VS, (o + 1) * VS)
            both = jnp.concatenate([high[rows], low[rows]], axis=0)
            dst_ref[chunk * GROUPS + o] = both.astype(bf16)


def row_col(pos_ref, core_s, s, t):
    i, g = pos_ref[s, PLACE + t], pos_ref[s, PLACE + TILES + t]
    row = (i >> 3) * GROUPS + core_s * N_Y + (i & 7)
    col = (g >> 1) * GROUPS + (g & 1) * N_Y + s
    return row, col


def mirror_kernel(me_ref, pos_a_ref, pos_b_ref, rows_ref, blocks_a_ref, blocks_b_ref, out_ref, v_ref, acc_ref):
    split_terms(rows_ref, v_ref)
    acc_ref[...] = jnp.zeros_like(acc_ref)
    core = me_ref[2]
    parts = ((pos_a_ref, blocks_a_ref, core), (pos_b_ref, blocks_b_ref, 1 - core))

    def four_sources(four, carry):
        for s in (4 * four + k for k in range(4)):
            for t in range(TILES):
                for pos_ref, blocks_ref, core_s in parts:
                    row, col = row_col(pos_ref, core_s, s, t)
                    both = jnp.dot(v_ref[row][:, :ORB], blocks_ref[s * SLOTS + t], preferred_element_type=f32)
                    acc_ref[col] += both[:VS] + both[VS:]
        return carry

    lax.fori_loop(0, N_Y // 4, four_sources, 0)
    for chunk in range(out_ref.shape[0]):
        x = acc_ref[chunk * GROUPS : (chunk + 1) * GROUPS].reshape(LANES, LANES)
        x = x + pltpu.roll(x, 64, 1)
        out_ref[chunk] = x.T[:ORB]


def direct_kernel(me_ref, pos_a_ref, pos_b_ref, cols_ref, blocks_a_ref, blocks_b_ref, out_ref, v_ref, acc_ref):
    split_terms(cols_ref, v_ref)
    acc_ref[...] = jnp.zeros_like(acc_ref)
    my_r, my_zh, core = me_ref[0], me_ref[1], me_ref[2]
    parts = ((pos_a_ref, blocks_a_ref, core), (pos_b_ref, blocks_b_ref, 1 - core))

    def one_source(s, carry):
        for t in range(SLOTS):
            for pos_ref, blocks_ref, core_s in parts:
                if t < TILES:
                    row, col = row_col(pos_ref, core_s, s, t)
                else:
                    row = my_zh * GROUPS + core_s * N_Y + s
                    col = my_r * GROUPS + core_s * N_Y + s
                both = lax.dot_general(
                    v_ref[col], blocks_ref[s * SLOTS + t], (((1,), (1,)), ((), ())),
                    preferred_element_type=f32,
                )
                acc_ref[row, :, 0:ORB] += both[:VS] + both[VS:]
        return carry

    lax.fori_loop(0, N_Y, one_source, 0)
    for chunk in range(out_ref.shape[0]):
        x = acc_ref[chunk * GROUPS : (chunk + 1) * GROUPS].reshape(LANES, LANES)
        out_ref[chunk] = x.T[:ORB]


def product(kernel, name, scalars, field, blocks, chunks):
    smem = pl.BlockSpec(memory_space=pltpu.SMEM)
    return pl.pallas_call(
        kernel,
        out_shape=jax.ShapeDtypeStruct((chunks, ORB, LANES), f32),
        in_specs=[smem] * len(scalars) + vmem(1 + len(blocks)),
        out_specs=vmem(1)[0],
        scratch_shapes=[
            pltpu.VMEM((field.shape[0] * GROUPS, 2 * VS, LANES), bf16),
            pltpu.VMEM((chunks * GROUPS, VS, LANES), f32),
        ],
        compiler_params=params(),
        cost_estimate=pl.CostEstimate(flops=200000000, bytes_accessed=4000000, transcendentals=0),
        name=name,
    )(*scalars, field, *blocks)


def finish_kernel(me_ref, rows_ref, own_ref, current_ref, previous_ref, out_ref):
    lane = lane_iota()
    zh, core = me_ref[1], me_ref[2]
    scale = 2.0 / half_width
    own = scale * own_ref[...] - (scale * centre) * current_ref[zh] - previous_ref[zh]
    for z in range(N_ZH):
        total = scale * rows_ref[z] + jnp.where(zh == z, own, 0.0)
        for k in range(N_CORE):
            x = total if k == 0 else pltpu.roll(total, 64, 1)
            x = jnp.where(lane < 64, x, 0.0)
            for step in (32, 16, 8):
                block = lane & (4 * step - 1)
                moved = pltpu.roll(x, step, 1)
                x = jnp.where(block < step, x, jnp.where((block >= 2 * step) & (block < 3 * step), moved, 0.0))
            out_ref[k * N_ZH + z] = pltpu.roll(x, core * VS, 1)


def finish(me, rows, own, current, previous):
    return pl.pallas_call(
        finish_kernel,
        out_shape=jax.ShapeDtypeStruct((N_CORE * N_ZH, ORB, LANES), f32),
        in_specs=[pl.BlockSpec(memory_space=pltpu.SMEM)] + vmem(4),
        out_specs=vmem(1)[0],
        compiler_params=params(),
        name="finish",
    )(me, rows, own, current, previous)


def spread_kernel(in_ref, out_hbm, held, sems):
    lane = lane_iota()
    copies = []
    for z in range(N_ZH):
        x = [in_ref[y, z] for y in range(N_Y)]
        for d in (4, 2, 1):
            upper = (lane & (16 * d)) != 0
            for a in range(N_Y):
                if a & d:
                    continue
                low, high = x[a], x[a + d]
                x[a] = jnp.where(upper, pltpu.roll(high, 16 * d, 1), low)
                x[a + d] = jnp.where(upper, high, pltpu.roll(low, LANES - 16 * d, 1))
        for y in range(N_Y):
            held[z, y] = x[y]
        copy = pltpu.make_async_copy(held.at[z], out_hbm.at[pl.ds(z * N_Y, N_Y)], sems.at[z])
        copy.start()
        copies.append(copy)
    for copy in copies:
        copy.wait()


def spread(gathered):
    return pl.pallas_call(
        spread_kernel,
        out_shape=jax.ShapeDtypeStruct((N_ZH * N_Y, ORB, LANES), f32),
        in_specs=vmem(1),
        out_specs=pl.BlockSpec(memory_space=pl.ANY),
        scratch_shapes=[
            pltpu.VMEM((N_ZH, N_Y, ORB, LANES), f32),
            pltpu.SemaphoreType.DMA((N_ZH,)),
        ],
        compiler_params=params(),
        name="spread",
    )(gathered)


def merge_kernel(me_ref, rows_ref, cols_ref, out_ref):
    own = cols_ref[0]
    for r in range(1, N_R):
        own = own + cols_ref[r]
    for z in range(N_ZH):
        total = rows_ref[z] + jnp.where(me_ref[1] == z, own, 0.0)
        for copy in range(N_ZH):
            out_ref[copy, z] = total


def merge(me, rows, cols):
    return pl.pallas_call(
        merge_kernel,
        out_shape=jax.ShapeDtypeStruct((N_ZH, N_ZH, ORB, LANES), f32),
        in_specs=[pl.BlockSpec(memory_space=pltpu.SMEM)] + vmem(2),
        out_specs=vmem(1)[0],
        compiler_params=params(),
        name="merge",
    )(me, rows, cols)


def exchange(x, axes):
    return lax.all_to_all(x, axes, split_axis=0, concat_axis=0, tiled=True)


def gather(x, axes, n):
    return exchange(jnp.broadcast_to(x[None], (n,) + x.shape), axes)


def body(vectors, tiles, tile_pos, diag_blocks):
    zh = lax.axis_index("zh")
    r = lax.axis_index("x") * N_ZL + lax.axis_index("zl")
    me = jnp.stack([r, zh, lax.axis_index("core"), lax.axis_index("y")]).astype(jnp.int32)
    swap = [(0, 1), (1, 0)]

    packed = pack(tiles[0, 0], diag_blocks[0], tile_pos[0, 0])
    packed = exchange(packed, "y")

    mine, other, own = slice_vectors(me, vectors.reshape(-1, ORB, LANES))
    cols = pick_half(me, lax.all_gather(own, ("x", "zl", "core"), axis=0, tiled=False))
    current = join_cores(me, mine, lax.ppermute(other, "core", swap))

    packed, current, cols = lax.optimization_barrier((packed, current, cols))
    blocks_a, pos_a = unpack(packed)
    blocks_b, pos_b = unpack(lax.ppermute(packed, "core", swap))
    where, blocks = (me, pos_a, pos_b), (blocks_a, blocks_b)

    previous = None
    for step in range(DEGREE):
        out_cols = product(mirror_kernel, "mirror", where, current, blocks, N_R)
        out_cols, cols = lax.optimization_barrier((out_cols, cols))
        got_cols = exchange(out_cols, ROW_AX)
        out_rows = product(direct_kernel, "direct", where, cols, blocks, N_ZH)
        if step == DEGREE - 1:
            break
        got = exchange(merge(me, out_rows, got_cols), "zh")
        got, current, own_at = lax.optimization_barrier((got, current, zh))
        shifted = (jnp.sum(got, 0) - centre * current) / half_width
        following = shifted if previous is None else 2.0 * shifted - previous
        previous, current = current, following
        cols = gather(lax.dynamic_index_in_dim(current, own_at, 0, keepdims=False), ROW_AX, N_R)

    result = jnp.sum(exchange(finish(me, out_rows, jnp.sum(got_cols, 0), current, previous), ("core", "zh")), 0)
    result = gather(result, ("y", "zh"), N_ZH * N_Y).reshape(N_Y, N_ZH, ORB, LANES)
    return spread(result).reshape(vectors.shape)


def solution(mesh):
    fine = Mesh(
        mesh.devices.reshape(N_X, N_ZL, N_CORE, N_ZH, N_Y), ("x", "zl", "core", "zh", "y")
    )
    row, col = ("x", "zl", "core"), ("zh", "y")
    return jax.shard_map(
        body,
        mesh=fine,
        in_specs=(
            P(row, None),
            P(row, col, None, None, None),
            P(row, col, None, None),
            P(row + col, None, None),
        ),
        out_specs=P(row, None),
        check_vma=False,
    )
```

```python
import functools

import jax
import jax.numpy as jnp
from jax import lax
from jax.experimental import pallas as pl
from jax.experimental.pallas import tpu as pltpu
from jax.sharding import Mesh, PartitionSpec as P

ORB = 56
DEGREE = 3
LANES = 128
N_X, N_ZL, N_CORE, N_ZH, N_Y = 4, 2, 2, 4, 8
N_R = N_X * N_ZL
TILES = 10
SLOTS = TILES + 1
WIDE = 640
VS = 8
PLACE = SLOTS * ORB - (WIDE - LANES)
ROW_AX = ("x", "zl")
GROUPS = N_CORE * N_Y

filter_low = 0.0
filter_high = 8.0
centre = 0.5 * (filter_high + filter_low)
half_width = 0.5 * (filter_high - filter_low)

f32 = jnp.float32
bf16 = jnp.bfloat16


def params():
    return pltpu.CompilerParams(vmem_limit_bytes=40 * 1024 * 1024)


def vmem(n):
    return [pl.BlockSpec(memory_space=pltpu.VMEM)] * n


def lane_iota(rows=ORB):
    return lax.broadcasted_iota(jnp.int32, (rows, LANES), 1)


def roll_to(x, source, target):
    shift = (target - source) % LANES
    return x if shift == 0 else pltpu.roll(x, shift, 1)


def pack_kernel(tiles_hbm, diag_hbm, pos_hbm, out_hbm, tiles_ref, diag_ref, pos_ref, out_ref, sems, out_sems):
    copies = [
        pltpu.make_async_copy(src, dst, sems.at[k])
        for k, (src, dst) in enumerate(((tiles_hbm, tiles_ref), (diag_hbm, diag_ref), (pos_hbm, pos_ref)))
    ]
    for copy in copies:
        copy.start()
    for copy in copies:
        copy.wait()
    lane = lane_iota()
    pieces = [tiles_ref[t] for t in range(TILES)] + [diag_ref[...]]
    wide = [
        jnp.concatenate([p, jnp.zeros((ORB, LANES - ORB), f32)], axis=1) for p in pieces
    ]
    gap = jnp.zeros((1, LANES - 2 * TILES), f32)
    both = pos_ref[...].astype(f32)
    places = jnp.concatenate([both[0:1], both[1:2], gap], axis=1)
    places = jnp.broadcast_to(places, (ORB, LANES))
    for q in range(WIDE // LANES):
        total = jnp.zeros((ORB, LANES), f32)
        for t in range(SLOTS):
            start = t * ORB - q * LANES
            if start <= -ORB or start >= LANES:
                continue
            inside = (lane >= max(start, 0)) & (lane < min(start + ORB, LANES))
            total = jnp.where(inside, roll_to(wide[t], 0, start), total)
        if q == WIDE // LANES - 1:
            start = SLOTS * ORB - q * LANES
            total = jnp.where(lane >= start, roll_to(places, 0, start), total)
        out_ref[:, q * LANES : (q + 1) * LANES] = total
    copies = [pltpu.make_async_copy(out_ref, out_hbm.at[k], out_sems.at[k]) for k in range(N_Y)]
    for copy in copies:
        copy.start()
    for copy in copies:
        copy.wait()


def pack(tile_data, diag, places):
    return pl.pallas_call(
        pack_kernel,
        out_shape=jax.ShapeDtypeStruct((N_Y, ORB, WIDE), f32),
        in_specs=[pl.BlockSpec(memory_space=pl.ANY)] * 3,
        out_specs=pl.BlockSpec(memory_space=pl.ANY),
        scratch_shapes=[
            pltpu.VMEM((TILES, ORB, ORB), f32),
            pltpu.VMEM((ORB, ORB), f32),
            pltpu.VMEM((2, TILES), jnp.int32),
            pltpu.VMEM((ORB, WIDE), f32),
            pltpu.SemaphoreType.DMA((3,)),
            pltpu.SemaphoreType.DMA((N_Y,)),
        ],
        compiler_params=pltpu.CompilerParams(vmem_limit_bytes=56 * 1024 * 1024),
        name="pack",
    )(tile_data, diag, places)


def unpack_kernel(in_ref, blocks_ref, places_ref):
    x = in_ref[...].reshape(N_Y * ORB, WIDE)
    high = x.astype(bf16)
    low = (x - high.astype(f32)).astype(bf16)
    for t in range(SLOTS):
        start = t * ORB
        q, off = start // LANES, start % LANES
        width = LANES if off + ORB <= LANES else 2 * LANES
        source = lax.broadcasted_iota(jnp.int32, (width, LANES), 0)
        target = lax.broadcasted_iota(jnp.int32, (width, LANES), 1)
        window = slice(q * LANES, q * LANES + width)
        total = None
        for term, at in ((high, 0), (low, 64)):
            hit = (target >= at) & (target < at + ORB) & (source == target - at + off)
            part = jnp.dot(term[:, window], jnp.where(hit, 1.0, 0.0).astype(bf16), preferred_element_type=f32)
            total = part if total is None else total + part
        for s in range(N_Y):
            blocks_ref[s * SLOTS + t] = total[s * ORB : (s + 1) * ORB].astype(bf16)
    for s in range(N_Y):
        last = in_ref[s, 0:1, WIDE - LANES : WIDE]
        shown = lax.broadcasted_iota(jnp.int32, (1, LANES), 1) >= PLACE
        places_ref[s : s + 1] = jnp.where(shown, last, 0.0).astype(jnp.int32)


def unpack(packed):
    return pl.pallas_call(
        unpack_kernel,
        out_shape=(
            jax.ShapeDtypeStruct((N_Y * SLOTS, ORB, LANES), bf16),
            jax.ShapeDtypeStruct((N_Y, LANES), jnp.int32),
        ),
        in_specs=vmem(1),
        out_specs=tuple(vmem(2)),
        compiler_params=params(),
        name="unpack",
    )(packed)


def slice_kernel(me_ref, in_ref, mine_ref, other_ref, own_ref):
    lane = lane_iota()
    zh, core, start = me_ref[1], me_ref[2], me_ref[3] * (2 * VS)

    def placed(block, k, target):
        shift = lax.rem(target - k * VS + 2 * LANES - start, LANES)
        return pltpu.roll(in_ref[block], shift, 1)

    for out_ref, k in ((mine_ref, core), (other_ref, 1 - core)):
        for zp in range(N_ZH // 2):
            total = jnp.zeros((ORB, LANES), f32)
            for half in range(2):
                for y in range(N_Y):
                    target = half * 64 + y * VS
                    inside = (lane >= target) & (lane < target + VS)
                    total = jnp.where(inside, placed((2 * zp + half) * N_Y + y, k, target), total)
            out_ref[zp] = total
    total = jnp.zeros((ORB, LANES), f32)
    for k in range(N_CORE):
        for y in range(N_Y):
            target = k * 64 + y * VS
            inside = (lane >= target) & (lane < target + VS)
            total = jnp.where(inside, placed(zh * N_Y + y, k, target), total)
    own_ref[...] = total


def slice_vectors(me, blocks):
    pair = jax.ShapeDtypeStruct((N_ZH // 2, ORB, LANES), f32)
    return pl.pallas_call(
        slice_kernel,
        out_shape=(pair, pair, jax.ShapeDtypeStruct((ORB, LANES), f32)),
        in_specs=[pl.BlockSpec(memory_space=pltpu.SMEM)] + vmem(1),
        out_specs=tuple(vmem(3)),
        compiler_params=params(),
        name="slice_vectors",
    )(me, blocks)


def join_kernel(me_ref, mine_ref, other_ref, out_ref):
    lane = lane_iota()
    is_zero = me_ref[2] == 0
    for zp in range(N_ZH // 2):
        mine, other = mine_ref[zp], other_ref[zp]
        a = jnp.where(is_zero, mine, other)
        b = jnp.where(is_zero, other, mine)
        out_ref[2 * zp] = jnp.where(lane < 64, a, pltpu.roll(b, 64, 1))
        out_ref[2 * zp + 1] = jnp.where(lane < 64, pltpu.roll(a, 64, 1), b)


def join_cores(me, mine, other):
    return pl.pallas_call(
        join_kernel,
        out_shape=jax.ShapeDtypeStruct((N_ZH, ORB, LANES), f32),
        in_specs=[pl.BlockSpec(memory_space=pltpu.SMEM)] + vmem(2),
        out_specs=vmem(1)[0],
        compiler_params=params(),
        name="join_cores",
    )(me, mine, other)


def pick_kernel(me_ref, in_ref, out_ref):
    lane = lane_iota()
    is_zero = me_ref[2] == 0
    for r in range(N_R):
        a, b = in_ref[2 * r], in_ref[2 * r + 1]
        first = jnp.where(is_zero, a, pltpu.roll(a, 64, 1))
        second = jnp.where(is_zero, pltpu.roll(b, 64, 1), b)
        out_ref[r] = jnp.where(lane < 64, first, second)


def pick_half(me, gathered):
    return pl.pallas_call(
        pick_kernel,
        out_shape=jax.ShapeDtypeStruct((N_R, ORB, LANES), f32),
        in_specs=[pl.BlockSpec(memory_space=pltpu.SMEM)] + vmem(1),
        out_specs=vmem(1)[0],
        compiler_params=params(),
        name="pick_half",
    )(me, gathered)


def split_terms(src_ref, dst_ref):
    gap = jnp.zeros((64 - ORB, LANES), f32)
    for chunk in range(src_ref.shape[0]):
        x = src_ref[chunk]
        x = jnp.concatenate([x, gap, x, gap], axis=0).T
        high = x.astype(bf16).astype(f32)
        low = x - high
        for o in range(GROUPS):
            rows = slice(o * VS, (o + 1) * VS)
            both = jnp.concatenate([high[rows], low[rows]], axis=0)
            dst_ref[chunk * GROUPS + o] = both.astype(bf16)


def row_col(pos_ref, core_s, s, t):
    i, g = pos_ref[s, PLACE + t], pos_ref[s, PLACE + TILES + t]
    row = (i >> 3) * GROUPS + core_s * N_Y + (i & 7)
    col = (g >> 1) * GROUPS + (g & 1) * N_Y + s
    return row, col


def mirror_kernel(me_ref, pos_a_ref, pos_b_ref, rows_ref, blocks_a_ref, blocks_b_ref, out_ref, v_ref, acc_ref):
    split_terms(rows_ref, v_ref)
    acc_ref[...] = jnp.zeros_like(acc_ref)
    core = me_ref[2]
    parts = ((pos_a_ref, blocks_a_ref, core), (pos_b_ref, blocks_b_ref, 1 - core))

    def two_sources(pair, carry):
        for s in (2 * pair, 2 * pair + 1):
            for t in range(TILES):
                for pos_ref, blocks_ref, core_s in parts:
                    row, col = row_col(pos_ref, core_s, s, t)
                    both = jnp.dot(v_ref[row][:, :ORB], blocks_ref[s * SLOTS + t], preferred_element_type=f32)
                    acc_ref[col] += both[:VS] + both[VS:]
        return carry

    lax.fori_loop(0, N_Y // 2, two_sources, 0)
    for chunk in range(out_ref.shape[0]):
        x = acc_ref[chunk * GROUPS : (chunk + 1) * GROUPS].reshape(LANES, LANES)
        x = x + pltpu.roll(x, 64, 1)
        out_ref[chunk] = x.T[:ORB]


def direct_kernel(me_ref, pos_a_ref, pos_b_ref, cols_ref, blocks_a_ref, blocks_b_ref, out_ref, v_ref, acc_ref):
    split_terms(cols_ref, v_ref)
    acc_ref[...] = jnp.zeros_like(acc_ref)
    my_r, my_zh, core = me_ref[0], me_ref[1], me_ref[2]
    parts = ((pos_a_ref, blocks_a_ref, core), (pos_b_ref, blocks_b_ref, 1 - core))

    def one_source(s, carry):
        for t in range(SLOTS):
            for pos_ref, blocks_ref, core_s in parts:
                if t < TILES:
                    row, col = row_col(pos_ref, core_s, s, t)
                else:
                    row = my_zh * GROUPS + core_s * N_Y + s
                    col = my_r * GROUPS + core_s * N_Y + s
                both = lax.dot_general(
                    v_ref[col], blocks_ref[s * SLOTS + t], (((1,), (1,)), ((), ())),
                    preferred_element_type=f32,
                )
                acc_ref[row, :, 0:ORB] += both[:VS] + both[VS:]
        return carry

    lax.fori_loop(0, N_Y, one_source, 0)
    for chunk in range(out_ref.shape[0]):
        x = acc_ref[chunk * GROUPS : (chunk + 1) * GROUPS].reshape(LANES, LANES)
        out_ref[chunk] = x.T[:ORB]


def product(kernel, name, scalars, field, blocks, chunks):
    smem = pl.BlockSpec(memory_space=pltpu.SMEM)
    return pl.pallas_call(
        kernel,
        out_shape=jax.ShapeDtypeStruct((chunks, ORB, LANES), f32),
        in_specs=[smem] * len(scalars) + vmem(1 + len(blocks)),
        out_specs=vmem(1)[0],
        scratch_shapes=[
            pltpu.VMEM((field.shape[0] * GROUPS, 2 * VS, LANES), bf16),
            pltpu.VMEM((chunks * GROUPS, VS, LANES), f32),
        ],
        compiler_params=params(),
        cost_estimate=pl.CostEstimate(flops=200000000, bytes_accessed=4000000, transcendentals=0),
        name=name,
    )(*scalars, field, *blocks)


def finish_kernel(me_ref, rows_ref, own_ref, current_ref, previous_ref, out_ref):
    lane = lane_iota()
    zh, core = me_ref[1], me_ref[2]
    scale = 2.0 / half_width
    own = scale * own_ref[...] - (scale * centre) * current_ref[zh] - previous_ref[zh]
    for z in range(N_ZH):
        total = scale * rows_ref[z] + jnp.where(zh == z, own, 0.0)
        for k in range(N_CORE):
            x = total if k == 0 else pltpu.roll(total, 64, 1)
            x = jnp.where(lane < 64, x, 0.0)
            for step in (32, 16, 8):
                block = lane & (4 * step - 1)
                moved = pltpu.roll(x, step, 1)
                x = jnp.where(block < step, x, jnp.where((block >= 2 * step) & (block < 3 * step), moved, 0.0))
            out_ref[k * N_ZH + z] = pltpu.roll(x, core * VS, 1)


def finish(me, rows, own, current, previous):
    return pl.pallas_call(
        finish_kernel,
        out_shape=jax.ShapeDtypeStruct((N_CORE * N_ZH, ORB, LANES), f32),
        in_specs=[pl.BlockSpec(memory_space=pltpu.SMEM)] + vmem(4),
        out_specs=vmem(1)[0],
        compiler_params=params(),
        name="finish",
    )(me, rows, own, current, previous)


def spread_kernel(in_ref, out_hbm, held, sems):
    lane = lane_iota()
    copies = []
    for z in range(N_ZH):
        x = [in_ref[y, z] for y in range(N_Y)]
        for d in (4, 2, 1):
            upper = (lane & (16 * d)) != 0
            for a in range(N_Y):
                if a & d:
                    continue
                low, high = x[a], x[a + d]
                x[a] = jnp.where(upper, pltpu.roll(high, 16 * d, 1), low)
                x[a + d] = jnp.where(upper, high, pltpu.roll(low, LANES - 16 * d, 1))
        for y in range(N_Y):
            held[z, y] = x[y]
        copy = pltpu.make_async_copy(held.at[z], out_hbm.at[pl.ds(z * N_Y, N_Y)], sems.at[z])
        copy.start()
        copies.append(copy)
    for copy in copies:
        copy.wait()


def spread(gathered):
    return pl.pallas_call(
        spread_kernel,
        out_shape=jax.ShapeDtypeStruct((N_ZH * N_Y, ORB, LANES), f32),
        in_specs=vmem(1),
        out_specs=pl.BlockSpec(memory_space=pl.ANY),
        scratch_shapes=[
            pltpu.VMEM((N_ZH, N_Y, ORB, LANES), f32),
            pltpu.SemaphoreType.DMA((N_ZH,)),
        ],
        compiler_params=params(),
        name="spread",
    )(gathered)


def merge_kernel(me_ref, rows_ref, cols_ref, out_ref):
    own = cols_ref[0]
    for r in range(1, N_R):
        own = own + cols_ref[r]
    for z in range(N_ZH):
        total = rows_ref[z] + jnp.where(me_ref[1] == z, own, 0.0)
        for copy in range(N_ZH):
            out_ref[copy, z] = total


def merge(me, rows, cols):
    return pl.pallas_call(
        merge_kernel,
        out_shape=jax.ShapeDtypeStruct((N_ZH, N_ZH, ORB, LANES), f32),
        in_specs=[pl.BlockSpec(memory_space=pltpu.SMEM)] + vmem(2),
        out_specs=vmem(1)[0],
        compiler_params=params(),
        name="merge",
    )(me, rows, cols)


def exchange(x, axes):
    return lax.all_to_all(x, axes, split_axis=0, concat_axis=0, tiled=True)


def gather(x, axes, n):
    return exchange(jnp.broadcast_to(x[None], (n,) + x.shape), axes)


def body(vectors, tiles, tile_pos, diag_blocks):
    zh = lax.axis_index("zh")
    r = lax.axis_index("x") * N_ZL + lax.axis_index("zl")
    me = jnp.stack([r, zh, lax.axis_index("core"), lax.axis_index("y")]).astype(jnp.int32)
    swap = [(0, 1), (1, 0)]

    packed = pack(tiles[0, 0], diag_blocks[0], tile_pos[0, 0])
    packed = exchange(packed, "y")

    mine, other, own = slice_vectors(me, vectors.reshape(-1, ORB, LANES))
    gathered = lax.all_gather(own, ("x", "zl", "core"), axis=0, tiled=False)
    other = lax.ppermute(other, "core", swap)

    packed, gathered, mine, other = lax.optimization_barrier((packed, gathered, mine, other))
    cols = pick_half(me, gathered)
    current = join_cores(me, mine, other)
    blocks_a, pos_a = unpack(packed)
    blocks_b, pos_b = unpack(lax.ppermute(packed, "core", swap))
    where, blocks = (me, pos_a, pos_b), (blocks_a, blocks_b)

    previous = None
    for step in range(DEGREE):
        out_cols = product(mirror_kernel, "mirror", where, current, blocks, N_R)
        out_cols, cols = lax.optimization_barrier((out_cols, cols))
        got_cols = exchange(out_cols, ROW_AX)
        out_rows = product(direct_kernel, "direct", where, cols, blocks, N_ZH)
        if step == DEGREE - 1:
            break
        got = exchange(merge(me, out_rows, got_cols), "zh")
        got, current, own_at = lax.optimization_barrier((got, current, zh))
        shifted = (jnp.sum(got, 0) - centre * current) / half_width
        following = shifted if previous is None else 2.0 * shifted - previous
        previous, current = current, following
        cols = gather(lax.dynamic_index_in_dim(current, own_at, 0, keepdims=False), ROW_AX, N_R)

    result = jnp.sum(exchange(finish(me, out_rows, jnp.sum(got_cols, 0), current, previous), ("core", "zh")), 0)
    result = gather(result, ("y", "zh"), N_ZH * N_Y).reshape(N_Y, N_ZH, ORB, LANES)
    return spread(result).reshape(vectors.shape)


def solution(mesh):
    fine = Mesh(
        mesh.devices.reshape(N_X, N_ZL, N_CORE, N_ZH, N_Y), ("x", "zl", "core", "zh", "y")
    )
    row, col = ("x", "zl", "core"), ("zh", "y")
    return jax.shard_map(
        body,
        mesh=fine,
        in_specs=(
            P(row, None),
            P(row, col, None, None, None),
            P(row, col, None, None),
            P(row + col, None, None),
        ),
        out_specs=P(row, None),
        check_vma=False,
    )
```

```python
import functools

import jax
import jax.numpy as jnp
from jax import lax
from jax.experimental import pallas as pl
from jax.experimental.pallas import tpu as pltpu
from jax.sharding import Mesh, PartitionSpec as P

ORB = 56
DEGREE = 3
LANES = 128
N_X, N_ZL, N_CORE, N_ZH, N_Y = 4, 2, 2, 4, 8
N_R = N_X * N_ZL
TILES = 10
SLOTS = TILES + 1
WIDE = 640
VS = 8
PLACE = SLOTS * ORB - (WIDE - LANES)
ROW_AX = ("x", "zl")
GROUPS = N_CORE * N_Y

filter_low = 0.0
filter_high = 8.0
centre = 0.5 * (filter_high + filter_low)
half_width = 0.5 * (filter_high - filter_low)

f32 = jnp.float32
bf16 = jnp.bfloat16


def params():
    return pltpu.CompilerParams(vmem_limit_bytes=40 * 1024 * 1024)


def vmem(n):
    return [pl.BlockSpec(memory_space=pltpu.VMEM)] * n


def lane_iota(rows=ORB):
    return lax.broadcasted_iota(jnp.int32, (rows, LANES), 1)


def roll_to(x, source, target):
    shift = (target - source) % LANES
    return x if shift == 0 else pltpu.roll(x, shift, 1)


def pack_kernel(tiles_hbm, diag_hbm, pos_hbm, out_hbm, tiles_ref, diag_ref, pos_ref, out_ref, sems, out_sems):
    copies = [
        pltpu.make_async_copy(src, dst, sems.at[k])
        for k, (src, dst) in enumerate(((tiles_hbm, tiles_ref), (diag_hbm, diag_ref), (pos_hbm, pos_ref)))
    ]
    for copy in copies:
        copy.start()
    for copy in copies:
        copy.wait()
    lane = lane_iota()
    pieces = [tiles_ref[t] for t in range(TILES)] + [diag_ref[...]]
    wide = [
        jnp.concatenate([p, jnp.zeros((ORB, LANES - ORB), f32)], axis=1) for p in pieces
    ]
    gap = jnp.zeros((1, LANES - 2 * TILES), f32)
    both = pos_ref[...].astype(f32)
    places = jnp.concatenate([both[0:1], both[1:2], gap], axis=1)
    places = jnp.broadcast_to(places, (ORB, LANES))
    for q in range(WIDE // LANES):
        total = jnp.zeros((ORB, LANES), f32)
        for t in range(SLOTS):
            start = t * ORB - q * LANES
            if start <= -ORB or start >= LANES:
                continue
            inside = (lane >= max(start, 0)) & (lane < min(start + ORB, LANES))
            total = jnp.where(inside, roll_to(wide[t], 0, start), total)
        if q == WIDE // LANES - 1:
            start = SLOTS * ORB - q * LANES
            total = jnp.where(lane >= start, roll_to(places, 0, start), total)
        out_ref[:, q * LANES : (q + 1) * LANES] = total
    copies = [pltpu.make_async_copy(out_ref, out_hbm.at[k], out_sems.at[k]) for k in range(N_Y)]
    for copy in copies:
        copy.start()
    for copy in copies:
        copy.wait()


def pack(tile_data, diag, places):
    return pl.pallas_call(
        pack_kernel,
        out_shape=jax.ShapeDtypeStruct((N_Y, ORB, WIDE), f32),
        in_specs=[pl.BlockSpec(memory_space=pl.ANY)] * 3,
        out_specs=pl.BlockSpec(memory_space=pl.ANY),
        scratch_shapes=[
            pltpu.VMEM((TILES, ORB, ORB), f32),
            pltpu.VMEM((ORB, ORB), f32),
            pltpu.VMEM((2, TILES), jnp.int32),
            pltpu.VMEM((ORB, WIDE), f32),
            pltpu.SemaphoreType.DMA((3,)),
            pltpu.SemaphoreType.DMA((N_Y,)),
        ],
        compiler_params=pltpu.CompilerParams(vmem_limit_bytes=56 * 1024 * 1024),
        name="pack",
    )(tile_data, diag, places)


def unpack_kernel(in_ref, blocks_ref, places_ref):
    x = in_ref[...].reshape(N_Y * ORB, WIDE)
    high = x.astype(bf16)
    low = (x - high.astype(f32)).astype(bf16)
    for t in range(SLOTS):
        start = t * ORB
        q, off = start // LANES, start % LANES
        width = LANES if off + ORB <= LANES else 2 * LANES
        source = lax.broadcasted_iota(jnp.int32, (width, LANES), 0)
        target = lax.broadcasted_iota(jnp.int32, (width, LANES), 1)
        window = slice(q * LANES, q * LANES + width)
        total = None
        for term, at in ((high, 0), (low, 64)):
            hit = (target >= at) & (target < at + ORB) & (source == target - at + off)
            part = jnp.dot(term[:, window], jnp.where(hit, 1.0, 0.0).astype(bf16), preferred_element_type=f32)
            total = part if total is None else total + part
        for s in range(N_Y):
            blocks_ref[s * SLOTS + t] = total[s * ORB : (s + 1) * ORB].astype(bf16)
    for s in range(N_Y):
        last = in_ref[s, 0:1, WIDE - LANES : WIDE]
        shown = lax.broadcasted_iota(jnp.int32, (1, LANES), 1) >= PLACE
        places_ref[s : s + 1] = jnp.where(shown, last, 0.0).astype(jnp.int32)


def unpack(packed):
    return pl.pallas_call(
        unpack_kernel,
        out_shape=(
            jax.ShapeDtypeStruct((N_Y * SLOTS, ORB, LANES), bf16),
            jax.ShapeDtypeStruct((N_Y, LANES), jnp.int32),
        ),
        in_specs=vmem(1),
        out_specs=tuple(vmem(2)),
        compiler_params=params(),
        name="unpack",
    )(packed)


def slice_kernel(me_ref, in_ref, mine_ref, other_ref, own_ref):
    lane = lane_iota()
    zh, core, start = me_ref[1], me_ref[2], me_ref[3] * (2 * VS)

    def placed(block, k, target):
        shift = lax.rem(target - k * VS + 2 * LANES - start, LANES)
        return pltpu.roll(in_ref[block], shift, 1)

    for out_ref, k in ((mine_ref, core), (other_ref, 1 - core)):
        for zp in range(N_ZH // 2):
            total = jnp.zeros((ORB, LANES), f32)
            for half in range(2):
                for y in range(N_Y):
                    target = half * 64 + y * VS
                    inside = (lane >= target) & (lane < target + VS)
                    total = jnp.where(inside, placed((2 * zp + half) * N_Y + y, k, target), total)
            out_ref[zp] = total
    total = jnp.zeros((ORB, LANES), f32)
    for k in range(N_CORE):
        for y in range(N_Y):
            target = k * 64 + y * VS
            inside = (lane >= target) & (lane < target + VS)
            total = jnp.where(inside, placed(zh * N_Y + y, k, target), total)
    own_ref[...] = total


def slice_vectors(me, blocks):
    pair = jax.ShapeDtypeStruct((N_ZH // 2, ORB, LANES), f32)
    return pl.pallas_call(
        slice_kernel,
        out_shape=(pair, pair, jax.ShapeDtypeStruct((ORB, LANES), f32)),
        in_specs=[pl.BlockSpec(memory_space=pltpu.SMEM)] + vmem(1),
        out_specs=tuple(vmem(3)),
        compiler_params=params(),
        name="slice_vectors",
    )(me, blocks)


def join_kernel(me_ref, mine_ref, other_ref, out_ref):
    lane = lane_iota()
    is_zero = me_ref[2] == 0
    for zp in range(N_ZH // 2):
        mine, other = mine_ref[zp], other_ref[zp]
        a = jnp.where(is_zero, mine, other)
        b = jnp.where(is_zero, other, mine)
        out_ref[2 * zp] = jnp.where(lane < 64, a, pltpu.roll(b, 64, 1))
        out_ref[2 * zp + 1] = jnp.where(lane < 64, pltpu.roll(a, 64, 1), b)


def join_cores(me, mine, other):
    return pl.pallas_call(
        join_kernel,
        out_shape=jax.ShapeDtypeStruct((N_ZH, ORB, LANES), f32),
        in_specs=[pl.BlockSpec(memory_space=pltpu.SMEM)] + vmem(2),
        out_specs=vmem(1)[0],
        compiler_params=params(),
        name="join_cores",
    )(me, mine, other)


def pick_kernel(me_ref, in_ref, out_ref):
    lane = lane_iota()
    is_zero = me_ref[2] == 0
    for r in range(N_R):
        a, b = in_ref[2 * r], in_ref[2 * r + 1]
        first = jnp.where(is_zero, a, pltpu.roll(a, 64, 1))
        second = jnp.where(is_zero, pltpu.roll(b, 64, 1), b)
        out_ref[r] = jnp.where(lane < 64, first, second)


def pick_half(me, gathered):
    return pl.pallas_call(
        pick_kernel,
        out_shape=jax.ShapeDtypeStruct((N_R, ORB, LANES), f32),
        in_specs=[pl.BlockSpec(memory_space=pltpu.SMEM)] + vmem(1),
        out_specs=vmem(1)[0],
        compiler_params=params(),
        name="pick_half",
    )(me, gathered)


def split_terms(src_ref, dst_ref):
    gap = jnp.zeros((64 - ORB, LANES), f32)
    for chunk in range(src_ref.shape[0]):
        x = src_ref[chunk]
        x = jnp.concatenate([x, gap, x, gap], axis=0).T
        high = x.astype(bf16).astype(f32)
        low = x - high
        for o in range(GROUPS):
            rows = slice(o * VS, (o + 1) * VS)
            both = jnp.concatenate([high[rows], low[rows]], axis=0)
            dst_ref[chunk * GROUPS + o] = both.astype(bf16)


def row_col(pos_ref, core_s, s, t):
    i, g = pos_ref[s, PLACE + t], pos_ref[s, PLACE + TILES + t]
    row = (i >> 3) * GROUPS + core_s * N_Y + (i & 7)
    col = (g >> 1) * GROUPS + (g & 1) * N_Y + s
    return row, col


def mirror_kernel(me_ref, pos_a_ref, pos_b_ref, rows_ref, blocks_a_ref, blocks_b_ref, out_ref, v_ref, acc_ref):
    split_terms(rows_ref, v_ref)
    mirror_split_kernel(me_ref, pos_a_ref, pos_b_ref, v_ref, blocks_a_ref, blocks_b_ref, out_ref, acc_ref)


def mirror_split_kernel(me_ref, pos_a_ref, pos_b_ref, v_ref, blocks_a_ref, blocks_b_ref, out_ref, acc_ref):
    acc_ref[...] = jnp.zeros_like(acc_ref)
    core = me_ref[2]
    parts = ((pos_a_ref, blocks_a_ref, core), (pos_b_ref, blocks_b_ref, 1 - core))

    def two_sources(pair, carry):
        for s in (2 * pair, 2 * pair + 1):
            for t in range(TILES):
                for pos_ref, blocks_ref, core_s in parts:
                    row, col = row_col(pos_ref, core_s, s, t)
                    both = jnp.dot(v_ref[row][:, :ORB], blocks_ref[s * SLOTS + t], preferred_element_type=f32)
                    acc_ref[col] += both[:VS] + both[VS:]
        return carry

    lax.fori_loop(0, N_Y // 2, two_sources, 0)
    for chunk in range(out_ref.shape[0]):
        x = acc_ref[chunk * GROUPS : (chunk + 1) * GROUPS].reshape(LANES, LANES)
        x = x + pltpu.roll(x, 64, 1)
        out_ref[chunk] = x.T[:ORB]


def direct_kernel(me_ref, pos_a_ref, pos_b_ref, cols_ref, blocks_a_ref, blocks_b_ref, out_ref, v_ref, acc_ref):
    split_terms(cols_ref, v_ref)
    acc_ref[...] = jnp.zeros_like(acc_ref)
    my_r, my_zh, core = me_ref[0], me_ref[1], me_ref[2]
    parts = ((pos_a_ref, blocks_a_ref, core), (pos_b_ref, blocks_b_ref, 1 - core))

    def one_source(s, carry):
        for t in range(SLOTS):
            for pos_ref, blocks_ref, core_s in parts:
                if t < TILES:
                    row, col = row_col(pos_ref, core_s, s, t)
                else:
                    row = my_zh * GROUPS + core_s * N_Y + s
                    col = my_r * GROUPS + core_s * N_Y + s
                both = lax.dot_general(
                    v_ref[col], blocks_ref[s * SLOTS + t], (((1,), (1,)), ((), ())),
                    preferred_element_type=f32,
                )
                acc_ref[row, :, 0:ORB] += both[:VS] + both[VS:]
        return carry

    lax.fori_loop(0, N_Y, one_source, 0)
    for chunk in range(out_ref.shape[0]):
        x = acc_ref[chunk * GROUPS : (chunk + 1) * GROUPS].reshape(LANES, LANES)
        out_ref[chunk] = x.T[:ORB]


def split(field):
    return pl.pallas_call(
        split_terms,
        out_shape=jax.ShapeDtypeStruct((field.shape[0] * GROUPS, 2 * VS, LANES), bf16),
        in_specs=vmem(1),
        out_specs=vmem(1)[0],
        compiler_params=params(),
        name="split",
    )(field)


def product(kernel, name, scalars, field, blocks, chunks):
    smem = pl.BlockSpec(memory_space=pltpu.SMEM)
    return pl.pallas_call(
        kernel,
        out_shape=jax.ShapeDtypeStruct((chunks, ORB, LANES), f32),
        in_specs=[smem] * len(scalars) + vmem(1 + len(blocks)),
        out_specs=vmem(1)[0],
        scratch_shapes=[
            pltpu.VMEM((field.shape[0] * GROUPS, 2 * VS, LANES), bf16),
        ] * (field.dtype == f32) + [
            pltpu.VMEM((chunks * GROUPS, VS, LANES), f32),
        ],
        compiler_params=params(),
        cost_estimate=pl.CostEstimate(flops=200000000, bytes_accessed=4000000, transcendentals=0),
        name=name,
    )(*scalars, field, *blocks)


def finish_kernel(me_ref, rows_ref, own_ref, current_ref, previous_ref, out_ref):
    lane = lane_iota()
    zh, core = me_ref[1], me_ref[2]
    scale = 2.0 / half_width
    own = scale * own_ref[...] - (scale * centre) * current_ref[zh] - previous_ref[zh]
    for z in range(N_ZH):
        total = scale * rows_ref[z] + jnp.where(zh == z, own, 0.0)
        for k in range(N_CORE):
            x = total if k == 0 else pltpu.roll(total, 64, 1)
            x = jnp.where(lane < 64, x, 0.0)
            for step in (32, 16, 8):
                block = lane & (4 * step - 1)
                moved = pltpu.roll(x, step, 1)
                x = jnp.where(block < step, x, jnp.where((block >= 2 * step) & (block < 3 * step), moved, 0.0))
            out_ref[k * N_ZH + z] = pltpu.roll(x, core * VS, 1)


def finish(me, rows, own, current, previous):
    return pl.pallas_call(
        finish_kernel,
        out_shape=jax.ShapeDtypeStruct((N_CORE * N_ZH, ORB, LANES), f32),
        in_specs=[pl.BlockSpec(memory_space=pltpu.SMEM)] + vmem(4),
        out_specs=vmem(1)[0],
        compiler_params=params(),
        name="finish",
    )(me, rows, own, current, previous)


def spread_kernel(in_ref, out_hbm, held, sems):
    lane = lane_iota()
    copies = []
    for z in range(N_ZH):
        x = [in_ref[y, z] for y in range(N_Y)]
        for d in (4, 2, 1):
            upper = (lane & (16 * d)) != 0
            for a in range(N_Y):
                if a & d:
                    continue
                low, high = x[a], x[a + d]
                x[a] = jnp.where(upper, pltpu.roll(high, 16 * d, 1), low)
                x[a + d] = jnp.where(upper, high, pltpu.roll(low, LANES - 16 * d, 1))
        for y in range(N_Y):
            held[z, y] = x[y]
        copy = pltpu.make_async_copy(held.at[z], out_hbm.at[pl.ds(z * N_Y, N_Y)], sems.at[z])
        copy.start()
        copies.append(copy)
    for copy in copies:
        copy.wait()


def spread(gathered):
    return pl.pallas_call(
        spread_kernel,
        out_shape=jax.ShapeDtypeStruct((N_ZH * N_Y, ORB, LANES), f32),
        in_specs=vmem(1),
        out_specs=pl.BlockSpec(memory_space=pl.ANY),
        scratch_shapes=[
            pltpu.VMEM((N_ZH, N_Y, ORB, LANES), f32),
            pltpu.SemaphoreType.DMA((N_ZH,)),
        ],
        compiler_params=params(),
        name="spread",
    )(gathered)


def merge_kernel(me_ref, rows_ref, cols_ref, out_ref):
    own = cols_ref[0]
    for r in range(1, N_R):
        own = own + cols_ref[r]
    for z in range(N_ZH):
        total = rows_ref[z] + jnp.where(me_ref[1] == z, own, 0.0)
        for copy in range(N_ZH):
            out_ref[copy, z] = total


def merge(me, rows, cols):
    return pl.pallas_call(
        merge_kernel,
        out_shape=jax.ShapeDtypeStruct((N_ZH, N_ZH, ORB, LANES), f32),
        in_specs=[pl.BlockSpec(memory_space=pltpu.SMEM)] + vmem(2),
        out_specs=vmem(1)[0],
        compiler_params=params(),
        name="merge",
    )(me, rows, cols)


def exchange(x, axes):
    return lax.all_to_all(x, axes, split_axis=0, concat_axis=0, tiled=True)


def gather(x, axes, n):
    return exchange(jnp.broadcast_to(x[None], (n,) + x.shape), axes)


def body(vectors, tiles, tile_pos, diag_blocks):
    zh = lax.axis_index("zh")
    r = lax.axis_index("x") * N_ZL + lax.axis_index("zl")
    me = jnp.stack([r, zh, lax.axis_index("core"), lax.axis_index("y")]).astype(jnp.int32)
    swap = [(0, 1), (1, 0)]

    packed = pack(tiles[0, 0], diag_blocks[0], tile_pos[0, 0])
    packed = exchange(packed, "y")

    mine, other, own = slice_vectors(me, vectors.reshape(-1, ORB, LANES))
    cols = pick_half(me, lax.all_gather(own, ("x", "zl", "core"), axis=0, tiled=False))
    current = join_cores(me, mine, lax.ppermute(other, "core", swap))

    terms = split(current)

    packed, current, cols, terms = lax.optimization_barrier((packed, current, cols, terms))
    blocks_a, pos_a = unpack(packed)
    blocks_b, pos_b = unpack(lax.ppermute(packed, "core", swap))
    where, blocks = (me, pos_a, pos_b), (blocks_a, blocks_b)

    previous = None
    for step in range(DEGREE):
        if step == 0:
            out_cols = product(mirror_split_kernel, "mirror", where, terms, blocks, N_R)
        else:
            out_cols = product(mirror_kernel, "mirror", where, current, blocks, N_R)
        out_cols, cols = lax.optimization_barrier((out_cols, cols))
        got_cols = exchange(out_cols, ROW_AX)
        out_rows = product(direct_kernel, "direct", where, cols, blocks, N_ZH)
        if step == DEGREE - 1:
            break
        got = exchange(merge(me, out_rows, got_cols), "zh")
        got, current, own_at = lax.optimization_barrier((got, current, zh))
        shifted = (jnp.sum(got, 0) - centre * current) / half_width
        following = shifted if previous is None else 2.0 * shifted - previous
        previous, current = current, following
        cols = gather(lax.dynamic_index_in_dim(current, own_at, 0, keepdims=False), ROW_AX, N_R)

    result = jnp.sum(exchange(finish(me, out_rows, jnp.sum(got_cols, 0), current, previous), ("core", "zh")), 0)
    result = gather(result, ("y", "zh"), N_ZH * N_Y).reshape(N_Y, N_ZH, ORB, LANES)
    return spread(result).reshape(vectors.shape)


def solution(mesh):
    fine = Mesh(
        mesh.devices.reshape(N_X, N_ZL, N_CORE, N_ZH, N_Y), ("x", "zl", "core", "zh", "y")
    )
    row, col = ("x", "zl", "core"), ("zh", "y")
    return jax.shard_map(
        body,
        mesh=fine,
        in_specs=(
            P(row, None),
            P(row, col, None, None, None),
            P(row, col, None, None),
            P(row + col, None, None),
        ),
        out_specs=P(row, None),
        check_vma=False,
    )
```
